32 devices in a mesh: exp: 8 (over y, x, core), tp: 4 (over z).
Axes of the slice: x: 2, y: 2, z: 4, core: 2. Of those that a mesh axis runs over, the one named last changes fastest.
Arguments:
- tokens: bfloat16 [4096, 2048], P(('exp', 'tp')), may hold values from -6 to 6
- cotangent: bfloat16 [4096, 2048], P(('exp', 'tp')), may hold values from -6 to 6
- segment_ids: int32 [4096], P('exp'), may hold values from 0 to 2, as said below
- routes: int32 [4096, 6], P('exp'), may hold values from 0 to 15, all different within a row; in each aligned block of 512 rows (0 to 511, 512 to 1023, ...) at most 256 rows name the same one
- norm1_gain: bfloat16 [2048], P('exp'), may hold values from 0.5 to 1.5
- attn_q: bfloat16 [2048, 2048], P('exp', 'tp'), may hold values from -0.21875 to 0.21875
- attn_k: bfloat16 [2048, 512], P('exp', 'tp'), may hold values from -0.125 to 0.125
- attn_v: bfloat16 [2048, 512], P('exp', 'tp'), may hold values from -0.125 to 0.125
- attn_o: bfloat16 [2048, 2048], P('tp', 'exp'), may hold values from -1 to 1
- norm2_gain: bfloat16 [2048], P('exp'), may hold values from 0.5 to 1.5
- router: bfloat16 [2048, 16], P('exp'), may hold values from -0.0625 to 0.0625
- shared_gate: bfloat16 [2048, 2816], P('exp', 'tp'), may hold values from -0.125 to 0.125
- shared_up: bfloat16 [2048, 2816], P('exp', 'tp'), may hold values from -0.125 to 0.125
- shared_down: bfloat16 [2816, 2048], P('tp', 'exp'), may hold values from -0.21875 to 0.21875
- expert_gate: bfloat16 [16, 2048, 1408], P('exp', None, 'tp'), may hold values from -0.125 to 0.125
- expert_up: bfloat16 [16, 2048, 1408], P('exp', None, 'tp'), may hold values from -0.125 to 0.125
- expert_down: bfloat16 [16, 1408, 2048], P('exp', 'tp'), may hold values from -0.625 to 0.625
Outputs:
- out: bfloat16 [4096, 2048], P(('exp', 'tp'))
- grad_tokens: float32 [4096, 2048], P(('exp', 'tp'))
- grad_norm1_gain: float32 [2048], P('exp')
- grad_attn_q: float32 [2048, 2048], P('exp', 'tp')
- grad_attn_k: float32 [2048, 512], P('exp', 'tp')
- grad_attn_v: float32 [2048, 512], P('exp', 'tp')
- grad_attn_o: float32 [2048, 2048], P('tp', 'exp')
- grad_norm2_gain: float32 [2048], P('exp')
- grad_router: float32 [2048, 16], P('exp')
- grad_shared_gate: float32 [2048, 2816], P('exp', 'tp')
- grad_shared_up: float32 [2048, 2816], P('exp', 'tp')
- grad_shared_down: float32 [2816, 2048], P('tp', 'exp')
- grad_expert_gate: float32 [16, 2048, 1408], P('exp', None, 'tp')
- grad_expert_up: float32 [16, 2048, 1408], P('exp', None, 'tp')
- grad_expert_down: float32 [16, 1408, 2048], P('exp', 'tp')
The draws below stay inside these ranges and needn't reach their ends.
Inputs may be any that keep to these rules, and one draw needn't show every extreme that they name: `segment_ids`: within each sequence of 512 tokens the ids start at 0 and never fall, and each sequence holds three documents with ids 0, 1 and 2; a token attends only to tokens of its own id. `routes`: each row names 6 different experts. Within each aligned block of 512 rows (one sequence) no expert is named more than 256 times, and in some block some expert exactly 256 times.
All inputs are finite; a program needn't handle non-finite values.
Results may differ from the reference program's by a relative error of at most 0.023.
Values may be sent and summed in bfloat16 or wider, within the bound.
A program may use at most 320 MiB of HBM per device.

```python
import math
import jax
import jax.numpy as jnp
import numpy as np
from jax import lax

D = 2048
HEADS = 16
KV_HEADS = 4
HEAD_DIM = 128
EXPERT_FF = 1408
SH_FF = 2816
TOP = 6
SEQ = 512
EXPERTS = 16
TOKENS = 4096
CAP = 256
N_TP = 4


def draw_segment_ids(key, part):
    key = jax.random.fold_in(key, 11)
    blocks = TOKENS // SEQ
    margin = max(SEQ // 8, 2)
    key_head, key_tail, key_flags = jax.random.split(key, 3)
    head_start = jax.random.randint(key_head, (blocks, 1), 1, margin)
    tail_size = jax.random.randint(key_tail, (blocks, 1), 1, margin)
    flags = jax.random.randint(key_flags, (blocks, SEQ), 0, 64) == 0
    positions = jnp.arange(SEQ, dtype=jnp.int32)[None, :]
    inside = (positions > head_start) & (positions < SEQ - tail_size)
    starts = (positions == head_start) | (positions == SEQ - tail_size)
    boundary = jnp.where(inside, False, flags | starts) & (positions > 0)
    segment_ids = jnp.minimum(jnp.cumsum(boundary.astype(jnp.int32), axis=1), 2)
    return segment_ids.reshape(TOKENS).astype(jnp.int32)


def block_scale(rng, extent, shards, least, high):
    factor_of, own = 1.0, jax.random.fold_in(rng, 6)
    for position, parts in shards:
        draws = jnp.exp(jax.random.uniform(jax.random.fold_in(own, position), (parts,), jnp.float32, least / len(shards), high / len(shards)))
        factor_of = factor_of * jnp.repeat(draws, extent[position] // parts).reshape([-1 if axis == position else 1 for axis in range(len(extent))])
    return factor_of


def routed_block(rng, own, number, rows, count, top, limit, lean):
    order = jax.random.permutation(rng, count)
    packed, ordinary = shares(count, rows * top, limit, lean, True), shares(count, rows * top, limit, lean, False)
    places = jnp.arange(count)

    def named(sizes, rotation):
        used = int((sizes > 0).sum())
        fixed = max(1, used // 4)
        moved = fixed + (places - fixed + rotation * (used - fixed)) % max(1, count - fixed)
        return jnp.zeros((count,), jnp.int32).at[order[jnp.where(places < fixed, places, moved)]].set(jnp.asarray(sizes, jnp.int32))

    sizes = jnp.where(number % 4 == 0, named(packed, number // 4), named(ordinary, number - number // 4 - 1))
    mixed = jax.random.permutation(jax.random.fold_in(own, 3), count)
    donor, taker = mixed[0:count // 2 * 2:2], mixed[1:count // 2 * 2:2]
    room = jnp.minimum(sizes[donor] - 1, limit - sizes[taker]) // 2
    room = jnp.where((donor == order[0]) | (taker == order[0]) | (sizes[taker] == 0), 0, jnp.maximum(room, 0))
    moved = jax.random.randint(jax.random.fold_in(own, 4), (count // 2,), 0, 1 << 20) % (room + 1)
    sizes = sizes.at[donor].add(-moved).at[taker].add(moved)
    labels = jnp.searchsorted(jnp.cumsum(sizes), jnp.arange(rows * top), side="right").astype(jnp.int32)
    table = labels.reshape(top, rows).T
    table = table[jax.random.permutation(jax.random.fold_in(own, 1), rows)]
    rotation = jax.random.randint(jax.random.fold_in(own, 2), (rows, 1), 0, top)
    return jnp.take_along_axis(table, (jnp.arange(top)[None, :] + rotation) % top, axis=1)


def shares(amount, total, limit, slope, full):
    portions = [(1 << 20) // math.isqrt(grade ** slope) + 1 for grade in range(1, amount + 1)]
    largest = limit if full else min(limit, max(-(-total // amount), total * portions[0] // sum(portions)))
    least = 1 if total - largest >= amount - 1 else 0
    counts, spare = [largest] + [least] * (amount - 1), total - largest - least * (amount - 1)
    while spare > 0:
        candidates = [i for i in range(1, amount) if counts[i] < largest] or [i for i in range(1, amount) if counts[i] < limit]
        whole, budget = sum([portions[i] for i in candidates]), spare
        for i in candidates:
            addition = min(limit - counts[i], max(1, budget * portions[i] // whole), spare)
            counts[i] = counts[i] + addition
            spare = spare - addition
    return np.array(counts)


def scatter_about(key, dims, width, reach, cuts=(), held_as=jnp.bfloat16):
    gain = block_scale(key, dims, cuts, -0.22, 0.18) if cuts else 1.0
    values = jax.random.normal(key, dims, jnp.float32) * width * gain
    return jnp.minimum(jnp.maximum(values, -reach), reach).astype(held_as)


def setup_inputs(seed: int = 0) -> dict:
    splits = jax.random.split(jax.random.key(seed), 18)
    tokens = scatter_about(splits[0], (TOKENS, D), 1.0, 6.0, ((0, 32),))
    cotangent = scatter_about(splits[1], (TOKENS, D), 1.0, 6.0, ((0, 32),))
    segment_ids = draw_segment_ids(jax.random.fold_in(splits[17], 71), 0)
    routes_keys = jax.random.split(jax.random.fold_in(splits[3], 1), TOKENS // SEQ)
    routes_turns = jax.random.permutation(jax.random.fold_in(splits[3], 3), TOKENS // SEQ)
    routes = jax.vmap(lambda own, number: routed_block(jax.random.fold_in(splits[3], 2), own, number, SEQ, EXPERTS, TOP, CAP, 1))(routes_keys, routes_turns).reshape((TOKENS, TOP))
    norm1_gain = jnp.clip(1.0 + 0.1 * jax.random.normal(splits[4], (D,), jnp.float32), 0.5, 1.5).astype(jnp.bfloat16)
    attn_q = scatter_about(splits[5], (D, HEADS * HEAD_DIM), (D // 3) ** -0.5, 0.21875, ((0, 8), (1, 4)))
    attn_k = scatter_about(splits[6], (D, KV_HEADS * HEAD_DIM), D ** -0.5, 0.125, ((0, 8), (1, 4)))
    attn_v = scatter_about(splits[7], (D, KV_HEADS * HEAD_DIM), D ** -0.5, 0.125, ((0, 8), (1, 4)))
    attn_o = scatter_about(splits[8], (HEADS * HEAD_DIM, D), (HEADS * HEAD_DIM // 64) ** -0.5, 1.0, ((0, 4), (1, 8)))
    norm2_gain = jnp.clip(1.0 + 0.1 * jax.random.normal(splits[9], (D,), jnp.float32), 0.5, 1.5).astype(jnp.bfloat16)
    router = scatter_about(splits[10], (D, EXPERTS), (4 * D) ** -0.5, 0.0625, ((0, 8),))
    shared_gate = scatter_about(splits[11], (D, SH_FF), D ** -0.5, 0.125, ((0, 8), (1, 4)))
    shared_up = scatter_about(splits[12], (D, SH_FF), D ** -0.5, 0.125, ((0, 8), (1, 4)))
    shared_down = scatter_about(splits[13], (SH_FF, D), (SH_FF // 4) ** -0.5, 0.21875, ((0, 4), (1, 8)))
    expert_gate = scatter_about(splits[14], (EXPERTS, D, EXPERT_FF), D ** -0.5, 0.125, ((0, 8), (2, 4)))
    expert_up = scatter_about(splits[15], (EXPERTS, D, EXPERT_FF), D ** -0.5, 0.125, ((0, 8), (2, 4)))
    expert_down = scatter_about(splits[16], (EXPERTS, EXPERT_FF, D), (EXPERT_FF // 16) ** -0.5, 0.625, ((0, 8), (1, 4)))
    return dict(tokens=tokens, cotangent=cotangent, segment_ids=segment_ids, routes=routes, norm1_gain=norm1_gain, attn_q=attn_q, attn_k=attn_k, attn_v=attn_v, attn_o=attn_o, norm2_gain=norm2_gain, router=router, shared_gate=shared_gate, shared_up=shared_up, shared_down=shared_down, expert_gate=expert_gate, expert_up=expert_up, expert_down=expert_down)


epsilon = 1e-06
rope_base = 600000.0

@jax.custom_vjp
def low(v):
    return lax.optimization_barrier(v.astype(jnp.bfloat16)).astype(jnp.float32)

@jax.custom_vjp
def lower_returned(v):
    return v

def low_keep(v):
    return (low(v), None)

def low_pass(kept, grad):
    return (grad,)

def back_keep(v):
    return (v, None)

def back_low(kept, grad):
    return (low(grad),)
low.defvjp(low_keep, low_pass)
lower_returned.defvjp(back_keep, back_low)

def product(left, right):
    return jnp.dot(left, right, precision=lax.Precision.HIGHEST)

def rms_scale(values):
    return lax.rsqrt(lax.optimization_barrier(jnp.mean(values * values, axis=-1, keepdims=True)) + epsilon)

def rotary_tables(length, head_width):
    half_width = head_width // 2
    frequency = rope_base ** (-(jnp.arange(half_width, dtype=jnp.float32) * 2.0 / head_width))
    angles = jnp.arange(length, dtype=jnp.float32)[:, None] * frequency[None, :]
    return (jnp.cos(angles), jnp.sin(angles))

def rotate(values, cosine, sine):
    half_width = values.shape[-1] // 2
    first_half = values[..., :half_width]
    second_half = values[..., half_width:]
    cos_rows = cosine[:, None, :]
    sin_rows = sine[:, None, :]
    return jnp.concatenate([first_half * cos_rows - second_half * sin_rows, second_half * cos_rows + first_half * sin_rows], axis=-1)

def attend(normed, segments, query_weight, key_weight, value_weight):
    length = normed.shape[0]
    query_lin = lower_returned(product(normed, query_weight)).reshape(length, HEADS, HEAD_DIM)
    key_lin = lower_returned(product(normed, key_weight)).reshape(length, KV_HEADS, HEAD_DIM)
    value_lin = lower_returned(product(normed, value_weight)).reshape(length, KV_HEADS, HEAD_DIM)
    cosine, sine = rotary_tables(length, HEAD_DIM)
    queries = low(rotate(query_lin, cosine, sine))
    keys_all = low(rotate(key_lin, cosine, sine))
    values = low(value_lin)
    group_size = HEADS // KV_HEADS
    keys_all = jnp.repeat(keys_all, group_size, axis=1)
    values = jnp.repeat(values, group_size, axis=1)
    raw_scores = lower_returned(jnp.einsum('qhd,khd->hqk', queries, keys_all, precision=lax.Precision.HIGHEST))
    positions = jnp.arange(length, dtype=jnp.int32)
    allowed = (positions[None, :] <= positions[:, None]) & (segments[:, None] == segments[None, :])
    scores = jnp.where(allowed[None], raw_scores * HEAD_DIM ** (-0.5), -1e+30)
    weights = low(jax.nn.softmax(scores, axis=-1))
    mixed = jnp.einsum('hqk,khd->qhd', weights, values, precision=lax.Precision.HIGHEST)
    return low(lower_returned(mixed.reshape(length, HEADS * HEAD_DIM)))

def expert_result_rows(row_contents, expert_gate_weight, expert_up_weight, expert_down_weight):
    column_slice_width = expert_gate_weight.shape[2] // N_TP
    summed = jnp.zeros(row_contents.shape, jnp.float32)
    for slice_index in range(N_TP):
        first_column = slice_index * column_slice_width
        input_tokens = lower_returned(row_contents)
        gate_lin = lower_returned(jnp.einsum('rgq,rqj->rgj', input_tokens, expert_gate_weight[:, :, first_column:first_column + column_slice_width], precision=lax.Precision.HIGHEST))
        up_projected = lower_returned(jnp.einsum('rgq,rqj->rgj', input_tokens, expert_up_weight[:, :, first_column:first_column + column_slice_width], precision=lax.Precision.HIGHEST))
        activation = low(jax.nn.silu(gate_lin) * up_projected)
        summed = summed + low(jnp.einsum('ecf,efd->ecd', activation, expert_down_weight[:, first_column:first_column + column_slice_width, :], precision=lax.Precision.HIGHEST))
    return lower_returned(summed)

def routed_expert_indices(second_normalized, gate_probabilities, routes, expert_gate_weight, expert_up_weight, expert_down_weight):
    assignments = SEQ * TOP
    flat_routes = routes.reshape(assignments)
    onehot = (flat_routes[:, None] == jnp.arange(EXPERTS, dtype=jnp.int32)[None, :]).astype(jnp.int32)
    slot_index = lax.optimization_barrier(jnp.sum(jnp.cumsum(onehot, axis=0) * onehot, axis=-1)) - 1
    destination = (flat_routes * CAP + slot_index).astype(jnp.int32)
    slot_source = jnp.full((EXPERTS * CAP,), assignments, jnp.int32).at[destination].set(jnp.arange(assignments, dtype=jnp.int32))
    padded_rows = jnp.concatenate([second_normalized, jnp.zeros((1, D), jnp.float32)], axis=0)
    row_contents = padded_rows[slot_source // TOP].reshape(EXPERTS, CAP, D)
    expert_token_rows = expert_result_rows(row_contents, expert_gate_weight, expert_up_weight, expert_down_weight)
    picked = expert_token_rows.reshape(EXPERTS * CAP, D)[destination].reshape(SEQ, TOP, D)
    return lax.optimization_barrier(jnp.sum(gate_probabilities[:, :, None] * picked, axis=1))

def layer_block(parameters, input_tokens, segments, routes):
    first_norm_scale, query_weight, key_weight, value_weight, output_weight, second_norm_scale, router_weight, shared_gate_weight, shared_up_weight, shared_down_weight, expert_gate_weight, expert_up_weight, expert_down_weight = parameters
    normed_one = low(input_tokens * rms_scale(input_tokens) * first_norm_scale)
    attended = attend(normed_one, segments, query_weight, key_weight, value_weight)
    residual = input_tokens + lower_returned(product(attended, output_weight))
    second_normalized = low(residual * rms_scale(residual) * second_norm_scale)
    logits = lower_returned(product(second_normalized, router_weight))
    router_probs = jax.nn.softmax(logits, axis=-1)
    chosen = jnp.take_along_axis(router_probs, routes, axis=1)
    gate_probabilities = chosen / lax.optimization_barrier(jnp.sum(chosen, axis=-1, keepdims=True))
    shared_gate_lin = lower_returned(product(second_normalized, shared_gate_weight))
    shared_up_lin = lower_returned(product(second_normalized, shared_up_weight))
    shared = lower_returned(product(low(jax.nn.silu(shared_gate_lin) * shared_up_lin), shared_down_weight))
    routed_tokens = routed_expert_indices(second_normalized, gate_probabilities, routes, expert_gate_weight, expert_up_weight, expert_down_weight)
    return residual + shared + routed_tokens

def reference(tokens, cotangent, segment_ids, routes, norm1_gain, attn_q, attn_k, attn_v, attn_o, norm2_gain, router, shared_gate, shared_up, shared_down, expert_gate, expert_up, expert_down):
    parameters = (norm1_gain.astype(jnp.float32), attn_q.astype(jnp.float32), attn_k.astype(jnp.float32), attn_v.astype(jnp.float32), attn_o.astype(jnp.float32), norm2_gain.astype(jnp.float32), router.astype(jnp.float32), shared_gate.astype(jnp.float32), shared_up.astype(jnp.float32), shared_down.astype(jnp.float32), expert_gate.astype(jnp.float32), expert_up.astype(jnp.float32), expert_down.astype(jnp.float32))
    blocks = TOKENS // SEQ
    segment_blocks = segment_ids.reshape(blocks, SEQ)
    route_blocks = routes.reshape(blocks, SEQ, TOP)

    def layer(input_tokens, weights):

        def one_block(item):
            return layer_block(weights, item[0], item[1], item[2])
        result = lax.map(jax.checkpoint(one_block), (input_tokens.reshape(blocks, SEQ, D), segment_blocks, route_blocks))
        return result.reshape(TOKENS, D)
    result, pullback = jax.vjp(layer, tokens.astype(jnp.float32), parameters)
    grad_inputs, grads = pullback(cotangent.astype(jnp.float32))
    return (result.astype(jnp.bfloat16), grad_inputs, grads[0], grads[1], grads[2], grads[3], grads[4], grads[5], grads[6], grads[7], grads[8], grads[9], grads[10], grads[11], grads[12])
```

```python
import functools

import jax
import jax.numpy as jnp
from jax import lax
from jax.experimental import pallas as pl
from jax.experimental.pallas import tpu as pltpu
from jax.sharding import PartitionSpec as P

D = 2048
HEAD_DIM = 128
TOP = 6


epsilon = 1e-06
rope_base = 600000.0
F32 = jnp.float32
BF16 = jnp.bfloat16


def rotary_tables(length, head_width):
    half_width = head_width // 2
    frequency = rope_base ** (-(jnp.arange(half_width, dtype=jnp.float32) * 2.0 / head_width))
    angles = jnp.arange(length, dtype=jnp.float32)[:, None] * frequency[None, :]
    return (jnp.cos(angles), jnp.sin(angles))


def rotate(values, cosine, sine):
    half_width = values.shape[-1] // 2
    first_half = values[..., :half_width]
    second_half = values[..., half_width:]
    cos_rows = cosine[:, None, :]
    sin_rows = sine[:, None, :]
    return jnp.concatenate(
        [
            first_half * cos_rows - second_half * sin_rows,
            second_half * cos_rows + first_half * sin_rows,
        ],
        axis=-1,
    )


def rotate_back(gradient, cosine, sine):
    return rotate(gradient, cosine, -sine)


def norm_back(grad_normed, input_tokens, scale_rows, gain):
    grad_gain = jnp.sum(grad_normed * input_tokens * scale_rows, axis=0)
    scaled_grad = grad_normed * gain
    grad_inputs = (
        scale_rows * scaled_grad
        - input_tokens
        * scale_rows
        * scale_rows
        * scale_rows
        * jnp.mean(scaled_grad * input_tokens, axis=-1, keepdims=True)
    )
    return (grad_gain, grad_inputs)


def dot(left, right, dims):
    return lax.dot_general(left, right, (dims, ((), ())), preferred_element_type=F32)


NN = ((1,), (0,))
NT = ((1,), (1,))
TN = ((0,), (0,))


def swap(value, axis, bit):
    size = lax.axis_size(axis)
    return lax.ppermute(value, axis, [(i, i ^ bit) for i in range(size)])


ORDER = (0, 1, 7, 6, 3, 2, 5, 4)
GROUP = len(ORDER)
LANES = 128
ROW_CHUNK = 64


def expert_kernel(sizes, *refs):
    parts, experts_all, local_experts, expert_tiles, shared_tiles = sizes
    refs = list(refs)

    def take(count):
        taken = refs[:count]
        del refs[:count]
        return taken

    rows_ref, grads_ref, mask_hbm, gate_hbm, up_hbm, down_hbm = take(6)
    shared_gate_hbm, shared_up_hbm, shared_down_hbm, router_hbm = take(4)
    all_rows, all_grads, act_hbm, wide_grad_hbm, out_even, out_odd, back_ref = take(7)
    wide_v, wide_t, down_v, rows_v, grads_v, mask_v, d_act_v, act_v, wide_grad_v = take(9)
    probs_v, gates_v, total_v, out_v, back_v, own_v, core_v, relay_v, cross_v, line_in, line_out = take(11)
    send, recv, local, weight_sem, mask_sem = take(5)
    quarter = rows_ref.shape[0]
    seq_len = parts * quarter
    half_rows = seq_len // 2
    inner = down_v.shape[0]
    wide = wide_v.shape[0]
    exp_index = lax.axis_index("exp")
    tp_index = lax.axis_index("tp")
    slot = {r: s for s, r in enumerate(ORDER)}

    def part(q):
        return pl.ds(q * quarter, quarter)

    def chip(r):
        return {"exp": exp_index ^ r}

    def line(k):
        return {"tp": tp_index ^ k}

    copies = {}
    for k in range(1, parts):
        copies["z", k] = (rows_ref, all_rows.at[slot[0], part(k)], line(k))
        copies["t", k] = (line_out.at[k - 1], line_in.at[k - 1], line(k))
    for q in range(parts):
        own = rows_ref if q == 0 else all_rows.at[slot[0], part(q)]
        copies["x", q] = (own, all_rows.at[slot[2], part(q)], chip(2))
        copies["y", q] = (own, all_rows.at[slot[4], part(q)], chip(4))
        via = 2 if 2 * q < parts else 4
        copies["d", q] = (all_rows.at[slot[via], part(q)], all_rows.at[slot[6], part(q)], chip(6 - via))
        for r in (0, 2, 4, 6):
            here = own if r == 0 else all_rows.at[slot[r], part(q)]
            copies["c", r, q] = (here, all_rows.at[slot[r + 1], part(q)], chip(1))
        for side, r in enumerate((2, 4)):
            copies["s", r, q] = (back_v.at[slot[r] % 2, part(q)], cross_v.at[side, part(q)], chip(r))
    for r in (0, 2, 4, 6):
        copies["b", r] = (back_v.at[slot[r + 1] % 2], core_v.at[r // 2], chip(1))
    for side in range(2):
        copies["r", side] = (
            back_v.at[slot[6] % 2, pl.ds(side * half_rows, half_rows)],
            relay_v.at[side],
            chip(4 - 2 * side),
        )
    for h in range(2):
        part_h = pl.ds(h * half_rows, half_rows)
        mine = grads_ref.at[part_h]
        copies["gx", h] = (mine, all_grads.at[slot[2], part_h], chip(2))
        copies["gy", h] = (mine, all_grads.at[slot[4], part_h], chip(4))
        via = 4 * h + 2 * (1 - h)
        copies["gd", h] = (all_grads.at[slot[via], part_h], all_grads.at[slot[6], part_h], chip(6 - via))
        for r in (0, 2, 4, 6):
            here = mine if r == 0 else all_grads.at[slot[r], part_h]
            copies["gc", r, h] = (here, all_grads.at[slot[r + 1], part_h], chip(1))
    number = {name: k for k, name in enumerate(copies)}

    def remote(*name):
        source, target, device = copies[name]
        return pltpu.make_async_remote_copy(
            source,
            target,
            send.at[number[name]],
            recv.at[number[name]],
            device_id=device,
            device_id_type=pl.DeviceIdType.MESH,
        )

    barrier = pltpu.get_barrier_semaphore()
    peers = [line(k) for k in range(1, parts)] + [chip(r) for r in (1, 2, 4)]
    for peer in peers:
        pl.semaphore_signal(barrier, inc=1, device_id=peer, device_id_type=pl.DeviceIdType.MESH)
    pl.semaphore_wait(barrier, len(peers))

    for k in range(1, parts):
        remote("z", k).start()

    def spread(q):
        remote("x" if 2 * q < parts else "y", q).start()
        remote("c", 0, q).start()

    def spread_rest(q):
        remote("y" if 2 * q < parts else "x", q).start()

    spread(0)
    own_copy = pltpu.make_async_copy(rows_ref, all_rows.at[slot[0], part(0)], local.at[0])
    padded = expert_tiles * LANES
    hidden = down_hbm.shape[1]
    shared_rows = shared_down_hbm.shape[0]
    weights = [(shared_down_hbm, down_v.at[pl.ds(local_experts * padded, shared_rows)])]
    weights.append((router_hbm, wide_v.at[pl.ds(wide - LANES, LANES)]))
    blanks = [(down_v, local_experts * padded + shared_rows, inner)]

    def load_tiles(source, count, first_tile, side):
        for k in range(-(-count // LANES)):
            rows = min(LANES, count - k * LANES)
            place = (2 * (first_tile + k) + side) * LANES
            weights.append((source.at[pl.ds(k * LANES, rows)], wide_v.at[pl.ds(place, rows)]))
            blanks.append((wide_v, place + rows, place + LANES))

    for e in range(local_experts):
        weights.append((down_hbm.at[e], down_v.at[pl.ds(e * padded, hidden)]))
        blanks.append((down_v, e * padded + hidden, (e + 1) * padded))
        load_tiles(gate_hbm.at[e], hidden, e * expert_tiles, 0)
        load_tiles(up_hbm.at[e], hidden, e * expert_tiles, 1)
    load_tiles(shared_gate_hbm, shared_rows, local_experts * expert_tiles, 0)
    load_tiles(shared_up_hbm, shared_rows, local_experts * expert_tiles, 1)
    weight_copies = [
        pltpu.make_async_copy(source, target, weight_sem.at[k])
        for k, (source, target) in enumerate(weights)
    ]
    own_grads = pltpu.make_async_copy(grads_ref, all_grads.at[slot[0]], local.at[1])

    def load_grads(u):
        return pltpu.make_async_copy(all_grads.at[u], grads_v, local.at[2])

    def load_rows(u):
        return pltpu.make_async_copy(all_rows.at[u], rows_v, local.at[6])

    for h in range(2):
        remote("gx", 0).start() if h == 0 else remote("gy", 1).start()
        remote("gc", 0, h).start()
    own_copy.start()
    own_grads.start()
    for copy in weight_copies:
        copy.start()
    for ref, first, last in blanks:
        if last > first:
            ref[first:last] = jnp.zeros((last - first, D), BF16)

    def arrived_x(q):
        remote("x", q).wait_recv()
        if 2 * q < parts:
            remote("d", q).start()
        remote("c", 2, q).start()

    def arrived_y(q):
        remote("y", q).wait_recv()
        if 2 * q >= parts:
            remote("d", q).start()
        remote("c", 4, q).start()

    def arrived_far(q):
        remote("d", q).wait_recv()
        remote("c", 6, q).start()

    own_grads.wait()
    load_grads(0).start()
    half_parts = parts // 2

    for copy in weight_copies:
        copy.wait()

    def turn(j, _):
        place = pl.ds(pl.multiple_of(j * LANES, LANES), LANES)
        wide_t[:, place] = wide_v[place, :].T
        return 0

    lax.fori_loop(0, wide // LANES, turn, 0)

    def arrived_grads(h):
        remote("gx" if h == 0 else "gy", h).wait_recv()
        remote("gd", h).start()
        remote("gc", 2 + 2 * h, h).start()

    for q in range(1, parts):
        remote("z", q).wait_recv()
        spread(q)
        if q == half_parts - 1:
            arrived_grads(0)
            arrived_grads(1)
        if q >= half_parts:
            arrived_x(q - half_parts)
    own_copy.wait()
    load_rows(0).start()

    def mask_loads(r):
        from_exp = (lax.rem(exp_index, GROUP) ^ r) * seq_len
        return [
            pltpu.make_async_copy(
                mask_hbm.at[pl.ds(pl.multiple_of(from_exp + (tp_index ^ q) * quarter, quarter), quarter)],
                mask_v.at[part(q)],
                mask_sem.at[q],
            )
            for q in range(parts)
        ]

    def act_store(u):
        return pltpu.make_async_copy(act_v, act_hbm.at[u], local.at[3])

    def wide_store(u):
        return pltpu.make_async_copy(wide_grad_v, wide_grad_hbm.at[u], local.at[4])

    def out_store(s):
        kept = out_odd if ORDER[s] % 2 else out_even
        return pltpu.make_async_copy(out_v, kept.at[ORDER[s] // 2], local.at[5])

    def add_into(target, others):
        def chunk(i, _):
            total = None
            for ref, first in [target] + others:
                rows = pl.ds(pl.multiple_of(first + i * ROW_CHUNK, ROW_CHUNK), ROW_CHUNK)
                value = ref[rows].astype(F32)
                total = value if total is None else total + value
            ref, first = target
            ref[pl.ds(pl.multiple_of(first + i * ROW_CHUNK, ROW_CHUNK), ROW_CHUNK)] = total.astype(BF16)
            return 0

        return chunk

    def sum_rows(count, target, others):
        lax.fori_loop(0, count // ROW_CHUNK, add_into(target, others), 0)

    def unit(u, _):
        into = lax.rem(u, 2)

        for s in range(GROUP):
            @pl.when(u == s)
            def _(s=s):
                for load in mask_loads(ORDER[s]):
                    load.start()

        load_grads(u).wait()
        grads = grads_v

        def d_act_tile(first, width):
            d_act_v[:, pl.ds(first, width)] = dot(
                grads[...], down_v[pl.ds(first, width), :], NT
            )

        for first in range(0, inner, 512):
            d_act_tile(first, min(512, inner - first))
        load_rows(u).wait()
        for load in mask_loads(0):
            load.wait()

        @pl.when(u > 0)
        def _():
            act_store(u - 1).wait()
            wide_store(u - 1).wait()

        shared_first = local_experts * expert_tiles
        linear = dot(rows_v[...], wide_t[:, shared_first * 256 :], NN)
        logits = linear[:, shared_tiles * 256 :]
        lane = lax.broadcasted_iota(jnp.int32, logits.shape, 1)
        logits = jnp.where(lane < experts_all, logits, -1e30)
        raised = jnp.exp(logits - jnp.max(logits, axis=1, keepdims=True))
        probs = raised / jnp.sum(raised, axis=1, keepdims=True)
        mask = mask_v[...].astype(F32)
        chosen = probs * mask
        chosen_sum = jnp.sum(chosen, axis=1, keepdims=True)
        probs_v[...] = probs
        gates_v[...] = chosen / chosen_sum

        def tile(linear, at, j, gate):
            one = pl.ds(j * LANES, LANES)
            for first in range(0, seq_len, ROW_CHUNK):
                last = first + ROW_CHUNK
                gate_lin = linear[first:last, at : at + LANES]
                up_lin = linear[first:last, at + LANES : at + 256]
                sigmoid = 1.0 / (1.0 + jnp.exp(-gate_lin))
                silu = gate_lin * sigmoid
                act = silu * up_lin
                d_act = d_act_v[first:last, one]
                if gate is not None:
                    total_v[first:last] += act.astype(BF16).astype(F32) * d_act
                    act = act * gate[first:last]
                    d_act = d_act * gate[first:last]
                act_v[first:last, one] = act.astype(BF16)
                d_gate = d_act * up_lin * (sigmoid * (1.0 + gate_lin * (1.0 - sigmoid)))
                wide_grad_v[first:last, pl.ds(j * 256, LANES)] = d_gate.astype(BF16)
                wide_grad_v[first:last, pl.ds(j * 256 + LANES, LANES)] = (d_act * silu).astype(BF16)

        for k in range(shared_tiles):
            tile(linear, k * 256, shared_first + k, None)
        d_gates = jnp.zeros(logits.shape, F32)
        for e in range(local_experts):
            mine = lane == exp_index * local_experts + e
            gate = jnp.sum(jnp.where(mine, gates_v[...], 0.0), axis=1, keepdims=True)
            total_v[...] = jnp.zeros(logits.shape, F32)
            first_tile = e * expert_tiles
            linear = dot(rows_v[...], wide_t[:, first_tile * 256 : (first_tile + expert_tiles) * 256], NN)
            for k in range(expert_tiles):
                tile(linear, k * 256, first_tile + k, gate)
            d_gates = jnp.where(mine, jnp.sum(total_v[...], axis=1, keepdims=True), d_gates)
        probs, gates, mask = probs_v[...], gates_v[...], mask_v[...].astype(F32)
        chosen_sum = jnp.sum(probs * mask, axis=1, keepdims=True)
        d_gates = d_gates * mask
        d_chosen = (d_gates - jnp.sum(d_gates * gates, axis=1, keepdims=True)) / chosen_sum
        d_probs = d_chosen * mask
        d_logits = probs * (d_probs - jnp.sum(d_probs * probs, axis=1, keepdims=True))
        high = d_logits.astype(BF16)
        low = pltpu.roll(d_logits - high.astype(F32), experts_all, 1)
        wide_grad_v[:, pl.ds(wide - LANES, LANES)] = jnp.where(
            lane < experts_all, high.astype(F32), low
        ).astype(BF16)
        act_store(u).start()
        wide_store(u).start()

        @pl.when(u == 0)
        def _():
            remote("gd", 0).wait_recv()
            remote("gc", 6, 0).start()

        @pl.when(u == 1)
        def _():
            remote("gd", 1).wait_recv()
            remote("gc", 6, 1).start()
            for q in range(half_parts):
                arrived_far(q)

        @pl.when(u == 3)
        def _():
            remote("gx", 1).wait_recv()
            remote("gc", 2, 1).start()
            for q in range(half_parts, parts):
                arrived_x(q)

        @pl.when(u == 4)
        def _():
            remote("gy", 0).wait_recv()
            remote("gc", 4, 0).start()
            for q in range(half_parts):
                arrived_y(q)

        @pl.when(u == 3)
        def _():
            remote("b", 0).wait_send()

        @pl.when(u == 4)
        def _():
            remote("b", 6).wait_send()

        @pl.when(u == 5)
        def _():
            remote("r", 0).wait_send()
            remote("r", 1).wait_send()

        @pl.when(u == 6)
        def _():
            remote("b", 2).wait_send()

        @pl.when(u == 7)
        def _():
            for q in range(parts):
                remote("s", 2, q).wait_send()

        back = back_v.at[into]

        def back_step(n, _):
            columns = pl.ds(pl.multiple_of(n * 512, 512), 512)
            back[:, columns] = dot(wide_grad_v[...], wide_v[:, columns], NN).astype(BF16)
            return 0

        lax.fori_loop(0, D // 512, back_step, 0)

        @pl.when(u == 0)
        def _():
            own_v[...] = back_v[0]

        @pl.when(u == slot[1])
        def _():
            remote("b", 0).start()

        @pl.when(u == slot[7])
        def _():
            remote("b", 6).start()

        @pl.when(u == slot[6])
        def _():
            remote("b", 6).wait_recv()
            sum_rows(seq_len, (back_v.at[slot[6] % 2], 0), [(core_v.at[3], 0)])
            remote("r", 0).start()
            remote("r", 1).start()

        @pl.when(u == slot[3])
        def _():
            remote("b", 2).start()

        @pl.when(u == slot[2])
        def _():
            remote("b", 2).wait_recv()
            remote("r", 0).wait_recv()
            mine = back_v.at[slot[2] % 2]
            sum_rows(half_rows, (mine, 0), [(core_v.at[1], 0), (relay_v.at[0], 0)])
            sum_rows(half_rows, (mine, half_rows), [(core_v.at[1], half_rows)])
            for q in range(parts):
                remote("s", 2, q).start()

        @pl.when(u == slot[5])
        def _():
            remote("b", 4).start()

        @pl.when(u == slot[4])
        def _():
            remote("b", 4).wait_recv()
            remote("r", 1).wait_recv()
            mine = back_v.at[slot[4] % 2]
            sum_rows(half_rows, (mine, half_rows), [(core_v.at[2], half_rows), (relay_v.at[1], 0)])
            sum_rows(half_rows, (mine, 0), [(core_v.at[2], 0)])
            for q in range(parts - 1, -1, -1):
                remote("s", 4, q).start()

        @pl.when(u == 0)
        def _():
            for q in range(half_parts, parts):
                arrived_y(q)
            remote("gy", 0).start()
            remote("gx", 1).start()
            for q in range(parts):
                spread_rest(q)
                remote("c", 0, q).wait_recv()
            for h in range(2):
                remote("gc", 0, h).wait_recv()

        for k, r in ((1, 6), (3, 2), (5, 4)):
            @pl.when(u == k)
            def _(k=k, r=r):
                if k == 1:
                    for q in range(half_parts, parts):
                        arrived_far(q)
                for q in range(parts):
                    remote("c", r, q).wait_recv()
                for h in range(2):
                    remote("gc", r, h).wait_recv()

        @pl.when(u < GROUP - 1)
        def _():
            load_grads(u + 1).start()
            load_rows(u + 1).start()

        @pl.when(u > 0)
        def _():
            out_store(0).wait()

        def out_step(n, _):
            columns = pl.ds(pl.multiple_of(n * 512, 512), 512)
            out_v[:, columns] = dot(act_v[...], down_v[:, columns], NN).astype(BF16)
            return 0

        lax.fori_loop(0, D // 512, out_step, 0)
        for s in range(GROUP):
            @pl.when(u == s)
            def _(s=s):
                out_store(s).start()

        return 0

    lax.fori_loop(0, GROUP, unit, 0)

    remote("b", 0).wait_recv()
    for q in range(parts - 1, -1, -1):
        remote("s", 2, q).wait_recv()
        remote("s", 4, q).wait_recv()
        first = q * quarter
        sources = [(own_v, first), (core_v.at[0], first), (cross_v.at[0], first), (cross_v.at[1], first)]

        def total_step(i, _, q=q, sources=sources):
            total = None
            for ref, start in sources:
                rows = pl.ds(pl.multiple_of(start + i * ROW_CHUNK, ROW_CHUNK), ROW_CHUNK)
                value = ref[rows].astype(F32)
                total = value if total is None else total + value
            rows = pl.ds(pl.multiple_of(i * ROW_CHUNK, ROW_CHUNK), ROW_CHUNK)
            if q == 0:
                back_ref[rows] = total
            else:
                line_out[q - 1, rows] = total.astype(BF16)
            return 0

        lax.fori_loop(0, quarter // ROW_CHUNK, total_step, 0)
        if q:
            remote("t", q).start()
    for k in range(parts - 1, 0, -1):
        remote("t", k).wait_recv()

    def last_step(i, _):
        rows = pl.ds(pl.multiple_of(i * ROW_CHUNK, ROW_CHUNK), ROW_CHUNK)
        total = back_ref[rows]
        for k in range(1, parts):
            total = total + line_in[k - 1, rows].astype(F32)
        back_ref[rows] = total
        return 0

    lax.fori_loop(0, quarter // ROW_CHUNK, last_step, 0)

    act_store(GROUP - 1).wait()
    wide_store(GROUP - 1).wait()
    out_store(GROUP - 1).wait()
    waited = [("b", 0), ("b", 6), ("r", 0), ("r", 1), ("b", 2)] + [("s", 2, q) for q in range(parts)]
    for name in copies:
        if name not in waited:
            remote(*name).wait_send()


def expert_layer(rows, grads, mask, weights, sizes):
    parts, _, local_experts, expert_tiles, shared_tiles = sizes
    quarter = rows.shape[0]
    seq_len = parts * quarter
    inner = (local_experts * expert_tiles + shared_tiles) * LANES
    wide = 2 * inner + LANES
    loads = 2 + local_experts * (1 + 2 * expert_tiles) + 2 * shared_tiles
    copies = 2 * (parts - 1) + 9 * parts + 6 + 14
    hbm = pl.BlockSpec(memory_space=pl.ANY)
    every = jax.ShapeDtypeStruct((GROUP, seq_len, D), BF16)
    some = jax.ShapeDtypeStruct((GROUP // 2, seq_len, D), BF16)
    flops = 2 * GROUP * seq_len * D * (2 * wide + 2 * inner)
    return pl.pallas_call(
        functools.partial(expert_kernel, sizes),
        out_shape=(
            every,
            every,
            jax.ShapeDtypeStruct((GROUP, seq_len, inner), BF16),
            jax.ShapeDtypeStruct((GROUP, seq_len, wide), BF16),
            some,
            some,
            jax.ShapeDtypeStruct((quarter, D), F32),
        ),
        in_specs=[hbm] * (3 + len(weights)),
        out_specs=(hbm,) * 6 + (pl.BlockSpec(memory_space=pltpu.VMEM),),
        scratch_shapes=[
            pltpu.VMEM((wide, D), BF16),
            pltpu.VMEM((D, wide), BF16),
            pltpu.VMEM((inner, D), BF16),
            pltpu.VMEM((seq_len, D), BF16),
            pltpu.VMEM((seq_len, D), BF16),
            pltpu.VMEM((seq_len, LANES), BF16),
            pltpu.VMEM((seq_len, inner), F32),
            pltpu.VMEM((seq_len, inner), BF16),
            pltpu.VMEM((seq_len, wide), BF16),
            pltpu.VMEM((seq_len, LANES), F32),
            pltpu.VMEM((seq_len, LANES), F32),
            pltpu.VMEM((seq_len, LANES), F32),
            pltpu.VMEM((seq_len, D), BF16),
            pltpu.VMEM((2, seq_len, D), BF16),
            pltpu.VMEM((seq_len, D), BF16),
            pltpu.VMEM((GROUP // 2, seq_len, D), BF16),
            pltpu.VMEM((2, seq_len // 2, D), BF16),
            pltpu.VMEM((2, seq_len, D), BF16),
            pltpu.VMEM((parts - 1, quarter, D), BF16),
            pltpu.VMEM((parts - 1, quarter, D), BF16),
            pltpu.SemaphoreType.DMA((copies,)),
            pltpu.SemaphoreType.DMA((copies,)),
            pltpu.SemaphoreType.DMA((8,)),
            pltpu.SemaphoreType.DMA((loads,)),
            pltpu.SemaphoreType.DMA((parts,)),
        ],
        compiler_params=pltpu.CompilerParams(
            collective_id=1, has_side_effects=True, vmem_limit_bytes=60 * 1024 * 1024
        ),
        cost_estimate=pl.CostEstimate(flops=flops, bytes_accessed=120_000_000, transcendentals=0),
        name="experts",
    )(rows, grads, mask, *weights)


def line_rows(own_rows):
    parts = lax.axis_size("tp")
    return [own_rows] + [swap(own_rows, "tp", k) for k in range(1, parts)]


def add_cores(even, odd_swapped):
    return [(e.astype(F32) + o.astype(F32)).astype(BF16) for e, o in zip(even, odd_swapped)]


def far_halves(mine):
    half = mine[3].shape[0] // 2
    return swap(mine[3][:half], "exp", 4), swap(mine[3][half:], "exp", 2)


def near_sums(mine, far):
    half = mine[3].shape[0] // 2
    first = jnp.concatenate([mine[1][:half] + far[0], mine[1][half:]], axis=0)
    second = jnp.concatenate([mine[2][:half], mine[2][half:] + far[1]], axis=0)
    return swap(first, "exp", 2), swap(second, "exp", 4)


def line_sums(mine, near):
    parts = lax.axis_size("tp")
    total = mine[0].astype(F32) + near[0].astype(F32) + near[1].astype(F32)
    total = total.reshape(parts, -1, total.shape[1])
    low = total.astype(BF16)
    result = total[0]
    for k in range(1, parts):
        result = result + swap(low[k], "tp", k).astype(F32)
    return result


def neighbours(parts):
    exp_index, tp_index = lax.axis_index("exp"), lax.axis_index("tp")
    line = [{"tp": tp_index ^ k} for k in range(1, parts)]
    return line, [{"exp": exp_index ^ r} for r in range(1, GROUP)]


def greet(peers):
    barrier = pltpu.get_barrier_semaphore()
    for peer in peers:
        pl.semaphore_signal(barrier, inc=1, device_id=peer, device_id_type=pl.DeviceIdType.MESH)
    pl.semaphore_wait(barrier, len(peers))


def remote_maker(copies, send, recv):
    number = {name: k for k, name in enumerate(copies)}

    def remote(*name):
        source, target, device = copies[name]
        return pltpu.make_async_remote_copy(
            source,
            target,
            send.at[number[name]],
            recv.at[number[name]],
            device_id=device,
            device_id_type=pl.DeviceIdType.MESH,
        )

    return remote


def gather_kernel(parts, *refs):
    tokens_ref, proj_ref, out_ref, mask_ref, gate_ref, up_ref, down_ref = refs[:7]
    tokens_all, proj_all, out_all, mask_all, gate_all, up_all, down_all = refs[7:14]
    send, recv, local = refs[14:]
    exp_index, tp_index = lax.axis_index("exp"), lax.axis_index("tp")
    line, near = neighbours(parts)
    quarter, depth, seq_len = tokens_ref.shape[0], proj_ref.shape[0], mask_ref.shape[0]
    width = down_ref.shape[2]

    def block(whole, size, r, axis=0):
        place = pl.ds(pl.multiple_of((exp_index ^ r) * size, size), size)
        return whole.at[place] if axis == 0 else whole.at[:, place]

    def arrays(r):
        return {
            "p": block(proj_all, depth, r),
            "o": block(out_all, out_ref.shape[1], r, 1),
            "m": block(mask_all, seq_len, r),
        }

    own = {"p": proj_ref, "o": out_ref, "m": mask_ref}
    my_rows = pl.ds(pl.multiple_of(tp_index * quarter, quarter), quarter)
    copies = {}
    def rows_from(s):
        return tokens_all.at[pl.ds(s * quarter, quarter)]

    for s in range(parts):
        for step in (1, -1):
            copies["z", s, step] = (rows_from(s), rows_from(s), {"tp": tp_index + step})
    for key, ref in own.items():
        mine = arrays(0)[key]
        copies["g", 2, key] = (ref, mine, near[1])
        copies["g", 4, key] = (ref, mine, near[3])
        via = 2 if key == "p" else 4
        passed = arrays(via)[key]
        copies["g", 6, key] = (passed, passed, near[5 - via])
        copies["c", 0, key] = (ref, mine, near[0])
        for r in (2, 4, 6):
            copies["c", r, key] = (arrays(r)[key], arrays(r)[key], near[0])
    for r in range(1, GROUP):
        to = exp_index ^ r
        copies["a", r, 0] = (gate_ref.at[to], block(gate_all, width, 0, 1), near[r - 1])
        copies["a", r, 1] = (up_ref.at[to], block(up_all, width, 0, 1), near[r - 1])
        copies["a", r, 2] = (down_ref.at[to], block(down_all, width, 0, 1), near[r - 1])
    remote = remote_maker(copies, send, recv)

    greet(line + near)
    for key in own:
        for r in (2, 4):
            remote("g", r, key).start()
        remote("c", 0, key).start()
    mine = pltpu.make_async_copy(tokens_ref, tokens_all.at[my_rows], local.at[6])
    mine.start()
    mine.wait()

    def at_each_place(body):
        for z in range(parts):
            pl.when(tp_index == z)(functools.partial(body, z))

    def first_hop(z):
        for step in (1, -1):
            if 0 <= z + step < parts:
                remote("z", z, step).start()

    def hop(d, z):
        for step in (1, -1):
            s = z - step * d
            if 0 <= s < parts:
                remote("z", s, step).wait_recv()
                if 0 <= z + step < parts:
                    remote("z", s, step).start()

    def sent(z):
        for step in (1, -1):
            if 0 <= z + step < parts:
                for s in range(z + 1) if step == 1 else range(z, parts):
                    remote("z", s, step).wait_send()

    at_each_place(first_hop)
    kept = [
        (proj_ref, arrays(0)["p"]),
        (out_ref, arrays(0)["o"]),
        (mask_ref, arrays(0)["m"]),
        (gate_ref.at[exp_index], block(gate_all, width, 0, 1)),
        (up_ref.at[exp_index], block(up_all, width, 0, 1)),
        (down_ref.at[exp_index], block(down_all, width, 0, 1)),
    ]
    kept = [pltpu.make_async_copy(s, t, local.at[k]) for k, (s, t) in enumerate(kept)]
    for copy in kept:
        copy.start()
    at_each_place(functools.partial(hop, 1))
    for key in own:
        for r in (2, 4):
            remote("g", r, key).wait_recv()
            if r == (2 if key == "p" else 4):
                remote("g", 6, key).start()
            remote("c", r, key).start()
    for r in range(1, GROUP):
        for k in range(3):
            remote("a", r, k).start()
    at_each_place(functools.partial(hop, 2))
    for key in own:
        remote("g", 6, key).wait_recv()
        remote("c", 6, key).start()
    for d in range(3, parts):
        at_each_place(functools.partial(hop, d))
    for copy in kept:
        copy.wait()
    for name in copies:
        if name[0] in "ca":
            remote(*name).wait_recv()
    at_each_place(sent)
    for name in copies:
        if name[0] != "z":
            remote(*name).wait_send()


def gather_inputs(tokens, proj, out, mask, gate, up, down):
    parts = lax.axis_size("tp")
    hbm = pl.BlockSpec(memory_space=pl.ANY)
    depth, seq_len = proj.shape[0], mask.shape[0]
    shapes = [
        (parts * tokens.shape[0], D),
        (GROUP * depth, proj.shape[1]),
        (out.shape[0], GROUP * out.shape[1]),
        (GROUP * seq_len, LANES),
        *((w.shape[1], GROUP * w.shape[2]) for w in (gate, up, down)),
    ]
    copies = 2 * parts + 3 * 7 + 3 * (GROUP - 1)
    return pl.pallas_call(
        functools.partial(gather_kernel, parts),
        out_shape=tuple(jax.ShapeDtypeStruct(s, BF16) for s in shapes),
        in_specs=[hbm] * 7,
        out_specs=(hbm,) * 7,
        scratch_shapes=[
            pltpu.SemaphoreType.DMA((copies,)),
            pltpu.SemaphoreType.DMA((copies,)),
            pltpu.SemaphoreType.DMA((7,)),
        ],
        compiler_params=pltpu.CompilerParams(collective_id=2, has_side_effects=True),
        name="gather_inputs",
    )(tokens, proj, out, mask, gate, up, down)


def scatter_kernel(parts, *refs):
    proj_ref, out_ref, gate_ref, up_ref, down_ref = refs[:5]
    proj_sum, out_sum, gate_back, up_back, down_back = refs[5:10]
    proj_core, out_core, proj_add, out_add, proj_relay, out_relay = refs[10:16]
    proj_cross, out_cross, narrow, narrow_in, send, recv, local = refs[16:]
    exp_index = lax.axis_index("exp")
    line, near = neighbours(parts)
    depth, width = proj_sum.shape[0], out_sum.shape[1]

    def proj_block(r):
        return proj_ref.at[pl.ds(pl.multiple_of((exp_index ^ r) * depth, depth), depth)]

    def out_block(r):
        return out_ref.at[:, pl.ds(pl.multiple_of((exp_index ^ r) * width, width), width)]

    copies = {}
    for r in (6, 2, 4, 0):
        copies["c", r, 0] = (proj_block(r + 1), proj_core.at[r // 2], near[0])
        copies["c", r, 1] = (out_block(r + 1), out_core.at[r // 2], near[0])
    copies["d", 0] = (proj_add.at[2], proj_relay, near[3])
    copies["d", 1] = (out_add.at[2], out_relay, near[1])
    for side, r in enumerate((2, 4)):
        copies["s", r, 0] = (proj_add.at[side], proj_cross.at[side], near[r - 1])
        copies["s", r, 1] = (out_add.at[side], out_cross.at[side], near[r - 1])
    for k in range(1, parts):
        copies["z", k] = (narrow, narrow_in.at[k - 1], line[k - 1])
    for r in range(1, GROUP):
        to = exp_index ^ r
        copies["a", r, 0] = (gate_ref.at[to], gate_back.at[exp_index], near[r - 1])
        copies["a", r, 1] = (up_ref.at[to], up_back.at[exp_index], near[r - 1])
        copies["a", r, 2] = (down_ref.at[to], down_back.at[exp_index], near[r - 1])
    remote = remote_maker(copies, send, recv)

    def total(target, sources):
        count = target.shape[0]

        def chunk(i, _):
            rows = pl.ds(pl.multiple_of(i * ROW_CHUNK, ROW_CHUNK), ROW_CHUNK)
            value = sum(ref[rows].astype(F32) for ref in sources[1:])
            target[rows] = (sources[0][rows].astype(F32) + value).astype(target.dtype)
            return 0

        lax.fori_loop(0, count // ROW_CHUNK, chunk, 0)

    greet(line + near)
    for r in (6, 2, 4, 0):
        for k in range(2):
            remote("c", r, k).start()
    for k in range(2):
        remote("c", 6, k).wait_recv()
    total(proj_add.at[2], [proj_block(6), proj_core.at[3]])
    remote("d", 0).start()
    total(out_add.at[2], [out_block(6), out_core.at[3]])
    remote("d", 1).start()
    for r in (2, 4):
        for k in range(2):
            remote("c", r, k).wait_recv()
    total(out_add.at[0], [out_block(2), out_core.at[1]])
    remote("s", 2, 1).start()
    total(proj_add.at[1], [proj_block(4), proj_core.at[2]])
    remote("s", 4, 0).start()
    remote("d", 0).wait_recv()
    total(proj_add.at[0], [proj_block(2), proj_core.at[1], proj_relay])
    remote("s", 2, 0).start()
    remote("d", 1).wait_recv()
    total(out_add.at[1], [out_block(4), out_core.at[2], out_relay])
    remote("s", 4, 1).start()
    kept = [
        pltpu.make_async_copy(source.at[exp_index], target.at[exp_index], local.at[k])
        for k, (source, target) in enumerate(
            ((gate_ref, gate_back), (up_ref, up_back), (down_ref, down_back))
        )
    ]
    for copy in kept:
        copy.start()
    for r in range(1, GROUP):
        for k in range(3):
            remote("a", r, k).start()
    for k in range(2):
        remote("c", 0, k).wait_recv()
        for r in (2, 4):
            remote("s", r, k).wait_recv()
        if k == 0:
            total(proj_sum, [proj_block(0), proj_core.at[0], proj_cross.at[0], proj_cross.at[1]])
            narrow[...] = proj_sum[:, proj_sum.shape[1] - LANES :]
            for j in range(1, parts):
                remote("z", j).start()
        else:
            total(out_sum, [out_block(0), out_core.at[0], out_cross.at[0], out_cross.at[1]])
    for j in range(1, parts):
        remote("z", j).wait_recv()
    value = narrow[...]
    for j in range(1, parts):
        value = value + narrow_in[j - 1]
    proj_sum[:, proj_sum.shape[1] - LANES :] = value
    for copy in kept:
        copy.wait()
    for r in range(1, GROUP):
        for k in range(3):
            remote("a", r, k).wait_recv()
    for name in copies:
        remote(*name).wait_send()


def scatter_grads(proj, out, gate, up, down):
    parts = lax.axis_size("tp")
    hbm, vmem = pl.BlockSpec(memory_space=pl.ANY), pl.BlockSpec(memory_space=pltpu.VMEM)
    one = (proj.shape[0] // GROUP, proj.shape[1])
    two = (out.shape[0], out.shape[1] // GROUP)
    narrow = (one[0], LANES)
    copies = 8 + 2 + 4 + (parts - 1) + 3 * (GROUP - 1)
    return pl.pallas_call(
        functools.partial(scatter_kernel, parts),
        out_shape=(
            jax.ShapeDtypeStruct(one, F32),
            jax.ShapeDtypeStruct(two, F32),
            *(jax.ShapeDtypeStruct(x.shape, x.dtype) for x in (gate, up, down)),
        ),
        in_specs=[vmem] * 2 + [hbm] * 3,
        out_specs=(vmem, vmem, hbm, hbm, hbm),
        scratch_shapes=[
            pltpu.VMEM((GROUP // 2, *one), BF16),
            pltpu.VMEM((GROUP // 2, *two), BF16),
            pltpu.VMEM((3, *one), BF16),
            pltpu.VMEM((3, *two), BF16),
            pltpu.VMEM(one, BF16),
            pltpu.VMEM(two, BF16),
            pltpu.VMEM((2, *one), BF16),
            pltpu.VMEM((2, *two), BF16),
            pltpu.VMEM(narrow, F32),
            pltpu.VMEM((parts - 1, *narrow), F32),
            pltpu.SemaphoreType.DMA((copies,)),
            pltpu.SemaphoreType.DMA((copies,)),
            pltpu.SemaphoreType.DMA((3,)),
        ],
        compiler_params=pltpu.CompilerParams(
            collective_id=3, has_side_effects=True, vmem_limit_bytes=40 * 1024 * 1024
        ),
        name="scatter_grads",
    )(proj, out, gate, up, down)


def pad_to(value, axis, multiple):
    widths = [(0, 0)] * value.ndim
    widths[axis] = (0, -value.shape[axis] % multiple)
    return jnp.pad(value, widths)


def shards(
    tokens,
    cotangent,
    segment_ids,
    routes,
    norm1_gain,
    attn_q,
    attn_k,
    attn_v,
    attn_o,
    norm2_gain,
    router,
    shared_gate,
    shared_up,
    shared_down,
    expert_gate,
    expert_up,
    expert_down,
):
    exp_count = lax.axis_size("exp")
    tp_count = lax.axis_size("tp")
    exp_index = lax.axis_index("exp")
    tp_index = lax.axis_index("tp")
    quarter = tokens.shape[0]
    seq_len = quarter * tp_count

    experts_all = router.shape[1]
    local_experts, _, hidden = expert_gate.shape
    shared_hidden = shared_gate.shape[1] // exp_count
    in_group = exp_count == GROUP
    qkv_widths = (attn_q.shape[1], attn_k.shape[1], attn_v.shape[1])
    gains = jnp.stack([norm1_gain, norm2_gain], axis=1)
    proj = jnp.concatenate([attn_q, attn_k, attn_v, router, gains], axis=1)
    qkv_width = sum(qkv_widths)
    proj = pad_to(proj, 1, LANES)
    member_lanes = jnp.any(
        routes[:, :, None] == jnp.arange(LANES, dtype=jnp.int32), axis=1
    ).astype(BF16)

    def cut(weight):
        return pad_to(weight.reshape(exp_count, shared_hidden, -1), 1, 16)

    cut_gate, cut_up, cut_down = cut(shared_gate.T), cut(shared_up.T), cut(shared_down)
    if in_group:
        whole, proj, output_weight, all_masks, my_gate, my_up, my_down = gather_inputs(
            tokens, proj, attn_o, member_lanes, cut_gate, cut_up, cut_down
        )
    else:
        whole = lax.all_gather(tokens, "tp", axis=0, tiled=True)
        proj = lax.all_gather(proj, "exp", axis=0, tiled=True)
        output_weight = lax.all_gather(attn_o, "exp", axis=1, tiled=True)
        all_masks = lax.all_gather(member_lanes, "exp", axis=0, tiled=True)
        my_gate, my_up, my_down = (
            lax.all_to_all(w, "exp", split_axis=0, concat_axis=2, tiled=True)
            for w in (cut_gate, cut_up, cut_down)
        )
        my_gate, my_up, my_down = my_gate[0], my_up[0], my_down[0]
    qkv_weight = proj[:, :qkv_width]
    narrow_weight = proj[:, qkv_width:].T
    first_norm_scale = narrow_weight[experts_all].astype(F32)
    second_norm_scale = narrow_weight[experts_all + 1].astype(F32)
    whole, cotangent = lax.optimization_barrier((whole, cotangent))
    grads_line = line_rows(cotangent)

    own_tokens = tokens.astype(F32)
    whole = whole.astype(F32)
    scale_one = lax.rsqrt(jnp.mean(whole * whole, axis=-1, keepdims=True) + epsilon)
    normed_one = (whole * scale_one * first_norm_scale).astype(BF16)
    heads_dev = qkv_widths[0] // HEAD_DIM
    kv_dev = qkv_widths[1] // HEAD_DIM
    group_size = heads_dev // kv_dev
    score_scale = HEAD_DIM ** (-0.5)
    cosine, sine = rotary_tables(seq_len, HEAD_DIM)
    qkv_lin = dot(normed_one, qkv_weight, NN).reshape(seq_len, -1, HEAD_DIM)
    turned = rotate(qkv_lin[:, : heads_dev + kv_dev], cosine, sine).astype(BF16)
    queries = turned[:, :heads_dev].reshape(seq_len, kv_dev, group_size, HEAD_DIM)
    keys_rot = turned[:, heads_dev:]
    values = qkv_lin[:, heads_dev + kv_dev :].astype(BF16)
    positions = jnp.arange(seq_len, dtype=jnp.int32)
    allowed = (positions[None, :] <= positions[:, None]) & (
        segment_ids[:, None] == segment_ids[None, :]
    )
    raw_scores = jnp.einsum("qkgd,ckd->kgqc", queries, keys_rot, preferred_element_type=F32)
    scores = jnp.where(allowed, raw_scores * score_scale, -1e30)
    exponent = jnp.exp(scores - jnp.max(scores, axis=-1, keepdims=True))
    probs = exponent / jnp.sum(exponent, axis=-1, keepdims=True)
    probs_low = probs.astype(BF16)
    attended = jnp.einsum("kgqc,ckd->qkgd", probs_low, values, preferred_element_type=F32)
    attended = attended.reshape(seq_len, heads_dev * HEAD_DIM).astype(BF16)
    attended, *grads_line[1:-1] = lax.optimization_barrier((attended, *grads_line[1:-1]))
    attn_mine = lax.psum_scatter(
        dot(attended, output_weight, NN).astype(BF16), "tp", scatter_dimension=0, tiled=True
    )

    residual = own_tokens + attn_mine.astype(F32)
    scale_two = lax.rsqrt(jnp.mean(residual * residual, axis=-1, keepdims=True) + epsilon)
    normed_two = (residual * scale_two * second_norm_scale).astype(BF16)
    expert_tiles, shared_tiles = -(-hidden // LANES), -(-my_gate.shape[0] // LANES)
    router_rows = narrow_weight[:experts_all]
    router_pad = jnp.zeros((LANES - 2 * experts_all, D), BF16)
    weights = (
        expert_gate.transpose(0, 2, 1),
        expert_up.transpose(0, 2, 1),
        expert_down,
        my_gate,
        my_up,
        my_down,
        jnp.concatenate([router_rows, router_rows, router_pad], axis=0),
    )
    inner = (local_experts * expert_tiles + shared_tiles) * LANES
    wide = 2 * inner + LANES
    sizes = (tp_count, experts_all, local_experts, expert_tiles, shared_tiles)
    all_masks = all_masks.reshape(exp_count // GROUP, -1, LANES)

    output = residual
    d_normed_two, wide_sum, down_sum = 0.0, 0.0, 0.0
    for base in range(0, exp_count, GROUP):
        rows_b = normed_two
        if base:
            rows_b, grads_line = swap(rows_b, "exp", base), line_rows(swap(cotangent, "exp", base))
        masks = lax.dynamic_index_in_dim(
            all_masks, (exp_index // GROUP) ^ (base // GROUP), keepdims=False
        )
        all_rows, all_grads, act, wide_grads, out_even, out_odd, back = expert_layer(
            rows_b, jnp.concatenate(grads_line, axis=0), masks, weights, sizes
        )
        swapped = swap(out_odd, "exp", 1)
        d_normed_two = d_normed_two + (swap(back, "exp", base) if base else back)
        count = GROUP * seq_len
        grads_seen, act = all_grads.reshape(count, D), act.reshape(count, -1)
        rows_seen, wide_grads = all_rows.reshape(count, D), wide_grads.reshape(count, wide)
        if base + GROUP < exp_count:
            wide_sum = wide_sum + dot(wide_grads, rows_seen, TN)
            down_sum = down_sum + dot(act, grads_seen, TN)
            mine = add_cores(out_even, swapped)
            part_out = line_sums(mine, near_sums(mine, far_halves(mine)))
            output = output + (swap(part_out, "exp", base) if base else part_out)
            cotangent, normed_two, wide_sum, down_sum, output = lax.optimization_barrier(
                (cotangent, normed_two, wide_sum, down_sum, output)
            )
    down_sum = down_sum + dot(act, grads_seen, TN)
    swapped, down_sum = lax.optimization_barrier((swapped, down_sum))

    grad_gain_two, d_residual = norm_back(d_normed_two, residual, scale_two, second_norm_scale)
    d_residual = cotangent.astype(F32) + d_residual

    d_attn_low = lax.all_gather(d_residual.astype(BF16), "tp", axis=0, tiled=True)
    mine = add_cores(out_even, swapped)
    d_attn_low, *far = lax.optimization_barrier((d_attn_low, *far_halves(mine)))
    near = near_sums(mine, far)
    grad_out_w = dot(attended, d_attn_low, TN)
    d_attended = dot(d_attn_low, output_weight, NT).astype(BF16)
    d_attended = d_attended.reshape(seq_len, kv_dev, group_size, HEAD_DIM)
    d_probs_att = jnp.einsum("qkgd,ckd->kgqc", d_attended, values, preferred_element_type=F32)
    row_inner = jnp.sum(d_probs_att * probs, axis=-1, keepdims=True)
    d_raw = (probs * (d_probs_att - row_inner) * score_scale).astype(BF16)
    d_query = jnp.einsum("kgqc,ckd->qkgd", d_raw, keys_rot, preferred_element_type=F32).reshape(
        seq_len, heads_dev, HEAD_DIM
    )
    d_key = jnp.einsum("kgqc,qkgd->ckd", d_raw, queries, preferred_element_type=F32)
    d_value = jnp.einsum("kgqc,qkgd->ckd", probs_low, d_attended, preferred_element_type=F32)
    d_qkv = jnp.concatenate(
        [
            rotate_back(jnp.concatenate([d_query, d_key], axis=1), cosine, sine).astype(BF16),
            d_value.astype(BF16),
        ],
        axis=1,
    ).reshape(seq_len, -1)
    d_normed_one = dot(d_qkv, qkv_weight, NT).astype(BF16)
    d_normed_one, wide_grads = lax.optimization_barrier((d_normed_one, wide_grads))
    d_normed_one = lax.psum_scatter(
        d_normed_one, "tp", scatter_dimension=0, tiled=True
    ).astype(F32)
    grad_qkv = dot(normed_one, d_qkv, TN)
    wide_sum = wide_sum + dot(wide_grads, rows_seen, TN)
    d_normed_one, *near = lax.optimization_barrier((d_normed_one, *near))

    def rows_of(first, count, height):
        tiles = [wide_sum[(first + 2 * k) * LANES : (first + 2 * k + 1) * LANES] for k in range(count)]
        return jnp.concatenate(tiles, axis=0)[:height]

    def both(side):
        experts = [
            rows_of(2 * e * expert_tiles + side, expert_tiles, hidden) for e in range(local_experts)
        ]
        return jnp.stack(experts).transpose(0, 2, 1)

    grad_egate, grad_eup = both(0), both(1)
    padded = expert_tiles * LANES
    grad_edown = jnp.stack(
        [down_sum[e * padded : e * padded + hidden] for e in range(local_experts)]
    )
    start = local_experts * padded
    first_shared = 2 * local_experts * expert_tiles
    grad_router = wide_sum[wide - LANES : wide - LANES + experts_all]
    grad_router = grad_router + wide_sum[wide - LANES + experts_all : wide - LANES + 2 * experts_all]
    output = output + (swap(line_sums(mine, near), "exp", base) if base else line_sums(mine, near))
    output = output.astype(BF16)
    own_scale = lax.rsqrt(jnp.mean(own_tokens * own_tokens, axis=-1, keepdims=True) + epsilon)
    grad_gain_one, d_input = norm_back(d_normed_one, own_tokens, own_scale, first_norm_scale)
    d_input = d_residual + d_input

    def uncut(grad):
        return grad.astype(BF16).reshape(grad.shape[0], exp_count, -1).transpose(1, 0, 2)

    narrow = jnp.concatenate(
        [grad_router.T, grad_gain_one[:, None], grad_gain_two[:, None]], axis=1
    )
    grad_proj = jnp.concatenate([grad_qkv, pad_to(narrow, 1, LANES)], axis=1).astype(BF16)
    grad_out_w = grad_out_w.astype(BF16)
    shared_rows = my_gate.shape[0]
    back_gate = uncut(rows_of(first_shared, shared_tiles, shared_rows))
    back_up = uncut(rows_of(first_shared + 1, shared_tiles, shared_rows))
    back_down = uncut(down_sum[start : start + shared_rows])
    if in_group:
        grad_proj, grad_out_w, back_gate, back_up, back_down = scatter_grads(
            grad_proj, grad_out_w, back_gate, back_up, back_down
        )
        narrow = grad_proj[:, qkv_width:]
    else:
        grad_proj = lax.psum_scatter(grad_proj, "exp", scatter_dimension=0, tiled=True).astype(F32)
        narrow = lax.psum(grad_proj[:, qkv_width:], "tp")
        grad_out_w = lax.psum_scatter(
            grad_out_w, "exp", scatter_dimension=1, tiled=True
        ).astype(F32)
        back_gate, back_up, back_down = (
            lax.all_to_all(x, "exp", split_axis=0, concat_axis=0, tiled=True)
            for x in (back_gate, back_up, back_down)
        )

    def joined(pieces):
        return pieces[:, :shared_hidden].reshape(-1, pieces.shape[2]).astype(F32)

    grad_sgate, grad_sup, grad_sdown = joined(back_gate).T, joined(back_up).T, joined(back_down)
    cuts = (qkv_widths[0], qkv_widths[0] + qkv_widths[1])
    return (
        output,
        d_input,
        narrow[:, experts_all],
        grad_proj[:, : cuts[0]],
        grad_proj[:, cuts[0] : cuts[1]],
        grad_proj[:, cuts[1] : qkv_width],
        grad_out_w,
        narrow[:, experts_all + 1],
        narrow[:, :experts_all],
        grad_sgate,
        grad_sup,
        grad_sdown,
        grad_egate,
        grad_eup,
        grad_edown,
    )


def solution(mesh):
    placed = (
        P(("exp", "tp"), None),
        P(("exp", "tp"), None),
        P("exp"),
        P("exp", None),
        P("exp"),
        P("exp", "tp"),
        P("exp", "tp"),
        P("exp", "tp"),
        P("tp", "exp"),
        P("exp"),
        P("exp", None),
        P("exp", "tp"),
        P("exp", "tp"),
        P("tp", "exp"),
        P("exp", None, "tp"),
        P("exp", None, "tp"),
        P("exp", "tp", None),
    )
    return jax.shard_map(
        shards,
        mesh=mesh,
        in_specs=placed,
        out_specs=(
            P(("exp", "tp"), None),
            P(("exp", "tp"), None),
            P("exp"),
            P("exp", "tp"),
            P("exp", "tp"),
            P("exp", "tp"),
            P("tp", "exp"),
            P("exp"),
            P("exp", None),
            P("exp", "tp"),
            P("exp", "tp"),
            P("tp", "exp"),
            P("exp", None, "tp"),
            P("exp", None, "tp"),
            P("exp", "tp", None),
        ),
        check_vma=False,
    )
```

```python
import functools

import jax
import jax.numpy as jnp
from jax import lax
from jax.experimental import pallas as pl
from jax.experimental.pallas import tpu as pltpu
from jax.sharding import PartitionSpec as P

D = 2048
HEAD_DIM = 128
TOP = 6


epsilon = 1e-06
rope_base = 600000.0
F32 = jnp.float32
BF16 = jnp.bfloat16


def rotary_tables(length, head_width):
    half_width = head_width // 2
    frequency = rope_base ** (-(jnp.arange(half_width, dtype=jnp.float32) * 2.0 / head_width))
    angles = jnp.arange(length, dtype=jnp.float32)[:, None] * frequency[None, :]
    return (jnp.cos(angles), jnp.sin(angles))


def rotate(values, cosine, sine):
    half_width = values.shape[-1] // 2
    first_half = values[..., :half_width]
    second_half = values[..., half_width:]
    cos_rows = cosine[:, None, :]
    sin_rows = sine[:, None, :]
    return jnp.concatenate(
        [
            first_half * cos_rows - second_half * sin_rows,
            second_half * cos_rows + first_half * sin_rows,
        ],
        axis=-1,
    )


def rotate_back(gradient, cosine, sine):
    return rotate(gradient, cosine, -sine)


def norm_back(grad_normed, input_tokens, scale_rows, gain):
    grad_gain = jnp.sum(grad_normed * input_tokens * scale_rows, axis=0)
    scaled_grad = grad_normed * gain
    grad_inputs = (
        scale_rows * scaled_grad
        - input_tokens
        * scale_rows
        * scale_rows
        * scale_rows
        * jnp.mean(scaled_grad * input_tokens, axis=-1, keepdims=True)
    )
    return (grad_gain, grad_inputs)


def dot(left, right, dims):
    return lax.dot_general(left, right, (dims, ((), ())), preferred_element_type=F32)


NN = ((1,), (0,))
NT = ((1,), (1,))
TN = ((0,), (0,))


def swap(value, axis, bit):
    size = lax.axis_size(axis)
    return lax.ppermute(value, axis, [(i, i ^ bit) for i in range(size)])


ORDER = (0, 1, 7, 6, 3, 2, 5, 4)
GROUP = len(ORDER)
LANES = 128
ROW_CHUNK = 64
SUM_CHUNK = 16


def expert_kernel(sizes, *refs):
    parts, experts_all, local_experts, expert_tiles, shared_tiles = sizes
    refs = list(refs)

    def take(count):
        taken = refs[:count]
        del refs[:count]
        return taken

    rows_ref, grads_ref, grads_x, grads_y, mask_hbm, gate_hbm, up_hbm, down_hbm = take(8)
    shared_gate_hbm, shared_up_hbm, shared_down_hbm, router_hbm = take(4)
    all_rows, all_grads, act_hbm, gate_grad_hbm, up_grad_hbm = take(5)
    out_even, out_odd, d_act_hbm, back_ref = take(4)
    wide_v, down_v, rows_v, grads_v, mask_v, d_act_v, act_v, wide_grad_v = take(8)
    probs_v, gates_v, total_v, out_v, back_v, own_v, core_v, relay_v, cross_v, line_in, line_out = take(11)
    send, recv, local, weight_sem, mask_sem, d_act_sem, act_sem, out_sem = take(8)
    quarter = rows_ref.shape[0]
    seq_len = parts * quarter
    half_rows = seq_len // 2
    inner = down_v.shape[0]
    wide = wide_v.shape[0]
    padded = expert_tiles * LANES
    shared_padded = shared_tiles * LANES
    first_part = 2 * padded
    shared_place = 2 * local_experts * padded
    router_place = shared_place + shared_padded
    exp_index = lax.axis_index("exp")
    tp_index = lax.axis_index("tp")
    slot = {r: s for s, r in enumerate(ORDER)}

    def part(q):
        return pl.ds(q * quarter, quarter)

    def chip(r):
        return {"exp": exp_index ^ r}

    def line(k):
        return {"tp": tp_index ^ k}

    copies = {}
    for k in range(1, parts):
        copies["z", k] = (rows_ref, all_rows.at[slot[0], part(k)], line(k))
        copies["t", k] = (line_out.at[k - 1], line_in.at[k - 1], line(k))
    for q in range(parts):
        own = rows_ref if q == 0 else all_rows.at[slot[0], part(q)]
        copies["x", q] = (own, all_rows.at[slot[2], part(q)], chip(2))
        copies["y", q] = (own, all_rows.at[slot[4], part(q)], chip(4))
        via = 2 if 2 * q < parts else 4
        copies["d", q] = (all_rows.at[slot[via], part(q)], all_rows.at[slot[6], part(q)], chip(6 - via))
        for r in (0, 2, 4, 6):
            here = own if r == 0 else all_rows.at[slot[r], part(q)]
            copies["c", r, q] = (here, all_rows.at[slot[r + 1], part(q)], chip(1))
        for side, r in enumerate((2, 4)):
            copies["s", r, q] = (back_v.at[slot[r] % 2, part(q)], cross_v.at[side, part(q)], chip(r))
    for r in (0, 2, 4, 6):
        copies["b", r] = (back_v.at[slot[r + 1] % 2], core_v.at[r // 2], chip(1))
    for side in range(2):
        copies["r", side] = (
            back_v.at[slot[6] % 2, pl.ds(side * half_rows, half_rows)],
            relay_v.at[side],
            chip(4 - 2 * side),
        )
    kept_grads = {0: grads_ref, 2: grads_x, 4: grads_y}
    for h in range(2):
        part_h = pl.ds(h * half_rows, half_rows)
        via = 4 * h + 2 * (1 - h)
        copies["gd", h] = (kept_grads[via].at[part_h], all_grads.at[slot[6], part_h], chip(6 - via))
        copies["gc", 6, h] = (all_grads.at[slot[6], part_h], all_grads.at[slot[7], part_h], chip(1))
    for r, ref in kept_grads.items():
        copies["gc", r, 0] = (ref, all_grads.at[slot[r + 1]], chip(1))
    number = {name: k for k, name in enumerate(copies)}

    def remote(*name):
        source, target, device = copies[name]
        return pltpu.make_async_remote_copy(
            source,
            target,
            send.at[number[name]],
            recv.at[number[name]],
            device_id=device,
            device_id_type=pl.DeviceIdType.MESH,
        )

    barrier = pltpu.get_barrier_semaphore()
    peers = [line(k) for k in range(1, parts)] + [chip(r) for r in (1, 2, 4)]
    for peer in peers:
        pl.semaphore_signal(barrier, inc=1, device_id=peer, device_id_type=pl.DeviceIdType.MESH)
    pl.semaphore_wait(barrier, len(peers))

    own_copy = pltpu.make_async_copy(rows_ref, all_rows.at[slot[0], part(0)], local.at[0])
    own_copy.start()

    def spread(q):
        remote("x" if 2 * q < parts else "y", q).start()
        remote("c", 0, q).start()

    def spread_rest(q):
        remote("y" if 2 * q < parts else "x", q).start()

    for k in range(1, parts):
        remote("z", k).start()
    spread(0)
    hidden = down_hbm.shape[1]
    shared_rows = shared_down_hbm.shape[0]
    weights = [(shared_down_hbm, down_v.at[pl.ds(local_experts * padded, shared_rows)])]
    weights.append((router_hbm, wide_v.at[pl.ds(router_place, LANES)]))
    blanks = [(down_v, local_experts * padded + shared_rows, inner)]

    def load_part(source, count, place):
        weights.append((source, wide_v.at[pl.ds(place, count)]))
        blanks.append((wide_v, place + count, place + -(-count // LANES) * LANES))

    for e in range(local_experts):
        weights.append((down_hbm.at[e], down_v.at[pl.ds(e * padded, hidden)]))
        blanks.append((down_v, e * padded + hidden, (e + 1) * padded))
        load_part(gate_hbm.at[e], hidden, 2 * e * padded)
        load_part(up_hbm.at[e], hidden, (2 * e + 1) * padded)
    load_part(shared_gate_hbm, shared_rows, shared_place)
    load_part(shared_up_hbm, shared_rows, router_place + LANES)
    weight_copies = [
        pltpu.make_async_copy(source, target, weight_sem.at[k])
        for k, (source, target) in enumerate(weights)
    ]
    grads_copies = [
        pltpu.make_async_copy(ref, all_grads.at[slot[r]], local.at[1 + k])
        for k, (r, ref) in enumerate(kept_grads.items())
    ]

    def load_rows(u):
        return pltpu.make_async_copy(all_rows.at[u], rows_v, local.at[6])

    for r in kept_grads:
        remote("gc", r, 0).start()
    for h in range(2):
        remote("gd", h).start()
    for copy in grads_copies:
        copy.start()
    for copy in weight_copies:
        copy.start()
    for ref, first, last in blanks:
        if last > first:
            ref[first:last] = jnp.zeros((last - first, D), BF16)

    def arrived_x(q):
        remote("x", q).wait_recv()
        if 2 * q < parts:
            remote("d", q).start()
        remote("c", 2, q).start()

    def arrived_y(q):
        remote("y", q).wait_recv()
        if 2 * q >= parts:
            remote("d", q).start()
        remote("c", 4, q).start()

    def arrived_far(q):
        remote("d", q).wait_recv()
        remote("c", 6, q).start()

    half_parts = parts // 2

    def d_act_store(s, into):
        return pltpu.make_async_copy(d_act_v.at[into], d_act_hbm.at[s], d_act_sem.at[into])

    def d_act_load(u, into):
        return pltpu.make_async_copy(d_act_hbm.at[u], d_act_v.at[into], d_act_sem.at[into])

    for copy in weight_copies:
        copy.wait()

    def first_product(k, r):
        if r == 6:
            for h in range(2):
                remote("gd", h).wait_recv()
                remote("gc", 6, h).start()
        elif r == 7:
            for h in range(2):
                remote("gc", 6, h).wait_recv()
        elif r % 2:
            remote("gc", r - 1, 0).wait_recv()
        source = kept_grads.get(r, all_grads.at[slot[r]])
        load = pltpu.make_async_copy(source, grads_v, local.at[5])
        load.start()
        if k >= 2:
            d_act_store(0, k % 2).wait()
        load.wait()
        for first in range(0, inner, 512):
            columns = pl.ds(first, min(512, inner - first))
            d_act_v[k % 2, :, columns] = dot(grads_v[...], down_v[columns, :], NT)
        d_act_store(slot[r], k % 2).start()

    arrivals = {2: 1, 5: 2, 7: 3}
    for k, r in enumerate((0, 1, 2, 3, 4, 5, 6, 7)):
        first_product(k, r)
        q = arrivals.get(k, parts)
        if q < parts:
            remote("z", q).wait_recv()
            spread(q)
            if q >= half_parts:
                arrived_x(q - half_parts)
    own_copy.wait()
    load_rows(0).start()
    for k in range(2):
        d_act_store(0, k).wait()
    d_act_load(0, 0).start()

    def mask_loads(r):
        from_exp = (lax.rem(exp_index, GROUP) ^ r) * seq_len
        return [
            pltpu.make_async_copy(
                mask_hbm.at[pl.ds(pl.multiple_of(from_exp + (tp_index ^ q) * quarter, quarter), quarter)],
                mask_v.at[part(q)],
                mask_sem.at[q],
            )
            for q in range(parts)
        ]

    def act_store(u):
        into = u % 2
        return pltpu.make_async_copy(act_v.at[into], act_hbm.at[u], act_sem.at[into])

    def act_load(u):
        into = u % 2
        return pltpu.make_async_copy(act_hbm.at[u], act_v.at[into], act_sem.at[into])

    def wide_stores(u):
        return [
            pltpu.make_async_copy(
                wide_grad_v.at[:, pl.ds(0, first_part)], gate_grad_hbm.at[u], local.at[4]
            ),
            pltpu.make_async_copy(
                wide_grad_v.at[:, pl.ds(first_part, wide - first_part)], up_grad_hbm.at[u], local.at[7]
            ),
        ]

    def out_store(s):
        kept = out_odd if ORDER[s] % 2 else out_even
        return pltpu.make_async_copy(out_v.at[s % 2], kept.at[ORDER[s] // 2], out_sem.at[s % 2])

    def add_into(target, others):
        def chunk(i, _):
            total = None
            for ref, first in [target] + others:
                rows = pl.ds(pl.multiple_of(first + i * SUM_CHUNK, SUM_CHUNK), SUM_CHUNK)
                value = ref[rows].astype(F32)
                total = value if total is None else total + value
            ref, first = target
            ref[pl.ds(pl.multiple_of(first + i * SUM_CHUNK, SUM_CHUNK), SUM_CHUNK)] = total.astype(BF16)
            return 0

        return chunk

    def sum_rows(count, target, others):
        lax.fori_loop(0, count // SUM_CHUNK, add_into(target, others), 0)

    def unit(u, _):
        into = lax.rem(u, 2)

        for s in range(GROUP):
            @pl.when(u == s)
            def _(s=s):
                for load in mask_loads(ORDER[s]):
                    load.start()

        load_rows(u).wait()
        for load in mask_loads(0):
            load.wait()

        d_act_load(u, into).wait()

        @pl.when(u > 1)
        def _():
            act_store(u - 2).wait()

        @pl.when(u > 0)
        def _():
            for store in wide_stores(u - 1):
                store.wait()

        linear = dot(rows_v[...], wide_v[shared_place:, :], NT)
        logits = linear[:, shared_padded : shared_padded + LANES]
        lane = lax.broadcasted_iota(jnp.int32, logits.shape, 1)
        logits = jnp.where(lane < experts_all, logits, -1e30)
        raised = jnp.exp(logits - jnp.max(logits, axis=1, keepdims=True))
        probs = raised / jnp.sum(raised, axis=1, keepdims=True)
        mask = mask_v[...].astype(F32)
        chosen = probs * mask
        chosen_sum = jnp.sum(chosen, axis=1, keepdims=True)
        probs_v[...] = probs
        gates_v[...] = chosen / chosen_sum

        def tile(linear, at_gate, at_up, place, j, gate):
            one = pl.ds(j * LANES, LANES)
            for first in range(0, seq_len, ROW_CHUNK):
                last = first + ROW_CHUNK
                gate_lin = linear[first:last, at_gate : at_gate + LANES]
                up_lin = linear[first:last, at_up : at_up + LANES]
                sigmoid = 0.5 * jnp.tanh(0.5 * gate_lin) + 0.5
                silu = gate_lin * sigmoid
                act = silu * up_lin
                d_act = d_act_v[into, first:last, one]
                if gate is not None:
                    total_v[first:last] += act * d_act
                    act = act * gate[first:last]
                    d_act = d_act * gate[first:last]
                act_v[into, first:last, one] = act.astype(BF16)
                d_up = d_act * silu
                d_gate = d_act * up_lin * (sigmoid + silu * (1.0 - sigmoid))
                wide_grad_v[first:last, pl.ds(place + at_gate, LANES)] = d_gate.astype(BF16)
                wide_grad_v[first:last, pl.ds(place + at_up, LANES)] = d_up.astype(BF16)

        for k in range(shared_tiles):
            at_up = shared_padded + LANES + k * LANES
            tile(linear, k * LANES, at_up, shared_place, local_experts * expert_tiles + k, None)
        d_gates = jnp.zeros(logits.shape, F32)
        for e in range(local_experts):
            mine = lane == exp_index * local_experts + e
            gate = jnp.sum(jnp.where(mine, gates_v[...], 0.0), axis=1, keepdims=True)
            total_v[...] = jnp.zeros(logits.shape, F32)
            place = 2 * e * padded
            linear = dot(rows_v[...], wide_v[place : place + 2 * padded, :], NT)
            for k in range(expert_tiles):
                tile(linear, k * LANES, padded + k * LANES, place, e * expert_tiles + k, gate)
            d_gates = jnp.where(mine, jnp.sum(total_v[...], axis=1, keepdims=True), d_gates)
        probs, gates, mask = probs_v[...], gates_v[...], mask_v[...].astype(F32)
        chosen_sum = jnp.sum(probs * mask, axis=1, keepdims=True)
        d_gates = d_gates * mask
        d_chosen = (d_gates - jnp.sum(d_gates * gates, axis=1, keepdims=True)) / chosen_sum
        d_probs = d_chosen * mask
        d_logits = probs * (d_probs - jnp.sum(d_probs * probs, axis=1, keepdims=True))
        high = d_logits.astype(BF16)
        low = pltpu.roll(d_logits - high.astype(F32), experts_all, 1)
        wide_grad_v[:, pl.ds(router_place, LANES)] = jnp.where(
            lane < experts_all, high.astype(F32), low
        ).astype(BF16)
        act_store(u).start()
        for store in wide_stores(u):
            store.start()

        @pl.when(u < GROUP - 1)
        def _():
            d_act_load(u + 1, 1 - into).start()

        @pl.when(u == 0)
        def _():
            for q in range(half_parts, parts):
                arrived_y(q)
            for q in range(parts):
                spread_rest(q)

        @pl.when(u == 1)
        def _():
            for q in range(half_parts):
                arrived_far(q)

        @pl.when(u == 3)
        def _():
            for q in range(half_parts, parts):
                arrived_x(q)

        @pl.when(u == 4)
        def _():
            for q in range(half_parts):
                arrived_y(q)

        @pl.when(u == 3)
        def _():
            remote("b", 0).wait_send()

        @pl.when(u == 4)
        def _():
            remote("b", 6).wait_send()

        @pl.when(u == 5)
        def _():
            remote("r", 0).wait_send()
            remote("r", 1).wait_send()

        @pl.when(u == 6)
        def _():
            remote("b", 2).wait_send()

        @pl.when(u == 7)
        def _():
            for q in range(parts):
                remote("s", 2, q).wait_send()

        back = back_v.at[into]

        def back_step(n, _):
            columns = pl.ds(pl.multiple_of(n * 512, 512), 512)
            back[:, columns] = dot(wide_grad_v[...], wide_v[:, columns], NN).astype(BF16)
            return 0

        lax.fori_loop(0, D // 512, back_step, 0)

        @pl.when(u == 0)
        def _():
            own_v[...] = back_v[0]

        @pl.when(u == slot[1])
        def _():
            remote("b", 0).start()

        @pl.when(u == slot[7])
        def _():
            remote("b", 6).start()

        @pl.when(u == slot[6])
        def _():
            remote("b", 6).wait_recv()
            sum_rows(seq_len, (back_v.at[slot[6] % 2], 0), [(core_v.at[3], 0)])
            remote("r", 0).start()
            remote("r", 1).start()

        @pl.when(u == slot[3])
        def _():
            remote("b", 2).start()

        @pl.when(u == slot[2])
        def _():
            remote("b", 2).wait_recv()
            remote("r", 0).wait_recv()
            mine = back_v.at[slot[2] % 2]
            sum_rows(half_rows, (mine, 0), [(core_v.at[1], 0), (relay_v.at[0], 0)])
            sum_rows(half_rows, (mine, half_rows), [(core_v.at[1], half_rows)])
            for q in range(parts):
                remote("s", 2, q).start()

        @pl.when(u == slot[5])
        def _():
            remote("b", 4).start()

        @pl.when(u == slot[4])
        def _():
            remote("b", 4).wait_recv()
            remote("r", 1).wait_recv()
            mine = back_v.at[slot[4] % 2]
            sum_rows(half_rows, (mine, half_rows), [(core_v.at[2], half_rows), (relay_v.at[1], 0)])
            sum_rows(half_rows, (mine, 0), [(core_v.at[2], 0)])
            for q in range(parts - 1, -1, -1):
                remote("s", 4, q).start()

        for k, r in ((0, 0), (1, 6), (3, 2), (5, 4)):
            @pl.when(u == k)
            def _(k=k, r=r):
                if k == 1:
                    for q in range(half_parts, parts):
                        arrived_far(q)
                for q in range(parts):
                    remote("c", r, q).wait_recv()

        @pl.when(u < GROUP - 1)
        def _():
            load_rows(u + 1).start()

        return 0

    lax.fori_loop(0, GROUP, unit, 0)

    remote("b", 0).wait_recv()

    def finish(q):
        remote("s", 2, q).wait_recv()
        remote("s", 4, q).wait_recv()
        first = q * quarter
        sources = [(own_v, first), (core_v.at[0], first), (cross_v.at[0], first), (cross_v.at[1], first)]

        def total_step(i, _):
            total = None
            for ref, start in sources:
                rows = pl.ds(pl.multiple_of(start + i * SUM_CHUNK, SUM_CHUNK), SUM_CHUNK)
                value = ref[rows].astype(F32)
                total = value if total is None else total + value
            rows = pl.ds(pl.multiple_of(i * SUM_CHUNK, SUM_CHUNK), SUM_CHUNK)
            if q == 0:
                back_ref[rows] = total
            else:
                line_out[q - 1, rows] = total.astype(BF16)
            return 0

        lax.fori_loop(0, quarter // SUM_CHUNK, total_step, 0)
        if q:
            remote("t", q).start()

    for u in (GROUP - 2, GROUP - 1):
        act_store(u).wait()
    for store in wide_stores(GROUP - 1):
        store.wait()
    act_load(0).start()

    def out_unit(u, _):
        into = lax.rem(u, 2)

        @pl.when(u < GROUP - 1)
        def _():
            act_load(u + 1).start()

        act_load(u).wait()
        for s in range(2, GROUP):
            @pl.when(u == s)
            def _(s=s):
                out_store(s - 2).wait()

        def out_step(n, _):
            columns = pl.ds(pl.multiple_of(n * 512, 512), 512)
            out_v[into, :, columns] = dot(act_v[into], down_v[:, columns], NN).astype(BF16)
            return 0

        lax.fori_loop(0, D // 512, out_step, 0)
        for s in range(GROUP):
            @pl.when(u == s)
            def _(s=s):
                out_store(s).start()

        for q in range(1, parts):
            @pl.when(u == GROUP - 1 - 2 * (q - 1))
            def _(q=q):
                finish(q)

        return 0

    lax.fori_loop(0, GROUP, out_unit, 0)
    finish(0)
    for s in (GROUP - 2, GROUP - 1):
        out_store(s).wait()
    for k in range(parts - 1, 0, -1):
        remote("t", k).wait_recv()

    def last_step(i, _):
        rows = pl.ds(pl.multiple_of(i * ROW_CHUNK, ROW_CHUNK), ROW_CHUNK)
        total = back_ref[rows]
        for k in range(1, parts):
            total = total + line_in[k - 1, rows].astype(F32)
        back_ref[rows] = total
        return 0

    lax.fori_loop(0, quarter // ROW_CHUNK, last_step, 0)

    for copy in grads_copies:
        copy.wait()
    waited = [("b", 0), ("b", 6), ("r", 0), ("r", 1), ("b", 2)] + [("s", 2, q) for q in range(parts)]
    for name in copies:
        if name not in waited:
            remote(*name).wait_send()


def expert_layer(rows, grads, mask, weights, sizes):
    parts, _, local_experts, expert_tiles, shared_tiles = sizes
    quarter = rows.shape[0]
    seq_len = parts * quarter
    inner = (local_experts * expert_tiles + shared_tiles) * LANES
    wide = 2 * inner + LANES
    first_part = 2 * expert_tiles * LANES
    loads = 4 + 3 * local_experts
    copies = 2 * (parts - 1) + 9 * parts + 6 + 7
    hbm = pl.BlockSpec(memory_space=pl.ANY)
    every = jax.ShapeDtypeStruct((GROUP, seq_len, D), BF16)
    some = jax.ShapeDtypeStruct((GROUP // 2, seq_len, D), BF16)
    flops = 2 * GROUP * seq_len * D * (2 * wide + 2 * inner)
    return pl.pallas_call(
        functools.partial(expert_kernel, sizes),
        out_shape=(
            every,
            every,
            jax.ShapeDtypeStruct((GROUP, seq_len, inner), BF16),
            jax.ShapeDtypeStruct((GROUP, seq_len, first_part), BF16),
            jax.ShapeDtypeStruct((GROUP, seq_len, wide - first_part), BF16),
            some,
            some,
            jax.ShapeDtypeStruct((GROUP, seq_len, inner), F32),
            jax.ShapeDtypeStruct((quarter, D), F32),
        ),
        in_specs=[hbm] * (5 + len(weights)),
        out_specs=(hbm,) * 8 + (pl.BlockSpec(memory_space=pltpu.VMEM),),
        scratch_shapes=[
            pltpu.VMEM((wide, D), BF16),
            pltpu.VMEM((inner, D), BF16),
            pltpu.VMEM((seq_len, D), BF16),
            pltpu.VMEM((seq_len, D), BF16),
            pltpu.VMEM((seq_len, LANES), BF16),
            pltpu.VMEM((2, seq_len, inner), F32),
            pltpu.VMEM((2, seq_len, inner), BF16),
            pltpu.VMEM((seq_len, wide), BF16),
            pltpu.VMEM((seq_len, LANES), F32),
            pltpu.VMEM((seq_len, LANES), F32),
            pltpu.VMEM((seq_len, LANES), F32),
            pltpu.VMEM((2, seq_len, D), BF16),
            pltpu.VMEM((2, seq_len, D), BF16),
            pltpu.VMEM((seq_len, D), BF16),
            pltpu.VMEM((GROUP // 2, seq_len, D), BF16),
            pltpu.VMEM((2, seq_len // 2, D), BF16),
            pltpu.VMEM((2, seq_len, D), BF16),
            pltpu.VMEM((parts - 1, quarter, D), BF16),
            pltpu.VMEM((parts - 1, quarter, D), BF16),
            pltpu.SemaphoreType.DMA((copies,)),
            pltpu.SemaphoreType.DMA((copies,)),
            pltpu.SemaphoreType.DMA((8,)),
            pltpu.SemaphoreType.DMA((loads,)),
            pltpu.SemaphoreType.DMA((parts,)),
            pltpu.SemaphoreType.DMA((2,)),
            pltpu.SemaphoreType.DMA((2,)),
            pltpu.SemaphoreType.DMA((2,)),
        ],
        compiler_params=pltpu.CompilerParams(
            collective_id=1, has_side_effects=True, vmem_limit_bytes=60 * 1024 * 1024
        ),
        cost_estimate=pl.CostEstimate(flops=flops, bytes_accessed=120_000_000, transcendentals=0),
        name="experts",
    )(rows, *grads, mask, *weights)


def line_rows(own_rows):
    parts = lax.axis_size("tp")
    return [own_rows] + [swap(own_rows, "tp", k) for k in range(1, parts)]


def add_cores(even, odd_swapped):
    return [(e.astype(F32) + o.astype(F32)).astype(BF16) for e, o in zip(even, odd_swapped)]


def far_halves(mine):
    half = mine[3].shape[0] // 2
    return swap(mine[3][:half], "exp", 4), swap(mine[3][half:], "exp", 2)


def near_sums(mine, far):
    half = mine[3].shape[0] // 2
    first = jnp.concatenate([mine[1][:half] + far[0], mine[1][half:]], axis=0)
    second = jnp.concatenate([mine[2][:half], mine[2][half:] + far[1]], axis=0)
    return swap(first, "exp", 2), swap(second, "exp", 4)


def chip_sums(mine, near):
    total = mine[0].astype(F32) + near[0].astype(F32) + near[1].astype(F32)
    total = total.reshape(lax.axis_size("tp"), -1, total.shape[1])
    return total[0], total.astype(BF16)


def line_sums(mine, near):
    result, low = chip_sums(mine, near)
    for k in range(1, low.shape[0]):
        result = result + swap(low[k], "tp", k).astype(F32)
    return result


def neighbours(parts):
    exp_index, tp_index = lax.axis_index("exp"), lax.axis_index("tp")
    line = [{"tp": tp_index ^ k} for k in range(1, parts)]
    return line, [{"exp": exp_index ^ r} for r in range(1, GROUP)]


def greet(peers):
    barrier = pltpu.get_barrier_semaphore()
    for peer in peers:
        pl.semaphore_signal(barrier, inc=1, device_id=peer, device_id_type=pl.DeviceIdType.MESH)
    pl.semaphore_wait(barrier, len(peers))


def remote_maker(copies, send, recv):
    number = {name: k for k, name in enumerate(copies)}

    def remote(*name):
        source, target, device = copies[name]
        return pltpu.make_async_remote_copy(
            source,
            target,
            send.at[number[name]],
            recv.at[number[name]],
            device_id=device,
            device_id_type=pl.DeviceIdType.MESH,
        )

    return remote


def gather_kernel(parts, *refs):
    tokens_ref, proj_ref, narrow_ref, out_ref, mask_ref, gate_ref, up_ref, down_ref = refs[:8]
    tokens_all, proj_all, narrow_all, out_all, mask_all, gate_all, up_all, down_all = refs[8:16]
    send, recv, local = refs[16:]
    exp_index, tp_index = lax.axis_index("exp"), lax.axis_index("tp")
    line, near = neighbours(parts)
    quarter, depth, seq_len = tokens_ref.shape[0], proj_ref.shape[0], mask_ref.shape[0]
    width = down_ref.shape[2]

    def block(whole, size, r, axis=0):
        place = pl.ds(pl.multiple_of((exp_index ^ r) * size, size), size)
        return whole.at[place] if axis == 0 else whole.at[:, place]

    def arrays(r):
        return {
            "p": block(proj_all, depth, r),
            "n": block(narrow_all, narrow_ref.shape[1], r, 1),
            "o": block(out_all, out_ref.shape[1], r, 1),
            "m": block(mask_all, seq_len, r),
        }

    own = {"p": proj_ref, "n": narrow_ref, "o": out_ref, "m": mask_ref}
    my_rows = pl.ds(pl.multiple_of(tp_index * quarter, quarter), quarter)
    copies = {}
    for k in range(1, parts):
        copies["z", k] = (tokens_ref, tokens_all.at[my_rows], line[k - 1])
    for key, ref in own.items():
        mine = arrays(0)[key]
        copies["g", 2, key] = (ref, mine, near[1])
        copies["g", 4, key] = (ref, mine, near[3])
        via = 2 if key in "pn" else 4
        passed = arrays(via)[key]
        copies["g", 6, key] = (passed, passed, near[5 - via])
        copies["c", 0, key] = (ref, mine, near[0])
        for r in (2, 4, 6):
            copies["c", r, key] = (arrays(r)[key], arrays(r)[key], near[0])
    for r in range(1, GROUP):
        to = exp_index ^ r
        copies["a", r, 0] = (gate_ref.at[to], block(gate_all, width, 0, 1), near[r - 1])
        copies["a", r, 1] = (up_ref.at[to], block(up_all, width, 0, 1), near[r - 1])
        copies["a", r, 2] = (down_ref.at[to], block(down_all, width, 0, 1), near[r - 1])
    remote = remote_maker(copies, send, recv)

    greet(line + near)
    for k in range(1, parts):
        remote("z", k).start()
    for key in own:
        for r in (2, 4):
            remote("g", r, key).start()
        remote("c", 0, key).start()
    kept = [
        (tokens_ref, tokens_all.at[my_rows]),
        (proj_ref, arrays(0)["p"]),
        (narrow_ref, arrays(0)["n"]),
        (out_ref, arrays(0)["o"]),
        (mask_ref, arrays(0)["m"]),
        (gate_ref.at[exp_index], block(gate_all, width, 0, 1)),
        (up_ref.at[exp_index], block(up_all, width, 0, 1)),
        (down_ref.at[exp_index], block(down_all, width, 0, 1)),
    ]
    kept = [pltpu.make_async_copy(s, t, local.at[k]) for k, (s, t) in enumerate(kept)]
    for copy in kept:
        copy.start()
    for key in own:
        for r in (2, 4):
            remote("g", r, key).wait_recv()
            if r == (2 if key in "pn" else 4):
                remote("g", 6, key).start()
            remote("c", r, key).start()
    for r in range(1, GROUP):
        for k in range(3):
            remote("a", r, k).start()
    for key in own:
        remote("g", 6, key).wait_recv()
        remote("c", 6, key).start()
    for copy in kept:
        copy.wait()
    for name in copies:
        if name[0] != "g":
            remote(*name).wait_recv()
    for name in copies:
        remote(*name).wait_send()


def gather_inputs(tokens, proj, narrow, out, mask, gate, up, down):
    parts = lax.axis_size("tp")
    hbm = pl.BlockSpec(memory_space=pl.ANY)
    depth, seq_len = proj.shape[0], mask.shape[0]
    shapes = [
        (parts * tokens.shape[0], D),
        (GROUP * depth, proj.shape[1]),
        (narrow.shape[0], GROUP * narrow.shape[1]),
        (out.shape[0], GROUP * out.shape[1]),
        (GROUP * seq_len, LANES),
        *((w.shape[1], GROUP * w.shape[2]) for w in (gate, up, down)),
    ]
    copies = (parts - 1) + 4 * 7 + 3 * (GROUP - 1)
    return pl.pallas_call(
        functools.partial(gather_kernel, parts),
        out_shape=tuple(jax.ShapeDtypeStruct(s, BF16) for s in shapes),
        in_specs=[hbm] * 8,
        out_specs=(hbm,) * 8,
        scratch_shapes=[
            pltpu.SemaphoreType.DMA((copies,)),
            pltpu.SemaphoreType.DMA((copies,)),
            pltpu.SemaphoreType.DMA((8,)),
        ],
        compiler_params=pltpu.CompilerParams(collective_id=2, has_side_effects=True),
        name="gather_inputs",
    )(tokens, proj, narrow, out, mask, gate, up, down)


def scatter_kernel(parts, *refs):
    proj_ref, out_ref, mine_ref, line_ref, gate_ref, up_ref, down_ref = refs[:7]
    proj_sum, out_sum, output_ref, gate_back, up_back, down_back = refs[7:13]
    proj_core, out_core, proj_add, out_add, proj_relay, out_relay = refs[13:19]
    proj_cross, out_cross, narrow, narrow_in, line_in, send, recv, local = refs[19:]
    exp_index = lax.axis_index("exp")
    line, near = neighbours(parts)
    depth, width = proj_sum.shape[0], out_sum.shape[1]

    def proj_block(r):
        return proj_ref.at[pl.ds(pl.multiple_of((exp_index ^ r) * depth, depth), depth)]

    def out_block(r):
        return out_ref.at[:, pl.ds(pl.multiple_of((exp_index ^ r) * width, width), width)]

    copies = {}
    for r in (6, 2, 4, 0):
        copies["c", r, 0] = (proj_block(r + 1), proj_core.at[r // 2], near[0])
        copies["c", r, 1] = (out_block(r + 1), out_core.at[r // 2], near[0])
    copies["d", 0] = (proj_add.at[2], proj_relay, near[3])
    copies["d", 1] = (out_add.at[2], out_relay, near[1])
    for side, r in enumerate((2, 4)):
        copies["s", r, 0] = (proj_add.at[side], proj_cross.at[side], near[r - 1])
        copies["s", r, 1] = (out_add.at[side], out_cross.at[side], near[r - 1])
    for k in range(1, parts):
        copies["z", k] = (narrow, narrow_in.at[k - 1], line[k - 1])
        copies["t", k] = (line_ref.at[k], line_in.at[k - 1], line[k - 1])
    for r in range(1, GROUP):
        to = exp_index ^ r
        copies["a", r, 0] = (gate_ref.at[to], gate_back.at[exp_index], near[r - 1])
        copies["a", r, 1] = (up_ref.at[to], up_back.at[exp_index], near[r - 1])
        copies["a", r, 2] = (down_ref.at[to], down_back.at[exp_index], near[r - 1])
    remote = remote_maker(copies, send, recv)

    def total(target, sources):
        count = target.shape[0]

        def chunk(i, _):
            rows = pl.ds(pl.multiple_of(i * 32, 32), 32)
            value = sum(ref[rows].astype(F32) for ref in sources[1:])
            target[rows] = (sources[0][rows].astype(F32) + value).astype(target.dtype)
            return 0

        lax.fori_loop(0, count // 32, chunk, 0)

    greet(line + near)
    for k in range(1, parts):
        remote("t", k).start()
    for r in (6, 2, 4, 0):
        for k in range(2):
            remote("c", r, k).start()
    for k in range(2):
        remote("c", 6, k).wait_recv()
    total(proj_add.at[2], [proj_block(6), proj_core.at[3]])
    remote("d", 0).start()
    total(out_add.at[2], [out_block(6), out_core.at[3]])
    remote("d", 1).start()
    for r in (2, 4):
        for k in range(2):
            remote("c", r, k).wait_recv()
    total(out_add.at[0], [out_block(2), out_core.at[1]])
    remote("s", 2, 1).start()
    total(proj_add.at[1], [proj_block(4), proj_core.at[2]])
    remote("s", 4, 0).start()
    remote("d", 0).wait_recv()
    total(proj_add.at[0], [proj_block(2), proj_core.at[1], proj_relay])
    remote("s", 2, 0).start()
    remote("d", 1).wait_recv()
    total(out_add.at[1], [out_block(4), out_core.at[2], out_relay])
    remote("s", 4, 1).start()
    for r in range(1, GROUP):
        for k in range(3):
            remote("a", r, k).start()
    kept = [
        pltpu.make_async_copy(source.at[exp_index], target.at[exp_index], local.at[k])
        for k, (source, target) in enumerate(
            ((gate_ref, gate_back), (up_ref, up_back), (down_ref, down_back))
        )
    ]
    for copy in kept:
        copy.start()
    for k in range(2):
        remote("c", 0, k).wait_recv()
        for r in (2, 4):
            remote("s", r, k).wait_recv()
        if k == 0:
            total(proj_sum, [proj_block(0), proj_core.at[0], proj_cross.at[0], proj_cross.at[1]])
            narrow[...] = proj_sum[:, proj_sum.shape[1] - LANES :]
            for j in range(1, parts):
                remote("z", j).start()
        else:
            total(out_sum, [out_block(0), out_core.at[0], out_cross.at[0], out_cross.at[1]])
    for j in range(1, parts):
        remote("z", j).wait_recv()
    value = narrow[...]
    for j in range(1, parts):
        value = value + narrow_in[j - 1]
    proj_sum[:, proj_sum.shape[1] - LANES :] = value
    for j in range(1, parts):
        remote("t", j).wait_recv()
    total(output_ref, [mine_ref] + [line_in.at[j - 1] for j in range(1, parts)])
    for copy in kept:
        copy.wait()
    for r in range(1, GROUP):
        for k in range(3):
            remote("a", r, k).wait_recv()
    for name in copies:
        remote(*name).wait_send()


def scatter_grads(proj, out, mine, line, gate, up, down):
    parts = lax.axis_size("tp")
    hbm, vmem = pl.BlockSpec(memory_space=pl.ANY), pl.BlockSpec(memory_space=pltpu.VMEM)
    one = (proj.shape[0] // GROUP, proj.shape[1])
    two = (out.shape[0], out.shape[1] // GROUP)
    narrow = (one[0], LANES)
    copies = 8 + 2 + 4 + 2 * (parts - 1) + 3 * (GROUP - 1)
    return pl.pallas_call(
        functools.partial(scatter_kernel, parts),
        out_shape=(
            jax.ShapeDtypeStruct(one, F32),
            jax.ShapeDtypeStruct(two, F32),
            jax.ShapeDtypeStruct(mine.shape, BF16),
            *(jax.ShapeDtypeStruct(x.shape, x.dtype) for x in (gate, up, down)),
        ),
        in_specs=[vmem] * 3 + [hbm] * 4,
        out_specs=(vmem, vmem, vmem, hbm, hbm, hbm),
        scratch_shapes=[
            pltpu.VMEM((GROUP // 2, *one), BF16),
            pltpu.VMEM((GROUP // 2, *two), BF16),
            pltpu.VMEM((3, *one), BF16),
            pltpu.VMEM((3, *two), BF16),
            pltpu.VMEM(one, BF16),
            pltpu.VMEM(two, BF16),
            pltpu.VMEM((2, *one), BF16),
            pltpu.VMEM((2, *two), BF16),
            pltpu.VMEM(narrow, F32),
            pltpu.VMEM((parts - 1, *narrow), F32),
            pltpu.VMEM((parts - 1, *mine.shape), BF16),
            pltpu.SemaphoreType.DMA((copies,)),
            pltpu.SemaphoreType.DMA((copies,)),
            pltpu.SemaphoreType.DMA((3,)),
        ],
        compiler_params=pltpu.CompilerParams(
            collective_id=3, has_side_effects=True, vmem_limit_bytes=40 * 1024 * 1024
        ),
        name="scatter_grads",
    )(proj, out, mine, line, gate, up, down)


def pad_to(value, axis, multiple):
    widths = [(0, 0)] * value.ndim
    widths[axis] = (0, -value.shape[axis] % multiple)
    return jnp.pad(value, widths)


def shards(
    tokens,
    cotangent,
    segment_ids,
    routes,
    norm1_gain,
    attn_q,
    attn_k,
    attn_v,
    attn_o,
    norm2_gain,
    router,
    shared_gate,
    shared_up,
    shared_down,
    expert_gate,
    expert_up,
    expert_down,
):
    exp_count = lax.axis_size("exp")
    tp_count = lax.axis_size("tp")
    exp_index = lax.axis_index("exp")
    tp_index = lax.axis_index("tp")
    quarter = tokens.shape[0]
    seq_len = quarter * tp_count

    experts_all = router.shape[1]
    local_experts, _, hidden = expert_gate.shape
    shared_hidden = shared_gate.shape[1] // exp_count
    in_group = exp_count == GROUP
    qkv_widths = (attn_q.shape[1], attn_k.shape[1], attn_v.shape[1])
    gains = jnp.stack([norm1_gain, norm2_gain], axis=0)
    proj = jnp.concatenate([attn_q, attn_k, attn_v], axis=1)
    qkv_width = sum(qkv_widths)
    narrow_weight = pad_to(jnp.concatenate([router.T, gains], axis=0), 0, 16)
    member_lanes = jnp.any(
        routes[:, :, None] == jnp.arange(LANES, dtype=jnp.int32), axis=1
    ).astype(BF16)

    def cut(weight):
        return pad_to(weight.reshape(exp_count, shared_hidden, -1), 1, 16)

    cut_gate, cut_up, cut_down = cut(shared_gate.T), cut(shared_up.T), cut(shared_down)
    if in_group:
        (
            whole,
            qkv_weight,
            narrow_weight,
            output_weight,
            all_masks,
            my_gate,
            my_up,
            my_down,
        ) = gather_inputs(
            tokens, proj, narrow_weight, attn_o, member_lanes, cut_gate, cut_up, cut_down
        )
    else:
        whole = lax.all_gather(tokens, "tp", axis=0, tiled=True)
        qkv_weight = lax.all_gather(proj, "exp", axis=0, tiled=True)
        narrow_weight = lax.all_gather(narrow_weight, "exp", axis=1, tiled=True)
        output_weight = lax.all_gather(attn_o, "exp", axis=1, tiled=True)
        all_masks = lax.all_gather(member_lanes, "exp", axis=0, tiled=True)
        my_gate, my_up, my_down = (
            lax.all_to_all(w, "exp", split_axis=0, concat_axis=2, tiled=True)
            for w in (cut_gate, cut_up, cut_down)
        )
        my_gate, my_up, my_down = my_gate[0], my_up[0], my_down[0]
    first_norm_scale = narrow_weight[experts_all].astype(F32)
    second_norm_scale = narrow_weight[experts_all + 1].astype(F32)
    whole, cotangent = lax.optimization_barrier((whole, cotangent))
    line_grads = line_rows(cotangent)

    own_tokens = tokens.astype(F32)
    whole = whole.astype(F32)
    scale_one = lax.rsqrt(jnp.mean(whole * whole, axis=-1, keepdims=True) + epsilon)
    normed_one = (whole * scale_one * first_norm_scale).astype(BF16)
    heads_dev = qkv_widths[0] // HEAD_DIM
    kv_dev = qkv_widths[1] // HEAD_DIM
    group_size = heads_dev // kv_dev
    score_scale = HEAD_DIM ** (-0.5)
    cosine, sine = rotary_tables(seq_len, HEAD_DIM)
    qkv_lin = dot(normed_one, qkv_weight, NN).reshape(seq_len, -1, HEAD_DIM)
    turned = rotate(qkv_lin[:, : heads_dev + kv_dev], cosine, sine).astype(BF16)
    queries = turned[:, :heads_dev].reshape(seq_len, kv_dev, group_size, HEAD_DIM)
    keys_rot = turned[:, heads_dev:]
    values = qkv_lin[:, heads_dev + kv_dev :].astype(BF16)
    positions = jnp.arange(seq_len, dtype=jnp.int32)
    allowed = (positions[None, :] <= positions[:, None]) & (
        segment_ids[:, None] == segment_ids[None, :]
    )
    raw_scores = jnp.einsum("qkgd,ckd->kgqc", queries, keys_rot, preferred_element_type=F32)
    scores = jnp.where(allowed, raw_scores * score_scale, -1e30)
    exponent = jnp.exp(scores - jnp.max(scores, axis=-1, keepdims=True))
    probs = exponent / jnp.sum(exponent, axis=-1, keepdims=True)
    probs_low = probs.astype(BF16)
    attended = jnp.einsum("kgqc,ckd->qkgd", probs_low, values, preferred_element_type=F32)
    attended = attended.reshape(seq_len, heads_dev * HEAD_DIM).astype(BF16)
    attended, *line_grads[1:-1] = lax.optimization_barrier((attended, *line_grads[1:-1]))
    own_grads = jnp.concatenate(line_grads, axis=0)
    grads_line = [own_grads, swap(own_grads, "exp", 2), swap(own_grads, "exp", 4)]
    attn_mine = lax.psum_scatter(
        dot(attended, output_weight, NN).astype(BF16), "tp", scatter_dimension=0, tiled=True
    )

    residual = own_tokens + attn_mine.astype(F32)
    scale_two = lax.rsqrt(jnp.mean(residual * residual, axis=-1, keepdims=True) + epsilon)
    normed_two = (residual * scale_two * second_norm_scale).astype(BF16)
    expert_tiles, shared_tiles = -(-hidden // LANES), -(-my_gate.shape[0] // LANES)
    router_rows = narrow_weight[:experts_all]
    router_pad = jnp.zeros((LANES - 2 * experts_all, D), BF16)
    weights = (
        expert_gate.transpose(0, 2, 1),
        expert_up.transpose(0, 2, 1),
        expert_down,
        my_gate,
        my_up,
        my_down,
        jnp.concatenate([router_rows, router_rows, router_pad], axis=0),
    )
    inner = (local_experts * expert_tiles + shared_tiles) * LANES
    sizes = (tp_count, experts_all, local_experts, expert_tiles, shared_tiles)
    all_masks = all_masks.reshape(exp_count // GROUP, -1, LANES)

    output = residual
    d_normed_two, rest_sum, first_sum, down_sum = 0.0, 0.0, 0.0, 0.0
    for base in range(0, exp_count, GROUP):
        rows_b = normed_two
        if base:
            rows_b, own_b = swap(rows_b, "exp", base), swap(own_grads, "exp", base)
            grads_line = [own_b, swap(own_b, "exp", 2), swap(own_b, "exp", 4)]
        masks = lax.dynamic_index_in_dim(
            all_masks, (exp_index // GROUP) ^ (base // GROUP), keepdims=False
        )
        all_rows, all_grads, act, first_grads, rest_grads, out_even, out_odd, _, back = expert_layer(
            rows_b, grads_line, masks, weights, sizes
        )
        swapped = swap(out_odd, "exp", 1)
        d_normed_two = d_normed_two + (swap(back, "exp", base) if base else back)
        count = GROUP * seq_len
        grads_seen, act = all_grads.reshape(count, D), act.reshape(count, -1)
        rows_seen = all_rows.reshape(count, D)
        rest_grads, first_grads = rest_grads.reshape(count, -1), first_grads.reshape(count, -1)
        if base + GROUP < exp_count:
            rest_sum = rest_sum + dot(rest_grads, rows_seen, TN)
            first_sum = first_sum + dot(first_grads, rows_seen, TN)
            down_sum = down_sum + dot(act, grads_seen, TN)
            mine = add_cores(out_even, swapped)
            part_out = line_sums(mine, near_sums(mine, far_halves(mine)))
            output = output + (swap(part_out, "exp", base) if base else part_out)
            own_grads, normed_two, rest_sum, first_sum, down_sum, output = lax.optimization_barrier(
                (own_grads, normed_two, rest_sum, first_sum, down_sum, output)
            )
    down_sum = down_sum + dot(act, grads_seen, TN)
    swapped, down_sum = lax.optimization_barrier((swapped, down_sum))

    grad_gain_two, d_residual = norm_back(d_normed_two, residual, scale_two, second_norm_scale)
    d_residual = cotangent.astype(F32) + d_residual

    d_attn_low = lax.all_gather(d_residual.astype(BF16), "tp", axis=0, tiled=True)
    mine = add_cores(out_even, swapped)
    mine, first_grads = lax.optimization_barrier((mine, first_grads))
    first_sum = first_sum + dot(first_grads, rows_seen, TN)
    d_attn_low, first_sum, *far = lax.optimization_barrier((d_attn_low, first_sum, *far_halves(mine)))
    near = near_sums(mine, far)
    grad_out_w = dot(attended, d_attn_low, TN)
    d_attended = dot(d_attn_low, output_weight, NT).astype(BF16)
    d_attended = d_attended.reshape(seq_len, kv_dev, group_size, HEAD_DIM)
    d_probs_att = jnp.einsum("qkgd,ckd->kgqc", d_attended, values, preferred_element_type=F32)
    row_inner = jnp.sum(d_probs_att * probs, axis=-1, keepdims=True)
    d_raw = (probs * (d_probs_att - row_inner) * score_scale).astype(BF16)
    d_query = jnp.einsum("kgqc,ckd->qkgd", d_raw, keys_rot, preferred_element_type=F32).reshape(
        seq_len, heads_dev, HEAD_DIM
    )
    d_key = jnp.einsum("kgqc,qkgd->ckd", d_raw, queries, preferred_element_type=F32)
    d_value = jnp.einsum("kgqc,qkgd->ckd", probs_low, d_attended, preferred_element_type=F32)
    d_qkv = jnp.concatenate(
        [
            rotate_back(jnp.concatenate([d_query, d_key], axis=1), cosine, sine).astype(BF16),
            d_value.astype(BF16),
        ],
        axis=1,
    ).reshape(seq_len, -1)
    d_normed_one = dot(d_qkv, qkv_weight, NT).astype(BF16)
    d_normed_one, rest_grads, first_sum, down_sum = lax.optimization_barrier(
        (d_normed_one, rest_grads, first_sum, down_sum)
    )
    d_normed_one = lax.psum_scatter(
        d_normed_one, "tp", scatter_dimension=0, tiled=True
    ).astype(F32)
    grad_qkv = dot(normed_one, d_qkv, TN)
    rest_sum = rest_sum + dot(rest_grads, rows_seen, TN)
    d_normed_one, *near = lax.optimization_barrier((d_normed_one, *near))

    padded = expert_tiles * LANES

    spans = [first_sum] + [
        rest_sum[2 * e * padded : 2 * (e + 1) * padded] for e in range(local_experts - 1)
    ]
    grad_egate = jnp.stack([s[:hidden] for s in spans]).transpose(0, 2, 1)
    grad_eup = jnp.stack([s[padded : padded + hidden] for s in spans]).transpose(0, 2, 1)
    grad_edown = jnp.stack(
        [down_sum[e * padded : e * padded + hidden] for e in range(local_experts)]
    )
    shared_sum = rest_sum[2 * (local_experts - 1) * padded :]
    start = local_experts * padded
    shared_rows = my_gate.shape[0]
    place = shared_tiles * LANES
    grad_router = shared_sum[place : place + experts_all]
    grad_router = grad_router + shared_sum[place + experts_all : place + 2 * experts_all]
    if in_group:
        own_sum, line_parts = chip_sums(mine, near)
    else:
        own_sum = line_sums(mine, near)
    output = output + (swap(own_sum, "exp", base) if base else own_sum)
    own_scale = lax.rsqrt(jnp.mean(own_tokens * own_tokens, axis=-1, keepdims=True) + epsilon)
    grad_gain_one, d_input = norm_back(d_normed_one, own_tokens, own_scale, first_norm_scale)
    d_input = d_residual + d_input

    def uncut(grad):
        return grad.astype(BF16).reshape(grad.shape[0], exp_count, -1).transpose(1, 0, 2)

    narrow = jnp.concatenate(
        [grad_router.T, grad_gain_one[:, None], grad_gain_two[:, None]], axis=1
    )
    grad_proj = jnp.concatenate([grad_qkv, pad_to(narrow, 1, LANES)], axis=1).astype(BF16)
    grad_out_w = grad_out_w.astype(BF16)
    back_gate, back_up, back_down = (
        uncut(sums[:shared_rows])
        for sums in (shared_sum, shared_sum[place + LANES :], down_sum[start:])
    )
    if in_group:
        grad_proj, grad_out_w, output, back_gate, back_up, back_down = scatter_grads(
            grad_proj, grad_out_w, output, line_parts, back_gate, back_up, back_down
        )
        narrow = grad_proj[:, qkv_width:]
    else:
        output = output.astype(BF16)
        grad_proj = lax.psum_scatter(grad_proj, "exp", scatter_dimension=0, tiled=True).astype(F32)
        narrow = lax.psum(grad_proj[:, qkv_width:], "tp")
        grad_out_w = lax.psum_scatter(
            grad_out_w, "exp", scatter_dimension=1, tiled=True
        ).astype(F32)
        back_gate, back_up, back_down = (
            lax.all_to_all(x, "exp", split_axis=0, concat_axis=0, tiled=True)
            for x in (back_gate, back_up, back_down)
        )

    def joined(pieces):
        return pieces[:, :shared_hidden].reshape(-1, pieces.shape[2]).astype(F32)

    grad_sgate, grad_sup, grad_sdown = joined(back_gate).T, joined(back_up).T, joined(back_down)
    cuts = (qkv_widths[0], qkv_widths[0] + qkv_widths[1])
    return (
        output,
        d_input,
        narrow[:, experts_all],
        grad_proj[:, : cuts[0]],
        grad_proj[:, cuts[0] : cuts[1]],
        grad_proj[:, cuts[1] : qkv_width],
        grad_out_w,
        narrow[:, experts_all + 1],
        narrow[:, :experts_all],
        grad_sgate,
        grad_sup,
        grad_sdown,
        grad_egate,
        grad_eup,
        grad_edown,
    )


def solution(mesh):
    placed = (
        P(("exp", "tp"), None),
        P(("exp", "tp"), None),
        P("exp"),
        P("exp", None),
        P("exp"),
        P("exp", "tp"),
        P("exp", "tp"),
        P("exp", "tp"),
        P("tp", "exp"),
        P("exp"),
        P("exp", None),
        P("exp", "tp"),
        P("exp", "tp"),
        P("tp", "exp"),
        P("exp", None, "tp"),
        P("exp", None, "tp"),
        P("exp", "tp", None),
    )
    return jax.shard_map(
        shards,
        mesh=mesh,
        in_specs=placed,
        out_specs=(
            P(("exp", "tp"), None),
            P(("exp", "tp"), None),
            P("exp"),
            P("exp", "tp"),
            P("exp", "tp"),
            P("exp", "tp"),
            P("tp", "exp"),
            P("exp"),
            P("exp", None),
            P("exp", "tp"),
            P("exp", "tp"),
            P("tp", "exp"),
            P("exp", None, "tp"),
            P("exp", None, "tp"),
            P("exp", "tp", None),
        ),
        check_vma=False,
    )
```

```python
import functools

import jax
import jax.numpy as jnp
from jax import lax
from jax.experimental import pallas as pl
from jax.experimental.pallas import tpu as pltpu
from jax.sharding import PartitionSpec as P

D = 2048
HEAD_DIM = 128
TOP = 6


epsilon = 1e-06
rope_base = 600000.0
F32 = jnp.float32
BF16 = jnp.bfloat16


def rotary_tables(length, head_width):
    half_width = head_width // 2
    frequency = rope_base ** (-(jnp.arange(half_width, dtype=jnp.float32) * 2.0 / head_width))
    angles = jnp.arange(length, dtype=jnp.float32)[:, None] * frequency[None, :]
    return (jnp.cos(angles), jnp.sin(angles))


def rotate(values, cosine, sine):
    half_width = values.shape[-1] // 2
    first_half = values[..., :half_width]
    second_half = values[..., half_width:]
    cos_rows = cosine[:, None, :]
    sin_rows = sine[:, None, :]
    return jnp.concatenate(
        [
            first_half * cos_rows - second_half * sin_rows,
            second_half * cos_rows + first_half * sin_rows,
        ],
        axis=-1,
    )


def rotate_back(gradient, cosine, sine):
    return rotate(gradient, cosine, -sine)


def norm_back(grad_normed, input_tokens, scale_rows, gain):
    grad_gain = jnp.sum(grad_normed * input_tokens * scale_rows, axis=0)
    scaled_grad = grad_normed * gain
    grad_inputs = (
        scale_rows * scaled_grad
        - input_tokens
        * scale_rows
        * scale_rows
        * scale_rows
        * jnp.mean(scaled_grad * input_tokens, axis=-1, keepdims=True)
    )
    return (grad_gain, grad_inputs)


def dot(left, right, dims):
    return lax.dot_general(left, right, (dims, ((), ())), preferred_element_type=F32)


NN = ((1,), (0,))
NT = ((1,), (1,))
TN = ((0,), (0,))


def swap(value, axis, bit):
    size = lax.axis_size(axis)
    return lax.ppermute(value, axis, [(i, i ^ bit) for i in range(size)])


ORDER = (0, 1, 7, 6, 3, 2, 5, 4)
GROUP = len(ORDER)
LANES = 128
ROW_CHUNK = 64
SUM_CHUNK = 16


def expert_kernel(sizes, *refs):
    parts, experts_all, local_experts, expert_tiles, shared_tiles, summed = sizes
    refs = list(refs)

    def take(count):
        taken = refs[:count]
        del refs[:count]
        return taken

    attn_hbm, tokens_hbm, gain_ref, grads_ref, mask_hbm, gate_hbm, up_hbm, down_hbm = take(8)
    shared_gate_hbm, shared_up_hbm, shared_down_hbm, router_hbm = take(4)
    all_rows, all_grads, act_hbm, gate_grad_hbm, up_grad_hbm = take(5)
    out_even, out_odd, d_act_hbm, back_ref, rows_ref, residual_ref = take(6)
    wide_v, down_v, rows_v, grads_v, mask_v, d_act_v, act_v, wide_grad_v = take(8)
    probs_v, gates_v, total_v, out_v, back_v, own_v, core_v, relay_v, cross_v, line_in, line_out, attn_in, attn_relay = take(13)
    send, recv, local, weight_sem, mask_sem, d_act_sem, act_sem, out_sem = take(8)
    quarter = rows_ref.shape[0]
    seq_len = parts * quarter
    half_rows = seq_len // 2
    inner = down_v.shape[0]
    wide = wide_v.shape[0]
    padded = expert_tiles * LANES
    shared_padded = shared_tiles * LANES
    first_part = 2 * padded
    shared_place = 2 * local_experts * padded
    router_place = shared_place + shared_padded
    exp_index = lax.axis_index("exp")
    tp_index = lax.axis_index("tp")
    slot = {r: s for s, r in enumerate(ORDER)}

    def part(q):
        return pl.ds(q * quarter, quarter)

    def chip(r):
        return {"exp": exp_index ^ r}

    def line(k):
        return {"tp": tp_index ^ k}

    copies = {}
    for k in range(1, parts):
        copies["z", k] = (rows_ref, all_rows.at[slot[0], part(k)], line(k))
        there = pl.ds(pl.multiple_of((tp_index ^ k) * quarter, quarter), quarter)
        if not summed:
            copies["n", k] = (attn_hbm.at[there], attn_in.at[k - 1], line(k))
        copies["t", k] = (line_out.at[k - 1], line_in.at[k - 1], line(k))
    copies["zr",] = (all_rows.at[slot[0], part(2)], all_rows.at[slot[0], part(3)], line(1))
    if not summed:
        copies["nr",] = (attn_hbm.at[there], attn_relay, line(1))
        copies["nm",] = (line_out.at[2], attn_in.at[1], line(2))
    for q in range(parts):
        own = rows_ref if q == 0 else all_rows.at[slot[0], part(q)]
        copies["x", q] = (own, all_rows.at[slot[2], part(q)], chip(2))
        copies["y", q] = (own, all_rows.at[slot[4], part(q)], chip(4))
        via = 2 if 2 * q < parts else 4
        copies["d", q] = (all_rows.at[slot[via], part(q)], all_rows.at[slot[6], part(q)], chip(6 - via))
        for r in (0, 2, 4, 6):
            here = own if r == 0 else all_rows.at[slot[r], part(q)]
            copies["c", r, q] = (here, all_rows.at[slot[r + 1], part(q)], chip(1))
        for side, r in enumerate((2, 4)):
            copies["s", r, q] = (back_v.at[slot[r] % 2, part(q)], cross_v.at[side, part(q)], chip(r))
    for r in (0, 2, 4, 6):
        copies["b", r] = (back_v.at[slot[r + 1] % 2], core_v.at[r // 2], chip(1))
    for side in range(2):
        copies["r", side] = (
            back_v.at[slot[6] % 2, pl.ds(side * half_rows, half_rows)],
            relay_v.at[side],
            chip(4 - 2 * side),
        )
    copies["gc", 0, 0] = (grads_ref, all_grads.at[slot[1]], chip(1))
    for h in range(2):
        part_h = pl.ds(h * half_rows, half_rows)
        via = 4 * h + 2 * (1 - h)
        copies["gx", h] = (grads_ref.at[part_h], all_grads.at[slot[2], part_h], chip(2))
        copies["gy", h] = (grads_ref.at[part_h], all_grads.at[slot[4], part_h], chip(4))
        copies["gd", h] = (all_grads.at[slot[via], part_h], all_grads.at[slot[6], part_h], chip(6 - via))
        for r in (2, 4, 6):
            here = all_grads.at[slot[r], part_h]
            copies["gc", r, h] = (here, all_grads.at[slot[r + 1], part_h], chip(1))
    number = {name: k for k, name in enumerate(copies)}

    def remote(*name):
        source, target, device = copies[name]
        return pltpu.make_async_remote_copy(
            source,
            target,
            send.at[number[name]],
            recv.at[number[name]],
            device_id=device,
            device_id_type=pl.DeviceIdType.MESH,
        )

    barrier = pltpu.get_barrier_semaphore()
    peers = [line(k) for k in range(1, parts)] + [chip(r) for r in (1, 2, 4)]
    for peer in peers:
        pl.semaphore_signal(barrier, inc=1, device_id=peer, device_id_type=pl.DeviceIdType.MESH)
    pl.semaphore_wait(barrier, len(peers))

    middle = inside(tp_index)
    outside = jnp.logical_not(middle)

    def rows_at(k):
        return pl.ds(pl.multiple_of((tp_index ^ k) * quarter, quarter), quarter)

    if summed:
        loads = [pltpu.make_async_copy(attn_hbm, rows_ref, local.at[0])]
    else:
        remote("n", 1).start()

        @pl.when(outside)
        def _():
            remote("nr").start()
            remote("n", 2).start()

        pl.when(middle)(remote("n", 3).start)
        loads = [
            pltpu.make_async_copy(source, line_out.at[k], local.at[k])
            for k, source in enumerate(
                (tokens_hbm, attn_hbm.at[rows_at(0)], attn_hbm.at[rows_at(2)])
            )
        ]
    for load in loads:
        load.start()
    remote("gx", 0).start()
    remote("gy", 1).start()
    remote("gc", 0, 0).start()
    remote("gx", 1).start()
    remote("gy", 0).start()

    def spread(q):
        remote("x" if 2 * q < parts else "y", q).start()
        remote("c", 0, q).start()

    def spread_rest(q):
        remote("y" if 2 * q < parts else "x", q).start()

    hidden = down_hbm.shape[1]
    shared_rows = shared_down_hbm.shape[0]
    weights = [(shared_down_hbm, down_v.at[pl.ds(local_experts * padded, shared_rows)])]
    weights.append((router_hbm, wide_v.at[pl.ds(router_place, LANES)]))
    blanks = [(down_v, local_experts * padded + shared_rows, inner)]

    def load_part(source, count, place):
        weights.append((source, wide_v.at[pl.ds(place, count)]))
        blanks.append((wide_v, place + count, place + -(-count // LANES) * LANES))

    for e in range(local_experts):
        weights.append((down_hbm.at[e], down_v.at[pl.ds(e * padded, hidden)]))
        blanks.append((down_v, e * padded + hidden, (e + 1) * padded))
        load_part(gate_hbm.at[e], hidden, 2 * e * padded)
        load_part(up_hbm.at[e], hidden, (2 * e + 1) * padded)
    load_part(shared_gate_hbm, shared_rows, shared_place)
    load_part(shared_up_hbm, shared_rows, router_place + LANES)
    weight_copies = [
        pltpu.make_async_copy(source, target, weight_sem.at[k])
        for k, (source, target) in enumerate(weights)
    ]
    grads_copy = pltpu.make_async_copy(grads_ref, all_grads.at[slot[0]], local.at[3])

    def load_rows(u):
        return pltpu.make_async_copy(all_rows.at[u], rows_v, local.at[6])

    grads_copy.start()
    for copy in weight_copies:
        copy.start()
    for ref, first, last in blanks:
        if last > first:
            ref[first:last] = jnp.zeros((last - first, D), BF16)

    def add_into(target, others):
        def chunk(i, _):
            total = None
            for ref, first in [target] + others:
                rows = pl.ds(pl.multiple_of(first + i * SUM_CHUNK, SUM_CHUNK), SUM_CHUNK)
                value = ref[rows].astype(F32)
                total = value if total is None else total + value
            ref, first = target
            ref[pl.ds(pl.multiple_of(first + i * SUM_CHUNK, SUM_CHUNK), SUM_CHUNK)] = total.astype(BF16)
            return 0

        return chunk

    def sum_rows(count, target, others):
        lax.fori_loop(0, count // SUM_CHUNK, add_into(target, others), 0)

    def arrived_x(q):
        remote("x", q).wait_recv()
        if 2 * q < parts:
            remote("d", q).start()
        remote("c", 2, q).start()

    def arrived_y(q):
        remote("y", q).wait_recv()
        if 2 * q >= parts:
            remote("d", q).start()
        remote("c", 4, q).start()

    def arrived_far(q):
        remote("d", q).wait_recv()
        remote("c", 6, q).start()

    half_parts = parts // 2

    def d_act_store(s, into):
        return pltpu.make_async_copy(d_act_v.at[into], d_act_hbm.at[s], d_act_sem.at[into])

    def d_act_load(u, into):
        return pltpu.make_async_copy(d_act_hbm.at[u], d_act_v.at[into], d_act_sem.at[into])

    for copy in weight_copies:
        copy.wait()

    def first_product(k, r):
        if r == 6:
            for h in range(2):
                remote("gd", h).wait_recv()
                remote("gc", 6, h).start()
        elif r % 2:
            for h in range(2 if r > 1 else 1):
                remote("gc", r - 1, h).wait_recv()
        source = grads_ref if r == 0 else all_grads.at[slot[r]]
        load = pltpu.make_async_copy(source, grads_v, local.at[5])
        load.start()
        if k >= 2:
            d_act_store(0, k % 2).wait()
        load.wait()
        for first in range(0, inner, 512):
            columns = pl.ds(first, min(512, inner - first))
            d_act_v[k % 2, :, columns] = dot(grads_v[...], down_v[columns, :], NT)
        d_act_store(slot[r], k % 2).start()

    first_product(0, 0)
    first_product(1, 1)
    for load in loads:
        load.wait()
    if summed:
        residual_ref[...] = jnp.zeros_like(residual_ref)
    else:
        @pl.when(middle)
        def _():
            remote("nr").wait_recv()
            sum_rows(quarter, (line_out.at[2], 0), [(attn_relay, 0)])
            remote("nm").start()

        remote("n", 1).wait_recv()

        def normed(arrived):
            def step(i, _):
                rows = pl.ds(pl.multiple_of(i * SUM_CHUNK, SUM_CHUNK), SUM_CHUNK)
                value = line_out[1, rows].astype(F32)
                for k in arrived:
                    value = value + attn_in[k, rows].astype(F32)
                value = value + line_out[0, rows].astype(F32)
                residual_ref[rows] = value
                mean = jnp.sum(value * value, axis=1, keepdims=True) * (1.0 / D)
                rows_ref[rows] = (value * lax.rsqrt(mean + epsilon) * gain_ref[...]).astype(BF16)
                return 0

            lax.fori_loop(0, quarter // SUM_CHUNK, step, 0)

        @pl.when(outside)
        def _():
            remote("nm").wait_recv()
            normed((0, 1))

        @pl.when(middle)
        def _():
            remote("n", 2).wait_recv()
            remote("n", 3).wait_recv()
            normed((0, 1, 2))

    remote("z", 2).start()
    remote("z", 1).start()
    pl.when(middle)(remote("z", 3).start)
    own_copy = pltpu.make_async_copy(rows_ref, all_rows.at[slot[0], part(0)], local.at[0])
    own_copy.start()
    spread(0)
    for h, r in ((0, 2), (1, 4), (1, 2), (0, 4)):
        remote("gx" if r == 2 else "gy", h).wait_recv()
        if r == 2 + 2 * h:
            remote("gd", h).start()
        remote("gc", r, h).start()
    first_product(2, 2)
    first_product(3, 3)
    remote("z", 1).wait_recv()
    spread(1)
    first_product(4, 4)
    first_product(5, 5)
    remote("z", 2).wait_recv()
    pl.when(middle)(remote("zr").start)
    spread(2)
    arrived_x(0)
    first_product(6, 6)
    first_product(7, 7)
    pl.when(middle)(remote("z", 3).wait_recv)
    pl.when(outside)(remote("zr").wait_recv)
    spread(3)
    arrived_x(1)
    own_copy.wait()
    load_rows(0).start()
    for k in range(2):
        d_act_store(0, k).wait()
    d_act_load(0, 0).start()

    def mask_loads(r):
        from_exp = (lax.rem(exp_index, GROUP) ^ r) * seq_len
        return [
            pltpu.make_async_copy(
                mask_hbm.at[pl.ds(pl.multiple_of(from_exp + (tp_index ^ q) * quarter, quarter), quarter)],
                mask_v.at[part(q)],
                mask_sem.at[q],
            )
            for q in range(parts)
        ]

    def act_store(u):
        into = u % 2
        return pltpu.make_async_copy(act_v.at[into], act_hbm.at[u], act_sem.at[into])

    def act_load(u):
        into = u % 2
        return pltpu.make_async_copy(act_hbm.at[u], act_v.at[into], act_sem.at[into])

    def wide_stores(u):
        return [
            pltpu.make_async_copy(
                wide_grad_v.at[:, pl.ds(0, first_part)], gate_grad_hbm.at[u], local.at[4]
            ),
            pltpu.make_async_copy(
                wide_grad_v.at[:, pl.ds(first_part, wide - first_part)], up_grad_hbm.at[u], local.at[7]
            ),
        ]

    def out_store(s):
        kept = out_odd if ORDER[s] % 2 else out_even
        return pltpu.make_async_copy(out_v.at[s % 2], kept.at[ORDER[s] // 2], out_sem.at[s % 2])

    def unit(u, _):
        into = lax.rem(u, 2)

        for s in range(GROUP):
            @pl.when(u == s)
            def _(s=s):
                for load in mask_loads(ORDER[s]):
                    load.start()

        load_rows(u).wait()
        for load in mask_loads(0):
            load.wait()

        d_act_load(u, into).wait()

        @pl.when(u > 1)
        def _():
            act_store(u - 2).wait()

        @pl.when(u > 0)
        def _():
            for store in wide_stores(u - 1):
                store.wait()

        linear = dot(rows_v[...], wide_v[shared_place:, :], NT)
        logits = linear[:, shared_padded : shared_padded + LANES]
        lane = lax.broadcasted_iota(jnp.int32, logits.shape, 1)
        logits = jnp.where(lane < experts_all, logits, -1e30)
        raised = jnp.exp(logits - jnp.max(logits, axis=1, keepdims=True))
        probs = raised / jnp.sum(raised, axis=1, keepdims=True)
        mask = mask_v[...].astype(F32)
        chosen = probs * mask
        chosen_sum = jnp.sum(chosen, axis=1, keepdims=True)
        probs_v[...] = probs
        gates_v[...] = chosen / chosen_sum

        def tile(linear, at_gate, at_up, place, j, gate):
            one = pl.ds(j * LANES, LANES)
            for first in range(0, seq_len, ROW_CHUNK):
                last = first + ROW_CHUNK
                gate_lin = linear[first:last, at_gate : at_gate + LANES]
                up_lin = linear[first:last, at_up : at_up + LANES]
                sigmoid = 0.5 * jnp.tanh(0.5 * gate_lin) + 0.5
                silu = gate_lin * sigmoid
                act = silu * up_lin
                d_act = d_act_v[into, first:last, one]
                if gate is not None:
                    total_v[first:last] += act * d_act
                    act = act * gate[first:last]
                    d_act = d_act * gate[first:last]
                act_v[into, first:last, one] = act.astype(BF16)
                d_up = d_act * silu
                d_gate = d_act * up_lin * (sigmoid + silu * (1.0 - sigmoid))
                wide_grad_v[first:last, pl.ds(place + at_gate, LANES)] = d_gate.astype(BF16)
                wide_grad_v[first:last, pl.ds(place + at_up, LANES)] = d_up.astype(BF16)

        for k in range(shared_tiles):
            at_up = shared_padded + LANES + k * LANES
            tile(linear, k * LANES, at_up, shared_place, local_experts * expert_tiles + k, None)
        d_gates = jnp.zeros(logits.shape, F32)
        for e in range(local_experts):
            mine = lane == exp_index * local_experts + e
            gate = jnp.sum(jnp.where(mine, gates_v[...], 0.0), axis=1, keepdims=True)
            total_v[...] = jnp.zeros(logits.shape, F32)
            place = 2 * e * padded
            linear = dot(rows_v[...], wide_v[place : place + 2 * padded, :], NT)
            for k in range(expert_tiles):
                tile(linear, k * LANES, padded + k * LANES, place, e * expert_tiles + k, gate)
            d_gates = jnp.where(mine, jnp.sum(total_v[...], axis=1, keepdims=True), d_gates)
        probs, gates, mask = probs_v[...], gates_v[...], mask_v[...].astype(F32)
        chosen_sum = jnp.sum(probs * mask, axis=1, keepdims=True)
        d_gates = d_gates * mask
        d_chosen = (d_gates - jnp.sum(d_gates * gates, axis=1, keepdims=True)) / chosen_sum
        d_probs = d_chosen * mask
        d_logits = probs * (d_probs - jnp.sum(d_probs * probs, axis=1, keepdims=True))
        high = d_logits.astype(BF16)
        low = pltpu.roll(d_logits - high.astype(F32), experts_all, 1)
        wide_grad_v[:, pl.ds(router_place, LANES)] = jnp.where(
            lane < experts_all, high.astype(F32), low
        ).astype(BF16)
        act_store(u).start()
        for store in wide_stores(u):
            store.start()

        @pl.when(u < GROUP - 1)
        def _():
            d_act_load(u + 1, 1 - into).start()

        @pl.when(u == 0)
        def _():
            for q in range(half_parts, parts):
                arrived_y(q)
            for q in range(parts):
                spread_rest(q)

        @pl.when(u == 1)
        def _():
            for q in range(half_parts):
                arrived_far(q)

        @pl.when(u == 3)
        def _():
            for q in range(half_parts, parts):
                arrived_x(q)

        @pl.when(u == 4)
        def _():
            for q in range(half_parts):
                arrived_y(q)

        @pl.when(u == 3)
        def _():
            remote("b", 0).wait_send()

        @pl.when(u == 4)
        def _():
            remote("b", 6).wait_send()

        @pl.when(u == 5)
        def _():
            remote("r", 0).wait_send()
            remote("r", 1).wait_send()

        @pl.when(u == 6)
        def _():
            remote("b", 2).wait_send()

        @pl.when(u == 7)
        def _():
            for q in range(parts):
                remote("s", 2, q).wait_send()

        back = back_v.at[into]

        def back_step(n, _):
            columns = pl.ds(pl.multiple_of(n * 512, 512), 512)
            back[:, columns] = dot(wide_grad_v[...], wide_v[:, columns], NN).astype(BF16)
            return 0

        lax.fori_loop(0, D // 512, back_step, 0)

        @pl.when(u == 0)
        def _():
            own_v[...] = back_v[0]

        @pl.when(u == slot[1])
        def _():
            remote("b", 0).start()

        @pl.when(u == slot[7])
        def _():
            remote("b", 6).start()

        @pl.when(u == slot[6])
        def _():
            remote("b", 6).wait_recv()
            sum_rows(seq_len, (back_v.at[slot[6] % 2], 0), [(core_v.at[3], 0)])
            remote("r", 0).start()
            remote("r", 1).start()

        @pl.when(u == slot[3])
        def _():
            remote("b", 2).start()

        @pl.when(u == slot[2])
        def _():
            remote("b", 2).wait_recv()
            remote("r", 0).wait_recv()
            mine = back_v.at[slot[2] % 2]
            sum_rows(half_rows, (mine, 0), [(core_v.at[1], 0), (relay_v.at[0], 0)])
            sum_rows(half_rows, (mine, half_rows), [(core_v.at[1], half_rows)])
            for q in range(parts):
                remote("s", 2, q).start()

        @pl.when(u == slot[5])
        def _():
            remote("b", 4).start()

        @pl.when(u == slot[4])
        def _():
            remote("b", 4).wait_recv()
            remote("r", 1).wait_recv()
            mine = back_v.at[slot[4] % 2]
            sum_rows(half_rows, (mine, half_rows), [(core_v.at[2], half_rows), (relay_v.at[1], 0)])
            sum_rows(half_rows, (mine, 0), [(core_v.at[2], 0)])
            for q in range(parts - 1, -1, -1):
                remote("s", 4, q).start()

        for k, r in ((0, 0), (1, 6), (3, 2), (5, 4)):
            @pl.when(u == k)
            def _(k=k, r=r):
                if k == 1:
                    for q in range(half_parts, parts):
                        arrived_far(q)
                for q in range(parts):
                    remote("c", r, q).wait_recv()

        @pl.when(u < GROUP - 1)
        def _():
            load_rows(u + 1).start()

        return 0

    lax.fori_loop(0, GROUP, unit, 0)

    remote("b", 0).wait_recv()

    def finish(q):
        remote("s", 2, q).wait_recv()
        remote("s", 4, q).wait_recv()
        first = q * quarter
        sources = [(own_v, first), (core_v.at[0], first), (cross_v.at[0], first), (cross_v.at[1], first)]

        def total_step(i, _):
            total = None
            for ref, start in sources:
                rows = pl.ds(pl.multiple_of(start + i * SUM_CHUNK, SUM_CHUNK), SUM_CHUNK)
                value = ref[rows].astype(F32)
                total = value if total is None else total + value
            rows = pl.ds(pl.multiple_of(i * SUM_CHUNK, SUM_CHUNK), SUM_CHUNK)
            if q == 0:
                back_ref[rows] = total
            else:
                line_out[q - 1, rows] = total.astype(BF16)
            return 0

        lax.fori_loop(0, quarter // SUM_CHUNK, total_step, 0)
        if q:
            remote("t", q).start()

    if not summed:
        pl.when(middle)(remote("nm").wait_send)

    for u in (GROUP - 2, GROUP - 1):
        act_store(u).wait()
    for store in wide_stores(GROUP - 1):
        store.wait()
    act_load(0).start()

    def out_unit(u, _):
        into = lax.rem(u, 2)

        @pl.when(u < GROUP - 1)
        def _():
            act_load(u + 1).start()

        act_load(u).wait()
        for s in range(2, GROUP):
            @pl.when(u == s)
            def _(s=s):
                out_store(s - 2).wait()

        def out_step(n, _):
            columns = pl.ds(pl.multiple_of(n * 512, 512), 512)
            out_v[into, :, columns] = dot(act_v[into], down_v[:, columns], NN).astype(BF16)
            return 0

        lax.fori_loop(0, D // 512, out_step, 0)
        for s in range(GROUP):
            @pl.when(u == s)
            def _(s=s):
                out_store(s).start()

        for q in range(1, parts):
            @pl.when(u == GROUP - 1 - 2 * (q - 1))
            def _(q=q):
                finish(q)

        return 0

    lax.fori_loop(0, GROUP, out_unit, 0)
    finish(0)
    for s in (GROUP - 2, GROUP - 1):
        out_store(s).wait()
    for k in range(parts - 1, 0, -1):
        remote("t", k).wait_recv()

    def last_step(i, _):
        rows = pl.ds(pl.multiple_of(i * ROW_CHUNK, ROW_CHUNK), ROW_CHUNK)
        total = back_ref[rows]
        for k in range(1, parts):
            total = total + line_in[k - 1, rows].astype(F32)
        back_ref[rows] = total
        return 0

    lax.fori_loop(0, quarter // ROW_CHUNK, last_step, 0)

    grads_copy.wait()

    @pl.when(middle)
    def _():
        remote("z", 3).wait_send()
        remote("zr").wait_send()
        if not summed:
            remote("n", 3).wait_send()

    if not summed:
        @pl.when(outside)
        def _():
            remote("n", 2).wait_send()
            remote("nr").wait_send()

    waited = [("b", 0), ("b", 6), ("r", 0), ("r", 1), ("b", 2)] + [("s", 2, q) for q in range(parts)]
    waited += [("z", 3), ("zr",), ("n", 2), ("n", 3), ("nr",), ("nm",)]
    for name in copies:
        if name not in waited:
            remote(*name).wait_send()


def expert_layer(attn, tokens, gain, grads, mask, weights, sizes):
    parts, _, local_experts, expert_tiles, shared_tiles, summed = sizes
    quarter = tokens.shape[0]
    seq_len = parts * quarter
    inner = (local_experts * expert_tiles + shared_tiles) * LANES
    wide = 2 * inner + LANES
    first_part = 2 * expert_tiles * LANES
    loads = 4 + 3 * local_experts
    copies = 3 * (parts - 1) + 9 * parts + 6 + 13 + 3
    hbm = pl.BlockSpec(memory_space=pl.ANY)
    every = jax.ShapeDtypeStruct((GROUP, seq_len, D), BF16)
    some = jax.ShapeDtypeStruct((GROUP // 2, seq_len, D), BF16)
    flops = 2 * GROUP * seq_len * D * (2 * wide + 2 * inner)
    return pl.pallas_call(
        functools.partial(expert_kernel, sizes),
        out_shape=(
            every,
            every,
            jax.ShapeDtypeStruct((GROUP, seq_len, inner), BF16),
            jax.ShapeDtypeStruct((GROUP, seq_len, first_part), BF16),
            jax.ShapeDtypeStruct((GROUP, seq_len, wide - first_part), BF16),
            some,
            some,
            jax.ShapeDtypeStruct((GROUP, seq_len, inner), F32),
            jax.ShapeDtypeStruct((quarter, D), F32),
            jax.ShapeDtypeStruct((quarter, D), BF16),
            jax.ShapeDtypeStruct((quarter, D), F32),
        ),
        in_specs=[hbm] * 2 + [pl.BlockSpec(memory_space=pltpu.VMEM)] + [hbm] * (2 + len(weights)),
        out_specs=(hbm,) * 8 + (pl.BlockSpec(memory_space=pltpu.VMEM),) * 3,
        scratch_shapes=[
            pltpu.VMEM((wide, D), BF16),
            pltpu.VMEM((inner, D), BF16),
            pltpu.VMEM((seq_len, D), BF16),
            pltpu.VMEM((seq_len, D), BF16),
            pltpu.VMEM((seq_len, LANES), BF16),
            pltpu.VMEM((2, seq_len, inner), F32),
            pltpu.VMEM((2, seq_len, inner), BF16),
            pltpu.VMEM((seq_len, wide), BF16),
            pltpu.VMEM((seq_len, LANES), F32),
            pltpu.VMEM((seq_len, LANES), F32),
            pltpu.VMEM((seq_len, LANES), F32),
            pltpu.VMEM((2, seq_len, D), BF16),
            pltpu.VMEM((2, seq_len, D), BF16),
            pltpu.VMEM((seq_len, D), BF16),
            pltpu.VMEM((GROUP // 2, seq_len, D), BF16),
            pltpu.VMEM((2, seq_len // 2, D), BF16),
            pltpu.VMEM((2, seq_len, D), BF16),
            pltpu.VMEM((parts - 1, quarter, D), BF16),
            pltpu.VMEM((parts - 1, quarter, D), BF16),
            pltpu.VMEM((parts - 1, quarter, D), BF16),
            pltpu.VMEM((quarter, D), BF16),
            pltpu.SemaphoreType.DMA((copies,)),
            pltpu.SemaphoreType.DMA((copies,)),
            pltpu.SemaphoreType.DMA((8,)),
            pltpu.SemaphoreType.DMA((loads,)),
            pltpu.SemaphoreType.DMA((parts,)),
            pltpu.SemaphoreType.DMA((2,)),
            pltpu.SemaphoreType.DMA((2,)),
            pltpu.SemaphoreType.DMA((2,)),
        ],
        compiler_params=pltpu.CompilerParams(
            collective_id=4 if summed else 1,
            has_side_effects=True,
            vmem_limit_bytes=60 * 1024 * 1024,
        ),
        cost_estimate=pl.CostEstimate(flops=flops, bytes_accessed=120_000_000, transcendentals=0),
        name="experts",
    )(attn, tokens, gain, grads, mask, *weights)


def line_rows(own_rows):
    parts = lax.axis_size("tp")
    return jnp.concatenate([own_rows] + [swap(own_rows, "tp", k) for k in range(1, parts)], axis=0)


def add_cores(even, odd_swapped):
    return [(e.astype(F32) + o.astype(F32)).astype(BF16) for e, o in zip(even, odd_swapped)]


def far_halves(mine):
    half = mine[3].shape[0] // 2
    return swap(mine[3][:half], "exp", 4), swap(mine[3][half:], "exp", 2)


def near_sums(mine, far):
    half = mine[3].shape[0] // 2
    first = jnp.concatenate([mine[1][:half] + far[0], mine[1][half:]], axis=0)
    second = jnp.concatenate([mine[2][:half], mine[2][half:] + far[1]], axis=0)
    return swap(first, "exp", 2), swap(second, "exp", 4)


def chip_sums(mine, near):
    total = mine[0].astype(F32) + near[0].astype(F32) + near[1].astype(F32)
    total = total.reshape(lax.axis_size("tp"), -1, total.shape[1])
    return total[0], total.astype(BF16)


def line_sums(mine, near):
    result, low = chip_sums(mine, near)
    for k in range(1, low.shape[0]):
        result = result + swap(low[k], "tp", k).astype(F32)
    return result


def neighbours(parts):
    exp_index, tp_index = lax.axis_index("exp"), lax.axis_index("tp")
    line = [{"tp": tp_index ^ k} for k in range(1, parts)]
    return line, [{"exp": exp_index ^ r} for r in range(1, GROUP)]


def greet(peers):
    barrier = pltpu.get_barrier_semaphore()
    for peer in peers:
        pl.semaphore_signal(barrier, inc=1, device_id=peer, device_id_type=pl.DeviceIdType.MESH)
    pl.semaphore_wait(barrier, len(peers))


def remote_maker(copies, send, recv):
    number = {name: k for k, name in enumerate(copies)}

    def remote(*name):
        source, target, device = copies[name]
        return pltpu.make_async_remote_copy(
            source,
            target,
            send.at[number[name]],
            recv.at[number[name]],
            device_id=device,
            device_id_type=pl.DeviceIdType.MESH,
        )

    return remote


def inside(place):
    return (place == 1) | (place == 2)


def gather_kernel(parts, *refs):
    tokens_ref, grads_ref, proj_ref, narrow_ref, out_ref, mask_ref = refs[:6]
    gate_ref, up_ref, down_ref, tokens_all, grads_all, proj_all = refs[6:12]
    narrow_all, out_all, mask_all, gate_all, up_all, down_all = refs[12:18]
    send, recv, local = refs[18:]
    exp_index, tp_index = lax.axis_index("exp"), lax.axis_index("tp")
    line, near = neighbours(parts)
    quarter, depth, seq_len = tokens_ref.shape[0], proj_ref.shape[0], mask_ref.shape[0]
    width = down_ref.shape[2]

    def block(whole, size, r, axis=0):
        place = pl.ds(pl.multiple_of((exp_index ^ r) * size, size), size)
        return whole.at[place] if axis == 0 else whole.at[:, place]

    def arrays(r):
        return {
            "p": block(proj_all, depth, r),
            "n": block(narrow_all, narrow_ref.shape[1], r, 1),
            "o": block(out_all, out_ref.shape[1], r, 1),
            "m": block(mask_all, seq_len, r),
        }

    own = {"p": proj_ref, "n": narrow_ref, "o": out_ref, "m": mask_ref}
    my_rows = pl.ds(pl.multiple_of(tp_index * quarter, quarter), quarter)
    copies = {}
    for k in range(1, parts):
        copies["z", 0, k] = (tokens_ref, tokens_all.at[my_rows], line[k - 1])
        copies["z", 1, k] = (grads_ref, grads_all.at[pl.ds(k * quarter, quarter)], line[k - 1])
    passed = pl.ds(pl.multiple_of((tp_index ^ 2) * quarter, quarter), quarter)
    copies["zr", 0] = (tokens_all.at[passed], tokens_all.at[passed], line[0])
    copies["zr", 1] = (
        grads_all.at[pl.ds(2 * quarter, quarter)],
        grads_all.at[pl.ds(3 * quarter, quarter)],
        line[0],
    )
    for key, ref in own.items():
        mine = arrays(0)[key]
        copies["g", 2, key] = (ref, mine, near[1])
        copies["g", 4, key] = (ref, mine, near[3])
        via = 2 if key in "pn" else 4
        passed = arrays(via)[key]
        copies["g", 6, key] = (passed, passed, near[5 - via])
        copies["c", 0, key] = (ref, mine, near[0])
        for r in (2, 4, 6):
            copies["c", r, key] = (arrays(r)[key], arrays(r)[key], near[0])
    for r in range(1, GROUP):
        to = exp_index ^ r
        copies["a", r, 0] = (gate_ref.at[to], block(gate_all, width, 0, 1), near[r - 1])
        copies["a", r, 1] = (up_ref.at[to], block(up_all, width, 0, 1), near[r - 1])
        copies["a", r, 2] = (down_ref.at[to], block(down_all, width, 0, 1), near[r - 1])
    remote = remote_maker(copies, send, recv)

    greet(line + near)
    for kind in range(2):
        remote("z", kind, 2).start()
        remote("z", kind, 1).start()
        pl.when(inside(tp_index))(remote("z", kind, 3).start)
    for key in own:
        for r in (2, 4):
            remote("g", r, key).start()
        remote("c", 0, key).start()
    kept = [
        (tokens_ref, tokens_all.at[my_rows]),
        (grads_ref, grads_all.at[pl.ds(0, quarter)]),
        (proj_ref, arrays(0)["p"]),
        (narrow_ref, arrays(0)["n"]),
        (out_ref, arrays(0)["o"]),
        (mask_ref, arrays(0)["m"]),
        (gate_ref.at[exp_index], block(gate_all, width, 0, 1)),
        (up_ref.at[exp_index], block(up_all, width, 0, 1)),
        (down_ref.at[exp_index], block(down_all, width, 0, 1)),
    ]
    kept = [pltpu.make_async_copy(s, t, local.at[k]) for k, (s, t) in enumerate(kept)]
    for copy in kept:
        copy.start()
    for key in own:
        for r in (2, 4):
            remote("g", r, key).wait_recv()
            if r == (2 if key in "pn" else 4):
                remote("g", 6, key).start()
            remote("c", r, key).start()
    for r in range(1, GROUP):
        for k in range(3):
            remote("a", r, k).start()
    for kind in range(2):
        remote("z", kind, 2).wait_recv()
        pl.when(inside(tp_index))(remote("zr", kind).start)
    for key in own:
        remote("g", 6, key).wait_recv()
        remote("c", 6, key).start()
    for copy in kept:
        copy.wait()
    for name in copies:
        if name[0] in "ca":
            remote(*name).wait_recv()
    for kind in range(2):
        remote("z", kind, 1).wait_recv()

        @pl.when(inside(tp_index))
        def _(kind=kind):
            remote("z", kind, 3).wait_recv()
            remote("z", kind, 3).wait_send()
            remote("zr", kind).wait_send()

        pl.when(jnp.logical_not(inside(tp_index)))(remote("zr", kind).wait_recv)
        for k in (1, 2):
            remote("z", kind, k).wait_send()
    for name in copies:
        if name[0] not in ("z", "zr"):
            remote(*name).wait_send()


def gather_inputs(tokens, grads, proj, narrow, out, mask, gate, up, down):
    parts = lax.axis_size("tp")
    hbm = pl.BlockSpec(memory_space=pl.ANY)
    depth, seq_len = proj.shape[0], mask.shape[0]
    shapes = [
        (parts * tokens.shape[0], D),
        (parts * tokens.shape[0], D),
        (GROUP * depth, proj.shape[1]),
        (narrow.shape[0], GROUP * narrow.shape[1]),
        (out.shape[0], GROUP * out.shape[1]),
        (GROUP * seq_len, LANES),
        *((w.shape[1], GROUP * w.shape[2]) for w in (gate, up, down)),
    ]
    copies = 2 * parts + 4 * 7 + 3 * (GROUP - 1)
    return pl.pallas_call(
        functools.partial(gather_kernel, parts),
        out_shape=tuple(jax.ShapeDtypeStruct(s, BF16) for s in shapes),
        in_specs=[hbm] * 9,
        out_specs=(hbm,) * 9,
        scratch_shapes=[
            pltpu.SemaphoreType.DMA((copies,)),
            pltpu.SemaphoreType.DMA((copies,)),
            pltpu.SemaphoreType.DMA((9,)),
        ],
        compiler_params=pltpu.CompilerParams(collective_id=2, has_side_effects=True),
        name="gather_inputs",
    )(tokens, grads, proj, narrow, out, mask, gate, up, down)


def scatter_kernel(parts, *refs):
    proj_ref, out_ref, mine_ref, line_ref, gate_ref, up_ref, down_ref = refs[:7]
    proj_sum, out_sum, output_ref, gate_back, up_back, down_back = refs[7:13]
    proj_core, out_core, proj_add, out_add, proj_relay, out_relay = refs[13:19]
    proj_cross, out_cross, narrow, narrow_in, line_in, send, recv, local = refs[19:]
    exp_index = lax.axis_index("exp")
    line, near = neighbours(parts)
    depth, width = proj_sum.shape[0], out_sum.shape[1]

    def proj_block(r):
        return proj_ref.at[pl.ds(pl.multiple_of((exp_index ^ r) * depth, depth), depth)]

    def out_block(r):
        return out_ref.at[:, pl.ds(pl.multiple_of((exp_index ^ r) * width, width), width)]

    copies = {}
    for r in (6, 2, 4, 0):
        copies["c", r, 0] = (proj_block(r + 1), proj_core.at[r // 2], near[0])
        copies["c", r, 1] = (out_block(r + 1), out_core.at[r // 2], near[0])
    copies["d", 0] = (proj_add.at[2], proj_relay, near[3])
    copies["d", 1] = (out_add.at[2], out_relay, near[1])
    for side, r in enumerate((2, 4)):
        copies["s", r, 0] = (proj_add.at[side], proj_cross.at[side], near[r - 1])
        copies["s", r, 1] = (out_add.at[side], out_cross.at[side], near[r - 1])
    for k in range(1, parts):
        copies["z", k] = (narrow, narrow_in.at[k - 1], line[k - 1])
        copies["t", k] = (line_ref.at[k], line_in.at[k - 1], line[k - 1])
    for r in range(1, GROUP):
        to = exp_index ^ r
        copies["a", r, 0] = (gate_ref.at[to], gate_back.at[exp_index], near[r - 1])
        copies["a", r, 1] = (up_ref.at[to], up_back.at[exp_index], near[r - 1])
        copies["a", r, 2] = (down_ref.at[to], down_back.at[exp_index], near[r - 1])
    remote = remote_maker(copies, send, recv)

    def total(target, sources):
        count = target.shape[0]

        def chunk(i, _):
            rows = pl.ds(pl.multiple_of(i * 32, 32), 32)
            value = sum(ref[rows].astype(F32) for ref in sources[1:])
            target[rows] = (sources[0][rows].astype(F32) + value).astype(target.dtype)
            return 0

        lax.fori_loop(0, count // 32, chunk, 0)

    greet(line + near)
    for k in range(1, parts):
        remote("t", k).start()
    for r in (6, 2, 4, 0):
        for k in range(2):
            remote("c", r, k).start()
    for k in range(2):
        remote("c", 6, k).wait_recv()
    total(proj_add.at[2], [proj_block(6), proj_core.at[3]])
    remote("d", 0).start()
    total(out_add.at[2], [out_block(6), out_core.at[3]])
    remote("d", 1).start()
    for r in (2, 4):
        for k in range(2):
            remote("c", r, k).wait_recv()
    total(out_add.at[0], [out_block(2), out_core.at[1]])
    remote("s", 2, 1).start()
    total(proj_add.at[1], [proj_block(4), proj_core.at[2]])
    remote("s", 4, 0).start()
    remote("d", 0).wait_recv()
    total(proj_add.at[0], [proj_block(2), proj_core.at[1], proj_relay])
    remote("s", 2, 0).start()
    remote("d", 1).wait_recv()
    total(out_add.at[1], [out_block(4), out_core.at[2], out_relay])
    remote("s", 4, 1).start()
    for r in range(1, GROUP):
        for k in range(3):
            remote("a", r, k).start()
    kept = [
        pltpu.make_async_copy(source.at[exp_index], target.at[exp_index], local.at[k])
        for k, (source, target) in enumerate(
            ((gate_ref, gate_back), (up_ref, up_back), (down_ref, down_back))
        )
    ]
    for copy in kept:
        copy.start()
    for k in range(2):
        remote("c", 0, k).wait_recv()
        for r in (2, 4):
            remote("s", r, k).wait_recv()
        if k == 0:
            total(proj_sum, [proj_block(0), proj_core.at[0], proj_cross.at[0], proj_cross.at[1]])
            narrow[...] = proj_sum[:, proj_sum.shape[1] - LANES :]
            for j in range(1, parts):
                remote("z", j).start()
        else:
            total(out_sum, [out_block(0), out_core.at[0], out_cross.at[0], out_cross.at[1]])
    for j in range(1, parts):
        remote("z", j).wait_recv()
    value = narrow[...]
    for j in range(1, parts):
        value = value + narrow_in[j - 1]
    proj_sum[:, proj_sum.shape[1] - LANES :] = value
    for j in range(1, parts):
        remote("t", j).wait_recv()
    total(output_ref, [mine_ref] + [line_in.at[j - 1] for j in range(1, parts)])
    for copy in kept:
        copy.wait()
    for r in range(1, GROUP):
        for k in range(3):
            remote("a", r, k).wait_recv()
    for name in copies:
        remote(*name).wait_send()


def scatter_grads(proj, out, mine, line, gate, up, down):
    parts = lax.axis_size("tp")
    hbm, vmem = pl.BlockSpec(memory_space=pl.ANY), pl.BlockSpec(memory_space=pltpu.VMEM)
    one = (proj.shape[0] // GROUP, proj.shape[1])
    two = (out.shape[0], out.shape[1] // GROUP)
    narrow = (one[0], LANES)
    copies = 8 + 2 + 4 + 2 * (parts - 1) + 3 * (GROUP - 1)
    return pl.pallas_call(
        functools.partial(scatter_kernel, parts),
        out_shape=(
            jax.ShapeDtypeStruct(one, F32),
            jax.ShapeDtypeStruct(two, F32),
            jax.ShapeDtypeStruct(mine.shape, BF16),
            *(jax.ShapeDtypeStruct(x.shape, x.dtype) for x in (gate, up, down)),
        ),
        in_specs=[vmem] * 3 + [hbm] * 4,
        out_specs=(vmem, vmem, vmem, hbm, hbm, hbm),
        scratch_shapes=[
            pltpu.VMEM((GROUP // 2, *one), BF16),
            pltpu.VMEM((GROUP // 2, *two), BF16),
            pltpu.VMEM((3, *one), BF16),
            pltpu.VMEM((3, *two), BF16),
            pltpu.VMEM(one, BF16),
            pltpu.VMEM(two, BF16),
            pltpu.VMEM((2, *one), BF16),
            pltpu.VMEM((2, *two), BF16),
            pltpu.VMEM(narrow, F32),
            pltpu.VMEM((parts - 1, *narrow), F32),
            pltpu.VMEM((parts - 1, *mine.shape), BF16),
            pltpu.SemaphoreType.DMA((copies,)),
            pltpu.SemaphoreType.DMA((copies,)),
            pltpu.SemaphoreType.DMA((3,)),
        ],
        compiler_params=pltpu.CompilerParams(
            collective_id=3, has_side_effects=True, vmem_limit_bytes=40 * 1024 * 1024
        ),
        name="scatter_grads",
    )(proj, out, mine, line, gate, up, down)


def pad_to(value, axis, multiple):
    widths = [(0, 0)] * value.ndim
    widths[axis] = (0, -value.shape[axis] % multiple)
    return jnp.pad(value, widths)


def shards(
    tokens,
    cotangent,
    segment_ids,
    routes,
    norm1_gain,
    attn_q,
    attn_k,
    attn_v,
    attn_o,
    norm2_gain,
    router,
    shared_gate,
    shared_up,
    shared_down,
    expert_gate,
    expert_up,
    expert_down,
):
    exp_count = lax.axis_size("exp")
    tp_count = lax.axis_size("tp")
    exp_index = lax.axis_index("exp")
    tp_index = lax.axis_index("tp")
    quarter = tokens.shape[0]
    seq_len = quarter * tp_count

    experts_all = router.shape[1]
    local_experts, _, hidden = expert_gate.shape
    shared_hidden = shared_gate.shape[1] // exp_count
    in_group = exp_count == GROUP
    qkv_widths = (attn_q.shape[1], attn_k.shape[1], attn_v.shape[1])
    gains = jnp.stack([norm1_gain, norm2_gain], axis=0)
    proj = jnp.concatenate([attn_q, attn_k, attn_v], axis=1)
    qkv_width = sum(qkv_widths)
    narrow_weight = pad_to(jnp.concatenate([router.T, gains], axis=0), 0, 16)
    member_lanes = jnp.any(
        routes[:, :, None] == jnp.arange(LANES, dtype=jnp.int32), axis=1
    ).astype(BF16)

    def cut(weight):
        return pad_to(weight.reshape(exp_count, shared_hidden, -1), 1, 16)

    cut_gate, cut_up, cut_down = cut(shared_gate.T), cut(shared_up.T), cut(shared_down)
    if in_group:
        (
            whole,
            own_grads,
            qkv_weight,
            narrow_weight,
            output_weight,
            all_masks,
            my_gate,
            my_up,
            my_down,
        ) = gather_inputs(
            tokens, cotangent, proj, narrow_weight, attn_o, member_lanes, cut_gate, cut_up, cut_down
        )
    else:
        whole = lax.all_gather(tokens, "tp", axis=0, tiled=True)
        own_grads = line_rows(cotangent)
        qkv_weight = lax.all_gather(proj, "exp", axis=0, tiled=True)
        narrow_weight = lax.all_gather(narrow_weight, "exp", axis=1, tiled=True)
        output_weight = lax.all_gather(attn_o, "exp", axis=1, tiled=True)
        all_masks = lax.all_gather(member_lanes, "exp", axis=0, tiled=True)
        my_gate, my_up, my_down = (
            lax.all_to_all(w, "exp", split_axis=0, concat_axis=2, tiled=True)
            for w in (cut_gate, cut_up, cut_down)
        )
        my_gate, my_up, my_down = my_gate[0], my_up[0], my_down[0]
    first_norm_scale = narrow_weight[experts_all].astype(F32)
    second_norm_scale = narrow_weight[experts_all + 1].astype(F32)
    own_tokens = tokens.astype(F32)
    whole = whole.astype(F32)
    scale_one = lax.rsqrt(jnp.mean(whole * whole, axis=-1, keepdims=True) + epsilon)
    normed_one = (whole * scale_one * first_norm_scale).astype(BF16)
    heads_dev = qkv_widths[0] // HEAD_DIM
    kv_dev = qkv_widths[1] // HEAD_DIM
    group_size = heads_dev // kv_dev
    score_scale = HEAD_DIM ** (-0.5)
    cosine, sine = rotary_tables(seq_len, HEAD_DIM)
    qkv_lin = dot(normed_one, qkv_weight, NN).reshape(seq_len, -1, HEAD_DIM)
    turned = rotate(qkv_lin[:, : heads_dev + kv_dev], cosine, sine).astype(BF16)
    queries = turned[:, :heads_dev].reshape(seq_len, kv_dev, group_size, HEAD_DIM)
    keys_rot = turned[:, heads_dev:]
    values = qkv_lin[:, heads_dev + kv_dev :].astype(BF16)
    positions = jnp.arange(seq_len, dtype=jnp.int32)
    allowed = (positions[None, :] <= positions[:, None]) & (
        segment_ids[:, None] == segment_ids[None, :]
    )
    raw_scores = jnp.einsum("qkgd,ckd->kgqc", queries, keys_rot, preferred_element_type=F32)
    scores = jnp.where(allowed, raw_scores * score_scale, -1e30)
    exponent = jnp.exp(scores - jnp.max(scores, axis=-1, keepdims=True))
    probs = exponent / jnp.sum(exponent, axis=-1, keepdims=True)
    probs_low = probs.astype(BF16)
    attended = jnp.einsum("kgqc,ckd->qkgd", probs_low, values, preferred_element_type=F32)
    attended = attended.reshape(seq_len, heads_dev * HEAD_DIM).astype(BF16)
    attn_part = dot(attended, output_weight, NN).astype(BF16)

    expert_tiles, shared_tiles = -(-hidden // LANES), -(-my_gate.shape[0] // LANES)
    router_rows = narrow_weight[:experts_all]
    router_pad = jnp.zeros((LANES - 2 * experts_all, D), BF16)
    weights = (
        expert_gate.transpose(0, 2, 1),
        expert_up.transpose(0, 2, 1),
        expert_down,
        my_gate,
        my_up,
        my_down,
        jnp.concatenate([router_rows, router_rows, router_pad], axis=0),
    )
    inner = (local_experts * expert_tiles + shared_tiles) * LANES
    sizes = (tp_count, experts_all, local_experts, expert_tiles, shared_tiles)
    gain_row = second_norm_scale[None, :]
    all_masks = all_masks.reshape(exp_count // GROUP, -1, LANES)

    d_normed_two, rest_sum, first_sum, down_sum = 0.0, 0.0, 0.0, 0.0
    for base in range(0, exp_count, GROUP):
        rows_b, own_b = attn_part, own_grads
        if base:
            rows_b, own_b = swap(normed_two, "exp", base), swap(own_grads, "exp", base)
        masks = lax.dynamic_index_in_dim(
            all_masks, (exp_index // GROUP) ^ (base // GROUP), keepdims=False
        )
        *results, back, rows_b, residual_b = expert_layer(
            rows_b, tokens, gain_row, own_b, masks, weights, (*sizes, base > 0)
        )
        all_rows, all_grads, act, first_grads, rest_grads, out_even, out_odd, _ = results
        if not base:
            normed_two, residual = rows_b, residual_b
            output = residual
        swapped = swap(out_odd, "exp", 1)
        d_normed_two = d_normed_two + (swap(back, "exp", base) if base else back)
        count = GROUP * seq_len
        grads_seen, act = all_grads.reshape(count, D), act.reshape(count, -1)
        rows_seen = all_rows.reshape(count, D)
        rest_grads, first_grads = rest_grads.reshape(count, -1), first_grads.reshape(count, -1)
        if base + GROUP < exp_count:
            rest_sum = rest_sum + dot(rest_grads, rows_seen, TN)
            first_sum = first_sum + dot(first_grads, rows_seen, TN)
            down_sum = down_sum + dot(act, grads_seen, TN)
            mine = add_cores(out_even, swapped)
            part_out = line_sums(mine, near_sums(mine, far_halves(mine)))
            output = output + (swap(part_out, "exp", base) if base else part_out)
            own_grads, normed_two, rest_sum, first_sum, down_sum, output = lax.optimization_barrier(
                (own_grads, normed_two, rest_sum, first_sum, down_sum, output)
            )
    down_sum = down_sum + dot(act, grads_seen, TN)
    swapped, down_sum = lax.optimization_barrier((swapped, down_sum))

    scale_two = lax.rsqrt(jnp.mean(residual * residual, axis=-1, keepdims=True) + epsilon)
    grad_gain_two, d_residual = norm_back(d_normed_two, residual, scale_two, second_norm_scale)
    d_residual = cotangent.astype(F32) + d_residual

    d_attn_low = lax.all_gather(d_residual.astype(BF16), "tp", axis=0, tiled=True)
    mine = add_cores(out_even, swapped)
    mine, first_grads = lax.optimization_barrier((mine, first_grads))
    first_sum = first_sum + dot(first_grads, rows_seen, TN)
    d_attn_low, first_sum, *far = lax.optimization_barrier((d_attn_low, first_sum, *far_halves(mine)))
    near = near_sums(mine, far)
    grad_out_w = dot(attended, d_attn_low, TN)
    d_attended = dot(d_attn_low, output_weight, NT).astype(BF16)
    d_attended = d_attended.reshape(seq_len, kv_dev, group_size, HEAD_DIM)
    d_probs_att = jnp.einsum("qkgd,ckd->kgqc", d_attended, values, preferred_element_type=F32)
    row_inner = jnp.sum(d_probs_att * probs, axis=-1, keepdims=True)
    d_raw = (probs * (d_probs_att - row_inner) * score_scale).astype(BF16)
    d_query = jnp.einsum("kgqc,ckd->qkgd", d_raw, keys_rot, preferred_element_type=F32).reshape(
        seq_len, heads_dev, HEAD_DIM
    )
    d_key = jnp.einsum("kgqc,qkgd->ckd", d_raw, queries, preferred_element_type=F32)
    d_value = jnp.einsum("kgqc,qkgd->ckd", probs_low, d_attended, preferred_element_type=F32)
    d_qkv = jnp.concatenate(
        [
            rotate_back(jnp.concatenate([d_query, d_key], axis=1), cosine, sine).astype(BF16),
            d_value.astype(BF16),
        ],
        axis=1,
    ).reshape(seq_len, -1)
    d_normed_one = dot(d_qkv, qkv_weight, NT).astype(BF16)
    d_normed_one, rest_grads, first_sum, down_sum = lax.optimization_barrier(
        (d_normed_one, rest_grads, first_sum, down_sum)
    )
    d_normed_one = lax.psum_scatter(
        d_normed_one, "tp", scatter_dimension=0, tiled=True
    ).astype(F32)
    grad_qkv = dot(normed_one, d_qkv, TN)
    rest_sum = rest_sum + dot(rest_grads, rows_seen, TN)
    d_normed_one, *near = lax.optimization_barrier((d_normed_one, *near))

    padded = expert_tiles * LANES

    spans = [first_sum] + [
        rest_sum[2 * e * padded : 2 * (e + 1) * padded] for e in range(local_experts - 1)
    ]
    grad_egate = jnp.stack([s[:hidden] for s in spans]).transpose(0, 2, 1)
    grad_eup = jnp.stack([s[padded : padded + hidden] for s in spans]).transpose(0, 2, 1)
    grad_edown = jnp.stack(
        [down_sum[e * padded : e * padded + hidden] for e in range(local_experts)]
    )
    shared_sum = rest_sum[2 * (local_experts - 1) * padded :]
    start = local_experts * padded
    shared_rows = my_gate.shape[0]
    place = shared_tiles * LANES
    grad_router = shared_sum[place : place + experts_all]
    grad_router = grad_router + shared_sum[place + experts_all : place + 2 * experts_all]
    if in_group:
        own_sum, line_parts = chip_sums(mine, near)
    else:
        own_sum = line_sums(mine, near)
    output = output + (swap(own_sum, "exp", base) if base else own_sum)
    own_scale = lax.rsqrt(jnp.mean(own_tokens * own_tokens, axis=-1, keepdims=True) + epsilon)
    grad_gain_one, d_input = norm_back(d_normed_one, own_tokens, own_scale, first_norm_scale)
    d_input = d_residual + d_input

    def uncut(grad):
        return grad.astype(BF16).reshape(grad.shape[0], exp_count, -1).transpose(1, 0, 2)

    narrow = jnp.concatenate(
        [grad_router.T, grad_gain_one[:, None], grad_gain_two[:, None]], axis=1
    )
    grad_proj = jnp.concatenate([grad_qkv, pad_to(narrow, 1, LANES)], axis=1).astype(BF16)
    grad_out_w = grad_out_w.astype(BF16)
    back_gate, back_up, back_down = (
        uncut(sums[:shared_rows])
        for sums in (shared_sum, shared_sum[place + LANES :], down_sum[start:])
    )
    if in_group:
        grad_proj, grad_out_w, output, back_gate, back_up, back_down = scatter_grads(
            grad_proj, grad_out_w, output, line_parts, back_gate, back_up, back_down
        )
        narrow = grad_proj[:, qkv_width:]
    else:
        output = output.astype(BF16)
        grad_proj = lax.psum_scatter(grad_proj, "exp", scatter_dimension=0, tiled=True).astype(F32)
        narrow = lax.psum(grad_proj[:, qkv_width:], "tp")
        grad_out_w = lax.psum_scatter(
            grad_out_w, "exp", scatter_dimension=1, tiled=True
        ).astype(F32)
        back_gate, back_up, back_down = (
            lax.all_to_all(x, "exp", split_axis=0, concat_axis=0, tiled=True)
            for x in (back_gate, back_up, back_down)
        )

    def joined(pieces):
        return pieces[:, :shared_hidden].reshape(-1, pieces.shape[2]).astype(F32)

    grad_sgate, grad_sup, grad_sdown = joined(back_gate).T, joined(back_up).T, joined(back_down)
    cuts = (qkv_widths[0], qkv_widths[0] + qkv_widths[1])
    return (
        output,
        d_input,
        narrow[:, experts_all],
        grad_proj[:, : cuts[0]],
        grad_proj[:, cuts[0] : cuts[1]],
        grad_proj[:, cuts[1] : qkv_width],
        grad_out_w,
        narrow[:, experts_all + 1],
        narrow[:, :experts_all],
        grad_sgate,
        grad_sup,
        grad_sdown,
        grad_egate,
        grad_eup,
        grad_edown,
    )


def solution(mesh):
    placed = (
        P(("exp", "tp"), None),
        P(("exp", "tp"), None),
        P("exp"),
        P("exp", None),
        P("exp"),
        P("exp", "tp"),
        P("exp", "tp"),
        P("exp", "tp"),
        P("tp", "exp"),
        P("exp"),
        P("exp", None),
        P("exp", "tp"),
        P("exp", "tp"),
        P("tp", "exp"),
        P("exp", None, "tp"),
        P("exp", None, "tp"),
        P("exp", "tp", None),
    )
    return jax.shard_map(
        shards,
        mesh=mesh,
        in_specs=placed,
        out_specs=(
            P(("exp", "tp"), None),
            P(("exp", "tp"), None),
            P("exp"),
            P("exp", "tp"),
            P("exp", "tp"),
            P("exp", "tp"),
            P("tp", "exp"),
            P("exp"),
            P("exp", None),
            P("exp", "tp"),
            P("exp", "tp"),
            P("tp", "exp"),
            P("exp", None, "tp"),
            P("exp", None, "tp"),
            P("exp", "tp", None),
        ),
        check_vma=False,
    )
```

```python
import functools

import jax
import jax.numpy as jnp
from jax import lax
from jax.experimental import pallas as pl
from jax.experimental.pallas import tpu as pltpu
from jax.sharding import PartitionSpec as P

D = 2048
HEAD_DIM = 128
TOP = 6


epsilon = 1e-06
rope_base = 600000.0
F32 = jnp.float32
BF16 = jnp.bfloat16


def rotary_tables(length, head_width):
    half_width = head_width // 2
    frequency = rope_base ** (-(jnp.arange(half_width, dtype=jnp.float32) * 2.0 / head_width))
    angles = jnp.arange(length, dtype=jnp.float32)[:, None] * frequency[None, :]
    return (jnp.cos(angles), jnp.sin(angles))


def rotate(values, cosine, sine):
    half_width = values.shape[-1] // 2
    first_half = values[..., :half_width]
    second_half = values[..., half_width:]
    cos_rows = cosine[:, None, :]
    sin_rows = sine[:, None, :]
    return jnp.concatenate(
        [
            first_half * cos_rows - second_half * sin_rows,
            second_half * cos_rows + first_half * sin_rows,
        ],
        axis=-1,
    )


def rotate_back(gradient, cosine, sine):
    return rotate(gradient, cosine, -sine)


def norm_back(grad_normed, input_tokens, scale_rows, gain):
    grad_gain = jnp.sum(grad_normed * input_tokens * scale_rows, axis=0)
    scaled_grad = grad_normed * gain
    grad_inputs = (
        scale_rows * scaled_grad
        - input_tokens
        * scale_rows
        * scale_rows
        * scale_rows
        * jnp.mean(scaled_grad * input_tokens, axis=-1, keepdims=True)
    )
    return (grad_gain, grad_inputs)


def dot(left, right, dims):
    return lax.dot_general(left, right, (dims, ((), ())), preferred_element_type=F32)


NN = ((1,), (0,))
NT = ((1,), (1,))
TN = ((0,), (0,))


def swap(value, axis, bit):
    size = lax.axis_size(axis)
    return lax.ppermute(value, axis, [(i, i ^ bit) for i in range(size)])


ORDER = (0, 1, 7, 6, 3, 2, 5, 4)
GROUP = len(ORDER)
LANES = 128
ROW_CHUNK = 64
SUM_CHUNK = 16


def expert_kernel(sizes, *refs):
    parts, experts_all, local_experts, expert_tiles, shared_tiles, summed = sizes
    refs = list(refs)

    def take(count):
        taken = refs[:count]
        del refs[:count]
        return taken

    attn_hbm, tokens_hbm, gain_ref, grads_ref, grads_x, grads_y = take(6)
    mask_hbm, gate_hbm, up_hbm, down_hbm = take(4)
    shared_gate_hbm, shared_up_hbm, shared_down_hbm, router_hbm = take(4)
    all_rows, all_grads, act_hbm, gate_grad_hbm, up_grad_hbm = take(5)
    out_even, out_odd, d_act_hbm, back_ref, rows_ref, residual_ref = take(6)
    wide_v, down_v, rows_v, grads_v, mask_v, d_act_v, act_v, wide_grad_v = take(8)
    probs_v, gates_v, total_v, out_v, back_v, own_v, core_v, relay_v, cross_v, line_in, line_out, attn_in, attn_relay = take(13)
    send, recv, local, weight_sem, mask_sem, d_act_sem, act_sem, out_sem = take(8)
    quarter = rows_ref.shape[0]
    seq_len = parts * quarter
    half_rows = seq_len // 2
    inner = down_v.shape[0]
    wide = wide_v.shape[0]
    padded = expert_tiles * LANES
    shared_padded = shared_tiles * LANES
    first_part = 2 * padded
    shared_place = 2 * local_experts * padded
    router_place = shared_place + shared_padded
    exp_index = lax.axis_index("exp")
    tp_index = lax.axis_index("tp")
    slot = {r: s for s, r in enumerate(ORDER)}

    def part(q):
        return pl.ds(q * quarter, quarter)

    def chip(r):
        return {"exp": exp_index ^ r}

    def line(k):
        return {"tp": tp_index ^ k}

    copies = {}
    for k in range(1, parts):
        copies["z", k] = (rows_ref, all_rows.at[slot[0], part(k)], line(k))
        there = pl.ds(pl.multiple_of((tp_index ^ k) * quarter, quarter), quarter)
        if not summed:
            copies["n", k] = (attn_hbm.at[there], attn_in.at[k - 1], line(k))
        copies["t", k] = (line_out.at[k - 1], line_in.at[k - 1], line(k))
    copies["zr",] = (all_rows.at[slot[0], part(2)], all_rows.at[slot[0], part(3)], line(1))
    if not summed:
        copies["nr",] = (attn_hbm.at[there], attn_relay, line(1))
        copies["nm",] = (line_out.at[2], attn_in.at[1], line(2))
    for q in range(parts):
        own = rows_ref if q == 0 else all_rows.at[slot[0], part(q)]
        copies["x", q] = (own, all_rows.at[slot[2], part(q)], chip(2))
        copies["y", q] = (own, all_rows.at[slot[4], part(q)], chip(4))
        via = 2 if 2 * q < parts else 4
        copies["d", q] = (all_rows.at[slot[via], part(q)], all_rows.at[slot[6], part(q)], chip(6 - via))
        for r in (0, 2, 4, 6):
            here = own if r == 0 else all_rows.at[slot[r], part(q)]
            copies["c", r, q] = (here, all_rows.at[slot[r + 1], part(q)], chip(1))
        for side, r in enumerate((2, 4)):
            copies["s", r, q] = (back_v.at[slot[r] % 2, part(q)], cross_v.at[side, part(q)], chip(r))
    for r in (0, 2, 4, 6):
        copies["b", r] = (back_v.at[slot[r + 1] % 2], core_v.at[r // 2], chip(1))
    for side in range(2):
        copies["r", side] = (
            back_v.at[slot[6] % 2, pl.ds(side * half_rows, half_rows)],
            relay_v.at[side],
            chip(4 - 2 * side),
        )
    kept_grads = {0: grads_ref, 2: grads_x, 4: grads_y}
    for r, ref in kept_grads.items():
        copies["gc", r, 0] = (ref, all_grads.at[slot[r + 1]], chip(1))
    for h in range(2):
        part_h = pl.ds(h * half_rows, half_rows)
        via = 4 * h + 2 * (1 - h)
        copies["gd", h] = (kept_grads[via].at[part_h], all_grads.at[slot[6], part_h], chip(6 - via))
        copies["gc", 6, h] = (all_grads.at[slot[6], part_h], all_grads.at[slot[7], part_h], chip(1))
    number = {name: k for k, name in enumerate(copies)}

    def remote(*name):
        source, target, device = copies[name]
        return pltpu.make_async_remote_copy(
            source,
            target,
            send.at[number[name]],
            recv.at[number[name]],
            device_id=device,
            device_id_type=pl.DeviceIdType.MESH,
        )

    barrier = pltpu.get_barrier_semaphore()
    peers = [line(k) for k in range(1, parts)] + [chip(r) for r in (1, 2, 4)]
    for peer in peers:
        pl.semaphore_signal(barrier, inc=1, device_id=peer, device_id_type=pl.DeviceIdType.MESH)
    pl.semaphore_wait(barrier, len(peers))

    middle = inside(tp_index)
    outside = jnp.logical_not(middle)

    def rows_at(k):
        return pl.ds(pl.multiple_of((tp_index ^ k) * quarter, quarter), quarter)

    if summed:
        loads = [pltpu.make_async_copy(attn_hbm, rows_ref, local.at[0])]
    else:
        remote("n", 1).start()

        @pl.when(outside)
        def _():
            remote("nr").start()
            remote("n", 2).start()

        pl.when(middle)(remote("n", 3).start)
        loads = [
            pltpu.make_async_copy(source, line_out.at[k], local.at[k])
            for k, source in enumerate(
                (tokens_hbm, attn_hbm.at[rows_at(0)], attn_hbm.at[rows_at(2)])
            )
        ]
    for load in loads:
        load.start()
    for h in range(2):
        remote("gd", h).start()
    for r in kept_grads:
        remote("gc", r, 0).start()

    def spread(q):
        remote("x" if 2 * q < parts else "y", q).start()
        remote("c", 0, q).start()

    def spread_rest(q):
        remote("y" if 2 * q < parts else "x", q).start()

    hidden = down_hbm.shape[1]
    shared_rows = shared_down_hbm.shape[0]
    weights = [(shared_down_hbm, down_v.at[pl.ds(local_experts * padded, shared_rows)])]
    weights.append((router_hbm, wide_v.at[pl.ds(router_place, LANES)]))
    blanks = [(down_v, local_experts * padded + shared_rows, inner)]

    def load_part(source, count, place):
        weights.append((source, wide_v.at[pl.ds(place, count)]))
        blanks.append((wide_v, place + count, place + -(-count // LANES) * LANES))

    for e in range(local_experts):
        weights.append((down_hbm.at[e], down_v.at[pl.ds(e * padded, hidden)]))
        blanks.append((down_v, e * padded + hidden, (e + 1) * padded))
        load_part(gate_hbm.at[e], hidden, 2 * e * padded)
        load_part(up_hbm.at[e], hidden, (2 * e + 1) * padded)
    load_part(shared_gate_hbm, shared_rows, shared_place)
    load_part(shared_up_hbm, shared_rows, router_place + LANES)
    weight_copies = [
        pltpu.make_async_copy(source, target, weight_sem.at[k])
        for k, (source, target) in enumerate(weights)
    ]
    def load_rows(u):
        return pltpu.make_async_copy(all_rows.at[u], rows_v, local.at[6])

    for copy in weight_copies:
        copy.start()
    for ref, first, last in blanks:
        if last > first:
            ref[first:last] = jnp.zeros((last - first, D), BF16)

    def add_into(target, others):
        def chunk(i, _):
            total = None
            for ref, first in [target] + others:
                rows = pl.ds(pl.multiple_of(first + i * SUM_CHUNK, SUM_CHUNK), SUM_CHUNK)
                value = ref[rows].astype(F32)
                total = value if total is None else total + value
            ref, first = target
            ref[pl.ds(pl.multiple_of(first + i * SUM_CHUNK, SUM_CHUNK), SUM_CHUNK)] = total.astype(BF16)
            return 0

        return chunk

    def sum_rows(count, target, others):
        lax.fori_loop(0, count // SUM_CHUNK, add_into(target, others), 0)

    def arrived_x(q):
        remote("x", q).wait_recv()
        if 2 * q < parts:
            remote("d", q).start()
        remote("c", 2, q).start()

    def arrived_y(q):
        remote("y", q).wait_recv()
        if 2 * q >= parts:
            remote("d", q).start()
        remote("c", 4, q).start()

    def arrived_far(q):
        remote("d", q).wait_recv()
        remote("c", 6, q).start()

    half_parts = parts // 2

    def d_act_store(s, into):
        return pltpu.make_async_copy(d_act_v.at[into], d_act_hbm.at[s], d_act_sem.at[into])

    def d_act_load(u, into):
        return pltpu.make_async_copy(d_act_hbm.at[u], d_act_v.at[into], d_act_sem.at[into])

    for copy in weight_copies:
        copy.wait()

    def first_product(k, r):
        if r == 6:
            for h in range(2):
                remote("gd", h).wait_recv()
                remote("gc", 6, h).start()
        elif r % 2:
            for h in range(2 if r == 7 else 1):
                remote("gc", r - 1, h).wait_recv()
        source = kept_grads.get(r, all_grads.at[slot[r]])
        load = pltpu.make_async_copy(source, grads_v, local.at[5])
        load.start()
        if k >= 2:
            d_act_store(0, k % 2).wait()
        load.wait()
        keep = pltpu.make_async_copy(grads_v, all_grads.at[slot[r]], local.at[3])
        if r in kept_grads:
            keep.start()
        for first in range(0, inner, 512):
            columns = pl.ds(first, min(512, inner - first))
            d_act_v[k % 2, :, columns] = dot(grads_v[...], down_v[columns, :], NT)
        d_act_store(slot[r], k % 2).start()
        if r in kept_grads:
            keep.wait()

    for k in range(3):
        first_product(k, k)
    for load in loads:
        load.wait()
    if summed:
        residual_ref[...] = jnp.zeros_like(residual_ref)
        for k in range(3, 6):
            first_product(k, k)
    else:
        @pl.when(middle)
        def _():
            remote("nr").wait_recv()
            sum_rows(quarter, (line_out.at[2], 0), [(attn_relay, 0)])
            remote("nm").start()

        for k in range(3, 6):
            first_product(k, k)
        remote("n", 1).wait_recv()

        def normed(arrived):
            def step(i, _):
                rows = pl.ds(pl.multiple_of(i * SUM_CHUNK, SUM_CHUNK), SUM_CHUNK)
                value = line_out[1, rows].astype(F32)
                for k in arrived:
                    value = value + attn_in[k, rows].astype(F32)
                value = value + line_out[0, rows].astype(F32)
                residual_ref[rows] = value
                mean = jnp.sum(value * value, axis=1, keepdims=True) * (1.0 / D)
                rows_ref[rows] = (value * lax.rsqrt(mean + epsilon) * gain_ref[...]).astype(BF16)
                return 0

            lax.fori_loop(0, quarter // SUM_CHUNK, step, 0)

        @pl.when(outside)
        def _():
            remote("nm").wait_recv()
            normed((0, 1))

        @pl.when(middle)
        def _():
            remote("n", 2).wait_recv()
            remote("n", 3).wait_recv()
            normed((0, 1, 2))

    remote("z", 2).start()
    remote("z", 1).start()
    pl.when(middle)(remote("z", 3).start)
    own_copy = pltpu.make_async_copy(rows_ref, all_rows.at[slot[0], part(0)], local.at[0])
    own_copy.start()
    spread(0)
    first_product(6, 6)
    first_product(7, 7)
    remote("z", 1).wait_recv()
    spread(1)
    remote("z", 2).wait_recv()
    pl.when(middle)(remote("zr").start)
    spread(2)
    arrived_x(0)
    pl.when(middle)(remote("z", 3).wait_recv)
    pl.when(outside)(remote("zr").wait_recv)
    spread(3)
    arrived_x(1)
    own_copy.wait()
    load_rows(0).start()
    for k in range(2):
        d_act_store(0, k).wait()
    d_act_load(0, 0).start()

    def mask_loads(r):
        from_exp = (lax.rem(exp_index, GROUP) ^ r) * seq_len
        return [
            pltpu.make_async_copy(
                mask_hbm.at[pl.ds(pl.multiple_of(from_exp + (tp_index ^ q) * quarter, quarter), quarter)],
                mask_v.at[part(q)],
                mask_sem.at[q],
            )
            for q in range(parts)
        ]

    def act_store(u):
        into = u % 2
        return pltpu.make_async_copy(act_v.at[into], act_hbm.at[u], act_sem.at[into])

    def act_load(u):
        into = u % 2
        return pltpu.make_async_copy(act_hbm.at[u], act_v.at[into], act_sem.at[into])

    def wide_stores(u):
        return [
            pltpu.make_async_copy(
                wide_grad_v.at[:, pl.ds(0, first_part)], gate_grad_hbm.at[u], local.at[4]
            ),
            pltpu.make_async_copy(
                wide_grad_v.at[:, pl.ds(first_part, wide - first_part)], up_grad_hbm.at[u], local.at[7]
            ),
        ]

    def out_store(s):
        kept = out_odd if ORDER[s] % 2 else out_even
        return pltpu.make_async_copy(out_v.at[s % 2], kept.at[ORDER[s] // 2], out_sem.at[s % 2])

    def unit(u, _):
        into = lax.rem(u, 2)

        for s in range(GROUP):
            @pl.when(u == s)
            def _(s=s):
                for load in mask_loads(ORDER[s]):
                    load.start()

        load_rows(u).wait()
        for load in mask_loads(0):
            load.wait()

        d_act_load(u, into).wait()

        @pl.when(u > 1)
        def _():
            act_store(u - 2).wait()

        @pl.when(u > 0)
        def _():
            for store in wide_stores(u - 1):
                store.wait()

        linear = dot(rows_v[...], wide_v[shared_place:, :], NT)
        logits = linear[:, shared_padded : shared_padded + LANES]
        lane = lax.broadcasted_iota(jnp.int32, logits.shape, 1)
        logits = jnp.where(lane < experts_all, logits, -1e30)
        raised = jnp.exp(logits - jnp.max(logits, axis=1, keepdims=True))
        probs = raised / jnp.sum(raised, axis=1, keepdims=True)
        mask = mask_v[...].astype(F32)
        chosen = probs * mask
        chosen_sum = jnp.sum(chosen, axis=1, keepdims=True)
        probs_v[...] = probs
        gates_v[...] = chosen / chosen_sum

        def tile(linear, at_gate, at_up, place, j, gate):
            one = pl.ds(j * LANES, LANES)
            for first in range(0, seq_len, ROW_CHUNK):
                last = first + ROW_CHUNK
                gate_lin = linear[first:last, at_gate : at_gate + LANES]
                up_lin = linear[first:last, at_up : at_up + LANES]
                sigmoid = 0.5 * jnp.tanh(0.5 * gate_lin) + 0.5
                silu = gate_lin * sigmoid
                act = silu * up_lin
                d_act = d_act_v[into, first:last, one]
                if gate is not None:
                    total_v[first:last] += act * d_act
                    act = act * gate[first:last]
                    d_act = d_act * gate[first:last]
                act_v[into, first:last, one] = act.astype(BF16)
                d_up = d_act * silu
                d_gate = d_act * up_lin * (sigmoid + silu * (1.0 - sigmoid))
                wide_grad_v[first:last, pl.ds(place + at_gate, LANES)] = d_gate.astype(BF16)
                wide_grad_v[first:last, pl.ds(place + at_up, LANES)] = d_up.astype(BF16)

        for k in range(shared_tiles):
            at_up = shared_padded + LANES + k * LANES
            tile(linear, k * LANES, at_up, shared_place, local_experts * expert_tiles + k, None)
        d_gates = jnp.zeros(logits.shape, F32)
        for e in range(local_experts):
            mine = lane == exp_index * local_experts + e
            gate = jnp.sum(jnp.where(mine, gates_v[...], 0.0), axis=1, keepdims=True)
            total_v[...] = jnp.zeros(logits.shape, F32)
            place = 2 * e * padded
            linear = dot(rows_v[...], wide_v[place : place + 2 * padded, :], NT)
            for k in range(expert_tiles):
                tile(linear, k * LANES, padded + k * LANES, place, e * expert_tiles + k, gate)
            d_gates = jnp.where(mine, jnp.sum(total_v[...], axis=1, keepdims=True), d_gates)
        probs, gates, mask = probs_v[...], gates_v[...], mask_v[...].astype(F32)
        chosen_sum = jnp.sum(probs * mask, axis=1, keepdims=True)
        d_gates = d_gates * mask
        d_chosen = (d_gates - jnp.sum(d_gates * gates, axis=1, keepdims=True)) / chosen_sum
        d_probs = d_chosen * mask
        d_logits = probs * (d_probs - jnp.sum(d_probs * probs, axis=1, keepdims=True))
        high = d_logits.astype(BF16)
        low = pltpu.roll(d_logits - high.astype(F32), experts_all, 1)
        wide_grad_v[:, pl.ds(router_place, LANES)] = jnp.where(
            lane < experts_all, high.astype(F32), low
        ).astype(BF16)
        act_store(u).start()
        for store in wide_stores(u):
            store.start()

        @pl.when(u < GROUP - 1)
        def _():
            d_act_load(u + 1, 1 - into).start()

        @pl.when(u == 0)
        def _():
            for q in range(half_parts, parts):
                arrived_y(q)
            for q in range(parts):
                spread_rest(q)

        @pl.when(u == 1)
        def _():
            for q in range(half_parts):
                arrived_far(q)

        @pl.when(u == 3)
        def _():
            for q in range(half_parts, parts):
                arrived_x(q)

        @pl.when(u == 4)
        def _():
            for q in range(half_parts):
                arrived_y(q)

        @pl.when(u == 3)
        def _():
            remote("b", 0).wait_send()

        @pl.when(u == 4)
        def _():
            remote("b", 6).wait_send()

        @pl.when(u == 5)
        def _():
            remote("r", 0).wait_send()
            remote("r", 1).wait_send()

        @pl.when(u == 6)
        def _():
            remote("b", 2).wait_send()

        @pl.when(u == 7)
        def _():
            for q in range(parts):
                remote("s", 2, q).wait_send()

        back = back_v.at[into]

        def back_step(n, _):
            columns = pl.ds(pl.multiple_of(n * 512, 512), 512)
            back[:, columns] = dot(wide_grad_v[...], wide_v[:, columns], NN).astype(BF16)
            return 0

        lax.fori_loop(0, D // 512, back_step, 0)

        @pl.when(u == 0)
        def _():
            own_v[...] = back_v[0]

        @pl.when(u == slot[1])
        def _():
            remote("b", 0).start()

        @pl.when(u == slot[7])
        def _():
            remote("b", 6).start()

        @pl.when(u == slot[6])
        def _():
            remote("b", 6).wait_recv()
            sum_rows(seq_len, (back_v.at[slot[6] % 2], 0), [(core_v.at[3], 0)])
            remote("r", 0).start()
            remote("r", 1).start()

        @pl.when(u == slot[3])
        def _():
            remote("b", 2).start()

        @pl.when(u == slot[2])
        def _():
            remote("b", 2).wait_recv()
            remote("r", 0).wait_recv()
            mine = back_v.at[slot[2] % 2]
            sum_rows(half_rows, (mine, 0), [(core_v.at[1], 0), (relay_v.at[0], 0)])
            sum_rows(half_rows, (mine, half_rows), [(core_v.at[1], half_rows)])
            for q in range(parts):
                remote("s", 2, q).start()

        @pl.when(u == slot[5])
        def _():
            remote("b", 4).start()

        @pl.when(u == slot[4])
        def _():
            remote("b", 4).wait_recv()
            remote("r", 1).wait_recv()
            mine = back_v.at[slot[4] % 2]
            sum_rows(half_rows, (mine, half_rows), [(core_v.at[2], half_rows), (relay_v.at[1], 0)])
            sum_rows(half_rows, (mine, 0), [(core_v.at[2], 0)])
            for q in range(parts - 1, -1, -1):
                remote("s", 4, q).start()

        for k, r in ((0, 0), (1, 6), (3, 2), (5, 4)):
            @pl.when(u == k)
            def _(k=k, r=r):
                if k == 1:
                    for q in range(half_parts, parts):
                        arrived_far(q)
                for q in range(parts):
                    remote("c", r, q).wait_recv()

        @pl.when(u < GROUP - 1)
        def _():
            load_rows(u + 1).start()

        return 0

    lax.fori_loop(0, GROUP, unit, 0)

    remote("b", 0).wait_recv()

    def finish(q):
        remote("s", 2, q).wait_recv()
        remote("s", 4, q).wait_recv()
        first = q * quarter
        sources = [(own_v, first), (core_v.at[0], first), (cross_v.at[0], first), (cross_v.at[1], first)]

        def total_step(i, _):
            total = None
            for ref, start in sources:
                rows = pl.ds(pl.multiple_of(start + i * SUM_CHUNK, SUM_CHUNK), SUM_CHUNK)
                value = ref[rows].astype(F32)
                total = value if total is None else total + value
            rows = pl.ds(pl.multiple_of(i * SUM_CHUNK, SUM_CHUNK), SUM_CHUNK)
            if q == 0:
                back_ref[rows] = total
            else:
                line_out[q - 1, rows] = total.astype(BF16)
            return 0

        lax.fori_loop(0, quarter // SUM_CHUNK, total_step, 0)
        if q:
            remote("t", q).start()

    if not summed:
        pl.when(middle)(remote("nm").wait_send)

    for u in (GROUP - 2, GROUP - 1):
        act_store(u).wait()
    for store in wide_stores(GROUP - 1):
        store.wait()
    act_load(0).start()

    def out_unit(u, _):
        into = lax.rem(u, 2)

        @pl.when(u < GROUP - 1)
        def _():
            act_load(u + 1).start()

        act_load(u).wait()
        for s in range(2, GROUP):
            @pl.when(u == s)
            def _(s=s):
                out_store(s - 2).wait()

        def out_step(n, _):
            columns = pl.ds(pl.multiple_of(n * 512, 512), 512)
            out_v[into, :, columns] = dot(act_v[into], down_v[:, columns], NN).astype(BF16)
            return 0

        lax.fori_loop(0, D // 512, out_step, 0)
        for s in range(GROUP):
            @pl.when(u == s)
            def _(s=s):
                out_store(s).start()

        for q in range(1, parts):
            @pl.when(u == GROUP - 1 - 2 * (q - 1))
            def _(q=q):
                finish(q)

        return 0

    lax.fori_loop(0, GROUP, out_unit, 0)
    finish(0)
    for s in (GROUP - 2, GROUP - 1):
        out_store(s).wait()
    for k in range(parts - 1, 0, -1):
        remote("t", k).wait_recv()

    def last_step(i, _):
        rows = pl.ds(pl.multiple_of(i * ROW_CHUNK, ROW_CHUNK), ROW_CHUNK)
        total = back_ref[rows]
        for k in range(1, parts):
            total = total + line_in[k - 1, rows].astype(F32)
        back_ref[rows] = total
        return 0

    lax.fori_loop(0, quarter // ROW_CHUNK, last_step, 0)


    @pl.when(middle)
    def _():
        remote("z", 3).wait_send()
        remote("zr").wait_send()
        if not summed:
            remote("n", 3).wait_send()

    if not summed:
        @pl.when(outside)
        def _():
            remote("n", 2).wait_send()
            remote("nr").wait_send()

    waited = [("b", 0), ("b", 6), ("r", 0), ("r", 1), ("b", 2)] + [("s", 2, q) for q in range(parts)]
    waited += [("z", 3), ("zr",), ("n", 2), ("n", 3), ("nr",), ("nm",)]
    for name in copies:
        if name not in waited:
            remote(*name).wait_send()


def expert_layer(attn, tokens, gain, grads, mask, weights, sizes):
    parts, _, local_experts, expert_tiles, shared_tiles, summed = sizes
    quarter = tokens.shape[0]
    seq_len = parts * quarter
    inner = (local_experts * expert_tiles + shared_tiles) * LANES
    wide = 2 * inner + LANES
    first_part = 2 * expert_tiles * LANES
    loads = 4 + 3 * local_experts
    copies = 3 * (parts - 1) + 9 * parts + 6 + 7 + 3
    hbm = pl.BlockSpec(memory_space=pl.ANY)
    every = jax.ShapeDtypeStruct((GROUP, seq_len, D), BF16)
    some = jax.ShapeDtypeStruct((GROUP // 2, seq_len, D), BF16)
    flops = 2 * GROUP * seq_len * D * (2 * wide + 2 * inner)
    return pl.pallas_call(
        functools.partial(expert_kernel, sizes),
        out_shape=(
            every,
            every,
            jax.ShapeDtypeStruct((GROUP, seq_len, inner), BF16),
            jax.ShapeDtypeStruct((GROUP, seq_len, first_part), BF16),
            jax.ShapeDtypeStruct((GROUP, seq_len, wide - first_part), BF16),
            some,
            some,
            jax.ShapeDtypeStruct((GROUP, seq_len, inner), F32),
            jax.ShapeDtypeStruct((quarter, D), F32),
            jax.ShapeDtypeStruct((quarter, D), BF16),
            jax.ShapeDtypeStruct((quarter, D), F32),
        ),
        in_specs=[hbm] * 2 + [pl.BlockSpec(memory_space=pltpu.VMEM)] + [hbm] * (4 + len(weights)),
        out_specs=(hbm,) * 8 + (pl.BlockSpec(memory_space=pltpu.VMEM),) * 3,
        scratch_shapes=[
            pltpu.VMEM((wide, D), BF16),
            pltpu.VMEM((inner, D), BF16),
            pltpu.VMEM((seq_len, D), BF16),
            pltpu.VMEM((seq_len, D), BF16),
            pltpu.VMEM((seq_len, LANES), BF16),
            pltpu.VMEM((2, seq_len, inner), F32),
            pltpu.VMEM((2, seq_len, inner), BF16),
            pltpu.VMEM((seq_len, wide), BF16),
            pltpu.VMEM((seq_len, LANES), F32),
            pltpu.VMEM((seq_len, LANES), F32),
            pltpu.VMEM((seq_len, LANES), F32),
            pltpu.VMEM((2, seq_len, D), BF16),
            pltpu.VMEM((2, seq_len, D), BF16),
            pltpu.VMEM((seq_len, D), BF16),
            pltpu.VMEM((GROUP // 2, seq_len, D), BF16),
            pltpu.VMEM((2, seq_len // 2, D), BF16),
            pltpu.VMEM((2, seq_len, D), BF16),
            pltpu.VMEM((parts - 1, quarter, D), BF16),
            pltpu.VMEM((parts - 1, quarter, D), BF16),
            pltpu.VMEM((parts - 1, quarter, D), BF16),
            pltpu.VMEM((quarter, D), BF16),
            pltpu.SemaphoreType.DMA((copies,)),
            pltpu.SemaphoreType.DMA((copies,)),
            pltpu.SemaphoreType.DMA((10,)),
            pltpu.SemaphoreType.DMA((loads,)),
            pltpu.SemaphoreType.DMA((parts,)),
            pltpu.SemaphoreType.DMA((2,)),
            pltpu.SemaphoreType.DMA((2,)),
            pltpu.SemaphoreType.DMA((2,)),
        ],
        compiler_params=pltpu.CompilerParams(
            collective_id=4 if summed else 1,
            has_side_effects=True,
            vmem_limit_bytes=60 * 1024 * 1024,
        ),
        cost_estimate=pl.CostEstimate(flops=flops, bytes_accessed=120_000_000, transcendentals=0),
        name="experts",
    )(attn, tokens, gain, *grads, mask, *weights)


def line_rows(own_rows):
    parts = lax.axis_size("tp")
    return jnp.concatenate([own_rows] + [swap(own_rows, "tp", k) for k in range(1, parts)], axis=0)


def add_cores(even, odd_swapped):
    return [(e.astype(F32) + o.astype(F32)).astype(BF16) for e, o in zip(even, odd_swapped)]


def far_halves(mine):
    half = mine[3].shape[0] // 2
    return swap(mine[3][:half], "exp", 4), swap(mine[3][half:], "exp", 2)


def near_sums(mine, far):
    half = mine[3].shape[0] // 2
    first = jnp.concatenate([mine[1][:half] + far[0], mine[1][half:]], axis=0)
    second = jnp.concatenate([mine[2][:half], mine[2][half:] + far[1]], axis=0)
    return swap(first, "exp", 2), swap(second, "exp", 4)


def chip_sums(mine, near):
    total = mine[0].astype(F32) + near[0].astype(F32) + near[1].astype(F32)
    total = total.reshape(lax.axis_size("tp"), -1, total.shape[1])
    return total[0], total.astype(BF16)


def line_sums(mine, near):
    result, low = chip_sums(mine, near)
    for k in range(1, low.shape[0]):
        result = result + swap(low[k], "tp", k).astype(F32)
    return result


def neighbours(parts):
    exp_index, tp_index = lax.axis_index("exp"), lax.axis_index("tp")
    line = [{"tp": tp_index ^ k} for k in range(1, parts)]
    return line, [{"exp": exp_index ^ r} for r in range(1, GROUP)]


def greet(peers):
    barrier = pltpu.get_barrier_semaphore()
    for peer in peers:
        pl.semaphore_signal(barrier, inc=1, device_id=peer, device_id_type=pl.DeviceIdType.MESH)
    pl.semaphore_wait(barrier, len(peers))


def remote_maker(copies, send, recv):
    number = {name: k for k, name in enumerate(copies)}

    def remote(*name):
        source, target, device = copies[name]
        return pltpu.make_async_remote_copy(
            source,
            target,
            send.at[number[name]],
            recv.at[number[name]],
            device_id=device,
            device_id_type=pl.DeviceIdType.MESH,
        )

    return remote


def inside(place):
    return (place == 1) | (place == 2)


def gather_kernel(parts, *refs):
    tokens_ref, grads_ref, proj_ref, narrow_ref, out_ref, mask_ref = refs[:6]
    gate_ref, up_ref, down_ref, tokens_all, grads_all, grads_x, grads_y = refs[6:13]
    proj_all, narrow_all, out_all, mask_all, gate_all, up_all, down_all = refs[13:20]
    send, recv, local, local_out = refs[20:24]
    staged = refs[24:]
    exp_index, tp_index = lax.axis_index("exp"), lax.axis_index("tp")
    line, near = neighbours(parts)
    quarter, depth, seq_len = tokens_ref.shape[0], proj_ref.shape[0], mask_ref.shape[0]
    width = down_ref.shape[2]

    def block(whole, size, r, axis=0):
        place = pl.ds(pl.multiple_of((exp_index ^ r) * size, size), size)
        return whole.at[place] if axis == 0 else whole.at[:, place]

    def arrays(r):
        return {
            "p": block(proj_all, depth, r),
            "n": block(narrow_all, narrow_ref.shape[1], r, 1),
            "o": block(out_all, out_ref.shape[1], r, 1),
            "m": block(mask_all, seq_len, r),
        }

    own = {"p": proj_ref, "n": narrow_ref, "o": out_ref, "m": mask_ref}
    my_rows = pl.ds(pl.multiple_of(tp_index * quarter, quarter), quarter)
    copies = {}
    for k in range(1, parts):
        copies["z", 0, k] = (tokens_ref, tokens_all.at[my_rows], line[k - 1])
        copies["z", 1, k] = (grads_ref, grads_all.at[pl.ds(k * quarter, quarter)], line[k - 1])
    passed = pl.ds(pl.multiple_of((tp_index ^ 2) * quarter, quarter), quarter)
    copies["zr", 0] = (tokens_all.at[passed], tokens_all.at[passed], line[0])
    copies["zr", 1] = (
        grads_all.at[pl.ds(2 * quarter, quarter)],
        grads_all.at[pl.ds(3 * quarter, quarter)],
        line[0],
    )
    for q in range(parts):
        rows = pl.ds(q * quarter, quarter)
        held = grads_ref if q == 0 else grads_all.at[rows]
        copies["x", q] = (held, grads_x.at[rows], near[1])
        copies["y", q] = (held, grads_y.at[rows], near[3])
    for key, ref in own.items():
        mine = arrays(0)[key]
        copies["g", 2, key] = (ref, mine, near[1])
        copies["g", 4, key] = (ref, mine, near[3])
        via = 2 if key in "pn" else 4
        passed = arrays(via)[key]
        copies["g", 6, key] = (passed, passed, near[5 - via])
        copies["c", 0, key] = (ref, mine, near[0])
        for r in (2, 4, 6):
            copies["c", r, key] = (arrays(r)[key], arrays(r)[key], near[0])
    for r in range(1, GROUP):
        to = exp_index ^ r
        copies["a", r, 0] = (gate_ref.at[to], block(gate_all, width, 0, 1), near[r - 1])
        copies["a", r, 1] = (up_ref.at[to], block(up_all, width, 0, 1), near[r - 1])
        copies["a", r, 2] = (down_ref.at[to], block(down_all, width, 0, 1), near[r - 1])
    remote = remote_maker(copies, send, recv)

    greet(line + near)
    for kind in range(2):
        remote("z", kind, 2).start()
        remote("z", kind, 1).start()
        pl.when(inside(tp_index))(remote("z", kind, 3).start)
    for key in own:
        for r in (2, 4):
            remote("g", r, key).start()
        remote("c", 0, key).start()
    remote("x", 0).start()
    remote("y", 0).start()
    kept = [
        (tokens_ref, tokens_all.at[my_rows]),
        (grads_ref, grads_all.at[pl.ds(0, quarter)]),
        (proj_ref, arrays(0)["p"]),
        (narrow_ref, arrays(0)["n"]),
        (out_ref, arrays(0)["o"]),
        (mask_ref, arrays(0)["m"]),
        (gate_ref.at[exp_index], block(gate_all, width, 0, 1)),
        (up_ref.at[exp_index], block(up_all, width, 0, 1)),
        (down_ref.at[exp_index], block(down_all, width, 0, 1)),
    ]
    for k, (source, _) in enumerate(kept):
        pltpu.make_async_copy(source, staged[k], local.at[k]).start()
    for k, (source, target) in enumerate(kept):
        pltpu.make_async_copy(source, staged[k], local.at[k]).wait()
        pltpu.make_async_copy(staged[k], target, local_out.at[k]).start()
    kept = [
        pltpu.make_async_copy(staged[k], target, local_out.at[k])
        for k, (_, target) in enumerate(kept)
    ]
    for key in own:
        for r in (2, 4):
            remote("g", r, key).wait_recv()
            if r == (2 if key in "pn" else 4):
                remote("g", 6, key).start()
            remote("c", r, key).start()
    for r in range(1, GROUP):
        for k in range(3):
            remote("a", r, k).start()
    for kind in range(2):
        remote("z", kind, 2).wait_recv()
        pl.when(inside(tp_index))(remote("zr", kind).start)
    remote("z", 1, 1).wait_recv()
    for q in (2, 1):
        remote("x", q).start()
        remote("y", q).start()
    for key in own:
        remote("g", 6, key).wait_recv()
        remote("c", 6, key).start()
    for copy in kept:
        copy.wait()
    for name in copies:
        if name[0] in "ca":
            remote(*name).wait_recv()
    remote("z", 0, 1).wait_recv()
    for kind in (1, 0):
        @pl.when(inside(tp_index))
        def _(kind=kind):
            remote("z", kind, 3).wait_recv()
            remote("z", kind, 3).wait_send()
            remote("zr", kind).wait_send()

        pl.when(jnp.logical_not(inside(tp_index)))(remote("zr", kind).wait_recv)
        if kind == 1:
            remote("x", 3).start()
            remote("y", 3).start()
        for k in (1, 2):
            remote("z", kind, k).wait_send()
    for name in copies:
        if name[0] in "xy":
            remote(*name).wait_recv()
    for name in copies:
        if name[0] not in ("z", "zr"):
            remote(*name).wait_send()


def gather_inputs(tokens, grads, proj, narrow, out, mask, gate, up, down):
    parts = lax.axis_size("tp")
    hbm = pl.BlockSpec(memory_space=pl.ANY)
    depth, seq_len = proj.shape[0], mask.shape[0]
    shapes = [
        *((parts * tokens.shape[0], D) for _ in range(4)),
        (GROUP * depth, proj.shape[1]),
        (narrow.shape[0], GROUP * narrow.shape[1]),
        (out.shape[0], GROUP * out.shape[1]),
        (GROUP * seq_len, LANES),
        *((w.shape[1], GROUP * w.shape[2]) for w in (gate, up, down)),
    ]
    copies = 4 * parts + 4 * 7 + 3 * (GROUP - 1)
    return pl.pallas_call(
        functools.partial(gather_kernel, parts),
        out_shape=tuple(jax.ShapeDtypeStruct(s, BF16) for s in shapes),
        in_specs=[hbm] * 9,
        out_specs=(hbm,) * 11,
        scratch_shapes=[
            pltpu.SemaphoreType.DMA((copies,)),
            pltpu.SemaphoreType.DMA((copies,)),
            pltpu.SemaphoreType.DMA((9,)),
            pltpu.SemaphoreType.DMA((9,)),
            *(
                pltpu.VMEM(x.shape[-2:], BF16)
                for x in (tokens, grads, proj, narrow, out, mask, gate, up, down)
            ),
        ],
        compiler_params=pltpu.CompilerParams(
            collective_id=2, has_side_effects=True, vmem_limit_bytes=16 * 1024 * 1024
        ),
        name="gather_inputs",
    )(tokens, grads, proj, narrow, out, mask, gate, up, down)


def scatter_kernel(parts, *refs):
    proj_ref, out_ref, mine_ref, line_ref, gate_ref, up_ref, down_ref = refs[:7]
    proj_sum, out_sum, output_ref, gate_back, up_back, down_back = refs[7:13]
    proj_core, out_core, proj_add, out_add, proj_relay, out_relay = refs[13:19]
    proj_cross, out_cross, narrow, narrow_in, line_in, send, recv, local = refs[19:]
    exp_index = lax.axis_index("exp")
    line, near = neighbours(parts)
    depth, width = proj_sum.shape[0], out_sum.shape[1]

    def proj_block(r):
        return proj_ref.at[pl.ds(pl.multiple_of((exp_index ^ r) * depth, depth), depth)]

    def out_block(r):
        return out_ref.at[:, pl.ds(pl.multiple_of((exp_index ^ r) * width, width), width)]

    copies = {}
    for r in (6, 2, 4, 0):
        copies["c", r, 0] = (proj_block(r + 1), proj_core.at[r // 2], near[0])
        copies["c", r, 1] = (out_block(r + 1), out_core.at[r // 2], near[0])
    copies["d", 0] = (proj_add.at[2], proj_relay, near[3])
    copies["d", 1] = (out_add.at[2], out_relay, near[1])
    for side, r in enumerate((2, 4)):
        copies["s", r, 0] = (proj_add.at[side], proj_cross.at[side], near[r - 1])
        copies["s", r, 1] = (out_add.at[side], out_cross.at[side], near[r - 1])
    for k in range(1, parts):
        copies["z", k] = (narrow, narrow_in.at[k - 1], line[k - 1])
        copies["t", k] = (line_ref.at[k], line_in.at[k - 1], line[k - 1])
    for r in range(1, GROUP):
        to = exp_index ^ r
        copies["a", r, 0] = (gate_ref.at[to], gate_back.at[exp_index], near[r - 1])
        copies["a", r, 1] = (up_ref.at[to], up_back.at[exp_index], near[r - 1])
        copies["a", r, 2] = (down_ref.at[to], down_back.at[exp_index], near[r - 1])
    remote = remote_maker(copies, send, recv)

    def total(target, sources):
        count = target.shape[0]

        def chunk(i, _):
            rows = pl.ds(pl.multiple_of(i * 32, 32), 32)
            value = sum(ref[rows].astype(F32) for ref in sources[1:])
            target[rows] = (sources[0][rows].astype(F32) + value).astype(target.dtype)
            return 0

        lax.fori_loop(0, count // 32, chunk, 0)

    greet(line + near)
    for k in range(1, parts):
        remote("t", k).start()
    for r in (6, 2, 4, 0):
        for k in range(2):
            remote("c", r, k).start()
    for k in range(2):
        remote("c", 6, k).wait_recv()
    total(proj_add.at[2], [proj_block(6), proj_core.at[3]])
    remote("d", 0).start()
    total(out_add.at[2], [out_block(6), out_core.at[3]])
    remote("d", 1).start()
    for r in (2, 4):
        for k in range(2):
            remote("c", r, k).wait_recv()
    total(out_add.at[0], [out_block(2), out_core.at[1]])
    remote("s", 2, 1).start()
    total(proj_add.at[1], [proj_block(4), proj_core.at[2]])
    remote("s", 4, 0).start()
    remote("d", 0).wait_recv()
    total(proj_add.at[0], [proj_block(2), proj_core.at[1], proj_relay])
    remote("s", 2, 0).start()
    remote("d", 1).wait_recv()
    total(out_add.at[1], [out_block(4), out_core.at[2], out_relay])
    remote("s", 4, 1).start()
    for r in range(1, GROUP):
        for k in range(3):
            remote("a", r, k).start()
    kept = [
        pltpu.make_async_copy(source.at[exp_index], target.at[exp_index], local.at[k])
        for k, (source, target) in enumerate(
            ((gate_ref, gate_back), (up_ref, up_back), (down_ref, down_back))
        )
    ]
    for copy in kept:
        copy.start()
    for k in range(2):
        remote("c", 0, k).wait_recv()
        for r in (2, 4):
            remote("s", r, k).wait_recv()
        if k == 0:
            total(proj_sum, [proj_block(0), proj_core.at[0], proj_cross.at[0], proj_cross.at[1]])
            narrow[...] = proj_sum[:, proj_sum.shape[1] - LANES :]
            for j in range(1, parts):
                remote("z", j).start()
        else:
            total(out_sum, [out_block(0), out_core.at[0], out_cross.at[0], out_cross.at[1]])
    for j in range(1, parts):
        remote("z", j).wait_recv()
    value = narrow[...]
    for j in range(1, parts):
        value = value + narrow_in[j - 1]
    proj_sum[:, proj_sum.shape[1] - LANES :] = value
    for j in range(1, parts):
        remote("t", j).wait_recv()
    total(output_ref, [mine_ref] + [line_in.at[j - 1] for j in range(1, parts)])
    for copy in kept:
        copy.wait()
    for r in range(1, GROUP):
        for k in range(3):
            remote("a", r, k).wait_recv()
    for name in copies:
        remote(*name).wait_send()


def scatter_grads(proj, out, mine, line, gate, up, down):
    parts = lax.axis_size("tp")
    hbm, vmem = pl.BlockSpec(memory_space=pl.ANY), pl.BlockSpec(memory_space=pltpu.VMEM)
    one = (proj.shape[0] // GROUP, proj.shape[1])
    two = (out.shape[0], out.shape[1] // GROUP)
    narrow = (one[0], LANES)
    copies = 8 + 2 + 4 + 2 * (parts - 1) + 3 * (GROUP - 1)
    return pl.pallas_call(
        functools.partial(scatter_kernel, parts),
        out_shape=(
            jax.ShapeDtypeStruct(one, F32),
            jax.ShapeDtypeStruct(two, F32),
            jax.ShapeDtypeStruct(mine.shape, BF16),
            *(jax.ShapeDtypeStruct(x.shape, x.dtype) for x in (gate, up, down)),
        ),
        in_specs=[vmem] * 3 + [hbm] * 4,
        out_specs=(vmem, vmem, vmem, hbm, hbm, hbm),
        scratch_shapes=[
            pltpu.VMEM((GROUP // 2, *one), BF16),
            pltpu.VMEM((GROUP // 2, *two), BF16),
            pltpu.VMEM((3, *one), BF16),
            pltpu.VMEM((3, *two), BF16),
            pltpu.VMEM(one, BF16),
            pltpu.VMEM(two, BF16),
            pltpu.VMEM((2, *one), BF16),
            pltpu.VMEM((2, *two), BF16),
            pltpu.VMEM(narrow, F32),
            pltpu.VMEM((parts - 1, *narrow), F32),
            pltpu.VMEM((parts - 1, *mine.shape), BF16),
            pltpu.SemaphoreType.DMA((copies,)),
            pltpu.SemaphoreType.DMA((copies,)),
            pltpu.SemaphoreType.DMA((3,)),
        ],
        compiler_params=pltpu.CompilerParams(
            collective_id=3, has_side_effects=True, vmem_limit_bytes=40 * 1024 * 1024
        ),
        name="scatter_grads",
    )(proj, out, mine, line, gate, up, down)


def cut_kernel(moves, *refs):
    sources, targets, held, sem_in, sem_out = refs[:3], refs[3:6], *refs[6:]

    def load(k):
        s, first, t, _ = moves[k]
        rows = pl.ds(first, targets[t].shape[1])
        return pltpu.make_async_copy(sources[s].at[rows], held.at[k], sem_in.at[k])

    def store(k):
        _, _, t, e = moves[k]
        return pltpu.make_async_copy(held.at[k], targets[t].at[e], sem_out.at[k])

    for k in range(len(moves)):
        load(k).start()
    for k in range(len(moves)):
        load(k).wait()
        store(k).start()
    for k in range(len(moves)):
        store(k).wait()


def cut_experts(moves, sums, count, hidden):
    hbm = pl.BlockSpec(memory_space=pl.ANY)
    shape = (count, hidden, D)
    return pl.pallas_call(
        functools.partial(cut_kernel, moves),
        out_shape=(jax.ShapeDtypeStruct(shape, F32),) * 3,
        in_specs=[hbm] * 3,
        out_specs=(hbm,) * 3,
        scratch_shapes=[
            pltpu.VMEM((len(moves), hidden, D), F32),
            pltpu.SemaphoreType.DMA((len(moves),)),
            pltpu.SemaphoreType.DMA((len(moves),)),
        ],
        compiler_params=pltpu.CompilerParams(vmem_limit_bytes=24 * 1024 * 1024),
        cost_estimate=pl.CostEstimate(flops=0, bytes_accessed=35_000_000, transcendentals=0),
        name="cut_experts",
    )(*sums)


def pad_to(value, axis, multiple):
    widths = [(0, 0)] * value.ndim
    widths[axis] = (0, -value.shape[axis] % multiple)
    return jnp.pad(value, widths)


def shards(
    tokens,
    cotangent,
    segment_ids,
    routes,
    norm1_gain,
    attn_q,
    attn_k,
    attn_v,
    attn_o,
    norm2_gain,
    router,
    shared_gate,
    shared_up,
    shared_down,
    expert_gate,
    expert_up,
    expert_down,
):
    exp_count = lax.axis_size("exp")
    tp_count = lax.axis_size("tp")
    exp_index = lax.axis_index("exp")
    tp_index = lax.axis_index("tp")
    quarter = tokens.shape[0]
    seq_len = quarter * tp_count

    experts_all = router.shape[1]
    local_experts, _, hidden = expert_gate.shape
    shared_hidden = shared_gate.shape[1] // exp_count
    in_group = exp_count == GROUP
    qkv_widths = (attn_q.shape[1], attn_k.shape[1], attn_v.shape[1])
    gains = jnp.stack([norm1_gain, norm2_gain], axis=0)
    proj = jnp.concatenate([attn_q, attn_k, attn_v], axis=1)
    qkv_width = sum(qkv_widths)
    narrow_weight = pad_to(jnp.concatenate([router.T, gains], axis=0), 0, 16)
    member_lanes = jnp.any(
        routes[:, :, None] == jnp.arange(LANES, dtype=jnp.int32), axis=1
    ).astype(BF16)

    def cut(weight):
        return pad_to(weight.reshape(exp_count, shared_hidden, -1), 1, 16)

    cut_gate, cut_up, cut_down = cut(shared_gate.T), cut(shared_up.T), cut(shared_down)
    if in_group:
        (
            whole,
            own_grads,
            *near_grads,
            qkv_weight,
            narrow_weight,
            output_weight,
            all_masks,
            my_gate,
            my_up,
            my_down,
        ) = gather_inputs(
            tokens, cotangent, proj, narrow_weight, attn_o, member_lanes, cut_gate, cut_up, cut_down
        )
    else:
        whole = lax.all_gather(tokens, "tp", axis=0, tiled=True)
        own_grads = line_rows(cotangent)
        near_grads = [swap(own_grads, "exp", 2), swap(own_grads, "exp", 4)]
        qkv_weight = lax.all_gather(proj, "exp", axis=0, tiled=True)
        narrow_weight = lax.all_gather(narrow_weight, "exp", axis=1, tiled=True)
        output_weight = lax.all_gather(attn_o, "exp", axis=1, tiled=True)
        all_masks = lax.all_gather(member_lanes, "exp", axis=0, tiled=True)
        my_gate, my_up, my_down = (
            lax.all_to_all(w, "exp", split_axis=0, concat_axis=2, tiled=True)
            for w in (cut_gate, cut_up, cut_down)
        )
        my_gate, my_up, my_down = my_gate[0], my_up[0], my_down[0]
    first_norm_scale = narrow_weight[experts_all].astype(F32)
    second_norm_scale = narrow_weight[experts_all + 1].astype(F32)
    own_tokens = tokens.astype(F32)
    whole = whole.astype(F32)
    scale_one = lax.rsqrt(jnp.mean(whole * whole, axis=-1, keepdims=True) + epsilon)
    normed_one = (whole * scale_one * first_norm_scale).astype(BF16)
    heads_dev = qkv_widths[0] // HEAD_DIM
    kv_dev = qkv_widths[1] // HEAD_DIM
    group_size = heads_dev // kv_dev
    score_scale = HEAD_DIM ** (-0.5)
    cosine, sine = rotary_tables(seq_len, HEAD_DIM)
    qkv_lin = dot(normed_one, qkv_weight, NN).reshape(seq_len, -1, HEAD_DIM)
    turned = rotate(qkv_lin[:, : heads_dev + kv_dev], cosine, sine).astype(BF16)
    queries = turned[:, :heads_dev].reshape(seq_len, kv_dev, group_size, HEAD_DIM)
    keys_rot = turned[:, heads_dev:]
    values = qkv_lin[:, heads_dev + kv_dev :].astype(BF16)
    positions = jnp.arange(seq_len, dtype=jnp.int32)
    allowed = (positions[None, :] <= positions[:, None]) & (
        segment_ids[:, None] == segment_ids[None, :]
    )
    raw_scores = jnp.einsum("qkgd,ckd->kgqc", queries, keys_rot, preferred_element_type=F32)
    scores = jnp.where(allowed, raw_scores * score_scale, -1e30)
    exponent = jnp.exp(scores - jnp.max(scores, axis=-1, keepdims=True))
    probs = exponent / jnp.sum(exponent, axis=-1, keepdims=True)
    probs_low = probs.astype(BF16)
    attended = jnp.einsum("kgqc,ckd->qkgd", probs_low, values, preferred_element_type=F32)
    attended = attended.reshape(seq_len, heads_dev * HEAD_DIM).astype(BF16)
    attn_part = dot(attended, output_weight, NN).astype(BF16)

    expert_tiles, shared_tiles = -(-hidden // LANES), -(-my_gate.shape[0] // LANES)
    router_rows = narrow_weight[:experts_all]
    router_pad = jnp.zeros((LANES - 2 * experts_all, D), BF16)
    weights = (
        expert_gate.transpose(0, 2, 1),
        expert_up.transpose(0, 2, 1),
        expert_down,
        my_gate,
        my_up,
        my_down,
        jnp.concatenate([router_rows, router_rows, router_pad], axis=0),
    )
    inner = (local_experts * expert_tiles + shared_tiles) * LANES
    sizes = (tp_count, experts_all, local_experts, expert_tiles, shared_tiles)
    gain_row = second_norm_scale[None, :]
    all_masks = all_masks.reshape(exp_count // GROUP, -1, LANES)

    d_normed_two, rest_sum, first_sum, down_sum = 0.0, 0.0, 0.0, 0.0
    for base in range(0, exp_count, GROUP):
        rows_b, grads_b = attn_part, (own_grads, *near_grads)
        if base:
            rows_b = swap(normed_two, "exp", base)
            grads_b = [swap(own_grads, "exp", base ^ r) for r in (0, 2, 4)]
        masks = lax.dynamic_index_in_dim(
            all_masks, (exp_index // GROUP) ^ (base // GROUP), keepdims=False
        )
        *results, back, rows_b, residual_b = expert_layer(
            rows_b, tokens, gain_row, grads_b, masks, weights, (*sizes, base > 0)
        )
        all_rows, all_grads, act, first_grads, rest_grads, out_even, out_odd, _ = results
        if not base:
            normed_two, residual = rows_b, residual_b
            output = residual
        swapped = swap(out_odd, "exp", 1)
        d_normed_two = d_normed_two + (swap(back, "exp", base) if base else back)
        count = GROUP * seq_len
        grads_seen, act = all_grads.reshape(count, D), act.reshape(count, -1)
        rows_seen = all_rows.reshape(count, D)
        rest_grads, first_grads = rest_grads.reshape(count, -1), first_grads.reshape(count, -1)
        if base + GROUP < exp_count:
            rest_sum = rest_sum + dot(rest_grads, rows_seen, TN)
            first_sum = first_sum + dot(first_grads, rows_seen, TN)
            down_sum = down_sum + dot(act, grads_seen, TN)
            mine = add_cores(out_even, swapped)
            part_out = line_sums(mine, near_sums(mine, far_halves(mine)))
            output = output + (swap(part_out, "exp", base) if base else part_out)
            own_grads, normed_two, rest_sum, first_sum, down_sum, output = lax.optimization_barrier(
                (own_grads, normed_two, rest_sum, first_sum, down_sum, output)
            )
    down_sum = down_sum + dot(act, grads_seen, TN)
    swapped, down_sum = lax.optimization_barrier((swapped, down_sum))

    scale_two = lax.rsqrt(jnp.mean(residual * residual, axis=-1, keepdims=True) + epsilon)
    grad_gain_two, d_residual = norm_back(d_normed_two, residual, scale_two, second_norm_scale)
    d_residual = cotangent.astype(F32) + d_residual

    d_attn_low = lax.all_gather(d_residual.astype(BF16), "tp", axis=0, tiled=True)
    mine = add_cores(out_even, swapped)
    mine, first_grads = lax.optimization_barrier((mine, first_grads))
    first_sum = first_sum + dot(first_grads, rows_seen, TN)
    d_attn_low, first_sum, *far = lax.optimization_barrier((d_attn_low, first_sum, *far_halves(mine)))
    near = near_sums(mine, far)
    grad_out_w = dot(attended, d_attn_low, TN)
    d_attended = dot(d_attn_low, output_weight, NT).astype(BF16)
    d_attended = d_attended.reshape(seq_len, kv_dev, group_size, HEAD_DIM)
    d_probs_att = jnp.einsum("qkgd,ckd->kgqc", d_attended, values, preferred_element_type=F32)
    row_inner = jnp.sum(d_probs_att * probs, axis=-1, keepdims=True)
    d_raw = (probs * (d_probs_att - row_inner) * score_scale).astype(BF16)
    d_query = jnp.einsum("kgqc,ckd->qkgd", d_raw, keys_rot, preferred_element_type=F32).reshape(
        seq_len, heads_dev, HEAD_DIM
    )
    d_key = jnp.einsum("kgqc,qkgd->ckd", d_raw, queries, preferred_element_type=F32)
    d_value = jnp.einsum("kgqc,qkgd->ckd", probs_low, d_attended, preferred_element_type=F32)
    d_qkv = jnp.concatenate(
        [
            rotate_back(jnp.concatenate([d_query, d_key], axis=1), cosine, sine).astype(BF16),
            d_value.astype(BF16),
        ],
        axis=1,
    ).reshape(seq_len, -1)
    d_normed_one = dot(d_qkv, qkv_weight, NT).astype(BF16)
    d_normed_one, rest_grads, first_sum, down_sum = lax.optimization_barrier(
        (d_normed_one, rest_grads, first_sum, down_sum)
    )
    d_normed_one = lax.psum_scatter(
        d_normed_one, "tp", scatter_dimension=0, tiled=True
    ).astype(F32)
    grad_qkv = dot(normed_one, d_qkv, TN)
    rest_sum = rest_sum + dot(rest_grads, rows_seen, TN)
    d_normed_one, *near = lax.optimization_barrier((d_normed_one, *near))

    padded = expert_tiles * LANES

    moves = []
    for e in range(local_experts):
        held, first = (0, 0) if e == 0 else (1, 2 * (e - 1) * padded)
        moves += [(held, first, 0, e), (held, first + padded, 1, e), (2, e * padded, 2, e)]
    grad_egate, grad_eup, grad_edown = cut_experts(
        moves, (first_sum, rest_sum, down_sum), local_experts, hidden
    )
    grad_egate, grad_eup = grad_egate.transpose(0, 2, 1), grad_eup.transpose(0, 2, 1)
    shared_sum = rest_sum[2 * (local_experts - 1) * padded :]
    start = local_experts * padded
    shared_rows = my_gate.shape[0]
    place = shared_tiles * LANES
    grad_router = shared_sum[place : place + experts_all]
    grad_router = grad_router + shared_sum[place + experts_all : place + 2 * experts_all]
    if in_group:
        own_sum, line_parts = chip_sums(mine, near)
    else:
        own_sum = line_sums(mine, near)
    output = output + (swap(own_sum, "exp", base) if base else own_sum)
    own_scale = lax.rsqrt(jnp.mean(own_tokens * own_tokens, axis=-1, keepdims=True) + epsilon)
    grad_gain_one, d_input = norm_back(d_normed_one, own_tokens, own_scale, first_norm_scale)
    d_input = d_residual + d_input

    def uncut(grad):
        return grad.astype(BF16).reshape(grad.shape[0], exp_count, -1).transpose(1, 0, 2)

    narrow = jnp.concatenate(
        [grad_router.T, grad_gain_one[:, None], grad_gain_two[:, None]], axis=1
    )
    grad_proj = jnp.concatenate([grad_qkv, pad_to(narrow, 1, LANES)], axis=1).astype(BF16)
    grad_out_w = grad_out_w.astype(BF16)
    back_gate, back_up, back_down = (
        uncut(sums[:shared_rows])
        for sums in (shared_sum, shared_sum[place + LANES :], down_sum[start:])
    )
    if in_group:
        grad_proj, grad_out_w, output, back_gate, back_up, back_down = scatter_grads(
            grad_proj, grad_out_w, output, line_parts, back_gate, back_up, back_down
        )
        narrow = grad_proj[:, qkv_width:]
    else:
        output = output.astype(BF16)
        grad_proj = lax.psum_scatter(grad_proj, "exp", scatter_dimension=0, tiled=True).astype(F32)
        narrow = lax.psum(grad_proj[:, qkv_width:], "tp")
        grad_out_w = lax.psum_scatter(
            grad_out_w, "exp", scatter_dimension=1, tiled=True
        ).astype(F32)
        back_gate, back_up, back_down = (
            lax.all_to_all(x, "exp", split_axis=0, concat_axis=0, tiled=True)
            for x in (back_gate, back_up, back_down)
        )

    def joined(pieces):
        return pieces[:, :shared_hidden].reshape(-1, pieces.shape[2]).astype(F32)

    grad_sgate, grad_sup, grad_sdown = joined(back_gate).T, joined(back_up).T, joined(back_down)
    cuts = (qkv_widths[0], qkv_widths[0] + qkv_widths[1])
    return (
        output,
        d_input,
        narrow[:, experts_all],
        grad_proj[:, : cuts[0]],
        grad_proj[:, cuts[0] : cuts[1]],
        grad_proj[:, cuts[1] : qkv_width],
        grad_out_w,
        narrow[:, experts_all + 1],
        narrow[:, :experts_all],
        grad_sgate,
        grad_sup,
        grad_sdown,
        grad_egate,
        grad_eup,
        grad_edown,
    )


def solution(mesh):
    placed = (
        P(("exp", "tp"), None),
        P(("exp", "tp"), None),
        P("exp"),
        P("exp", None),
        P("exp"),
        P("exp", "tp"),
        P("exp", "tp"),
        P("exp", "tp"),
        P("tp", "exp"),
        P("exp"),
        P("exp", None),
        P("exp", "tp"),
        P("exp", "tp"),
        P("tp", "exp"),
        P("exp", None, "tp"),
        P("exp", None, "tp"),
        P("exp", "tp", None),
    )
    return jax.shard_map(
        shards,
        mesh=mesh,
        in_specs=placed,
        out_specs=(
            P(("exp", "tp"), None),
            P(("exp", "tp"), None),
            P("exp"),
            P("exp", "tp"),
            P("exp", "tp"),
            P("exp", "tp"),
            P("tp", "exp"),
            P("exp"),
            P("exp", None),
            P("exp", "tp"),
            P("exp", "tp"),
            P("tp", "exp"),
            P("exp", None, "tp"),
            P("exp", None, "tp"),
            P("exp", "tp", None),
        ),
        check_vma=False,
    )
```
